512 devices in a mesh: bulk: 32 (over x, y), group: 16 (over z, core).
Axes of the slice: x: 4, y: 8, z: 8, core: 2. Of those that a mesh axis runs over, the one named last changes fastest.
Arguments:
- rhs: bfloat16 [64, 256, 64, 64], P('bulk', 'group'), may hold values from -40 to 40
- diag_blocks: bfloat16 [64, 256, 64, 64], P('bulk', 'group'), may hold values from -0.4 to 2
- precond_blocks: bfloat16 [64, 256, 64, 64], P('bulk', 'group'), may hold values from -0.15 to 0.7
- coupling: float32 [64, 256, 256], P('bulk', 'group'), may hold values from 0.05 to 1.2
- face_open: int32 [64, 256, 4], P('bulk', 'group'), may hold values 0 or 1
- agg_id: int32 [64, 256], P('bulk', 'group'), may hold values from 0 to 3
- coarse_basis: float32 [64, 8], replicated, may hold values from -0.75 to 0.75
- coarse_inv: float32 [32, 512, 512], P('bulk', None, 'group'), may hold values from -1 to 2, as said below
Outputs:
- adjoint: bfloat16 [64, 256, 64, 64], P('bulk', 'group')
The draws below stay inside these ranges and needn't reach their ends.
Inputs may be any that keep to these rules, and one draw needn't show every extreme that they name: coarse_inv[b] is symmetric for every b.
All inputs are finite; a program needn't handle non-finite values. No bound on the sum of `face_open` on one device may be relied on, other than what follows from the above.
Results may differ from the reference program's by a relative error of at most 0.012.
Values may be sent and summed in bfloat16 or wider, within the bound.
A program may use at most 64 MiB of HBM per device.

```python
import math
import jax
import jax.numpy as jnp
from jax import lax

NS = 64
COLS = 64
CX = 2
CY = 16
AGGS = 4
COMPS = 8
ITERS = 3
NX = 64
NY = 256
GROUPS = 32
NCG = 512
N_GROUP = 16


def draw_rhs(key, part):
    row_pos = jnp.arange(NX, dtype=jnp.float32)[:, None] / max(NX - 1, 1)
    col_pos = jnp.arange(NY, dtype=jnp.float32)[None, :] / max(NY - 1, 1)
    rising = jnp.exp(math.log(3.0) * 0.5 * (row_pos + col_pos))[:, :, None, None]
    value_key = jax.random.fold_in(key, 21)
    values = jnp.clip(jax.random.normal(value_key, (NX, NY, NS, COLS), jnp.float32), -4.0, 4.0) * rising
    return values.astype(jnp.bfloat16)


def block_field(key, lowest, highest, spread):
    diag_key = jax.random.fold_in(key, 11)
    off_key = jax.random.fold_in(key, 12)
    diagonal = jnp.exp(jax.random.uniform(diag_key, (NX, NY, NS), jnp.float32, math.log(lowest), math.log(highest)))
    off_part = jnp.clip(jax.random.normal(off_key, (NX, NY, NS, NS), jnp.float32), -6.0, 6.0) * spread
    identity = jnp.eye(NS, dtype=jnp.float32)
    return off_part * (1.0 - identity) + identity * diagonal[..., None]


def draw_diag_blocks(key, part):
    return block_field(jax.random.fold_in(key, 1), 1.0, 2.0, 0.06).astype(jnp.bfloat16)


def draw_precond_blocks(key, part):
    return block_field(jax.random.fold_in(key, 2), 1.0 / 3.0, 2.0 / 3.0, 0.02).astype(jnp.bfloat16)


def draw_coupling(key, part):
    key = jax.random.fold_in(key, 4)
    unit = jax.random.uniform(key, (NX, NY, 4, NS), jnp.float32, 0.0, 1.0)
    lowest = jnp.log(jnp.array([0.05, 0.05, 0.6, 0.6], jnp.float32))[:, None]
    highest = jnp.log(jnp.array([0.5, 0.5, 1.2, 1.2], jnp.float32))[:, None]
    values = jnp.exp(lowest + unit * (highest - lowest))
    return values.reshape(NX, NY, 4 * NS).astype(jnp.float32)


def draw_coarse_inv(key, part):
    inner_key = jax.random.fold_in(key, 3)
    raw = jnp.clip(jax.random.normal(inner_key, (GROUPS, NCG, NCG), jnp.float32), -6.0, 6.0)
    raw = raw * (0.5 / math.sqrt(NCG))
    symmetric = (raw + jnp.swapaxes(raw, 1, 2)) * 0.5
    return symmetric + jnp.eye(NCG, dtype=jnp.float32)[None, :, :]


def touch_ends(values, key, least, high):
    shape = values.shape
    place = [jax.random.randint(jax.random.fold_in(key, axis), (), 0, shape[axis]) for axis in range(len(shape))]
    values = values.at[tuple(place)].set(least)
    longest = shape.index(max(shape))
    place[longest] = (place[longest] + 1) % shape[longest]
    return values.at[tuple(place)].set(high)


def bell_draw(own_key, shape, scale, bound, kind=jnp.bfloat16):
    values = jax.random.normal(own_key, shape, jnp.float32) * scale
    return jnp.minimum(jnp.maximum(values, -bound), bound).astype(kind)


def setup_inputs(seed: int = 0) -> dict:
    seeds = jax.random.split(jax.random.key(seed), 9)
    rhs = draw_rhs(jax.random.fold_in(seeds[8], 71), 0)
    diag_blocks = draw_diag_blocks(jax.random.fold_in(seeds[8], 71), 0)
    precond_blocks = draw_precond_blocks(jax.random.fold_in(seeds[8], 71), 0)
    coupling = draw_coupling(jax.random.fold_in(seeds[8], 71), 0)
    face_open = touch_ends((jax.random.randint(seeds[4], (NX, NY, 4), 0, 8) < 7).astype(jnp.int32), jax.random.fold_in(seeds[4], 1), 0, 1)
    agg_id = touch_ends(jax.random.randint(seeds[5], (NX, NY), 0, AGGS), jax.random.fold_in(seeds[5], 1), 0, AGGS - 1).astype(jnp.int32)
    coarse_basis = bell_draw(seeds[6], (NS, COMPS), NS ** -0.5, 0.75, jnp.float32)
    coarse_inv = draw_coarse_inv(jax.random.fold_in(seeds[8], 71), 0)
    return dict(rhs=rhs, diag_blocks=diag_blocks, precond_blocks=precond_blocks, coupling=coupling, face_open=face_open, agg_id=agg_id, coarse_basis=coarse_basis, coarse_inv=coarse_inv)


column_block = 8
tiny_eps = 1e-06

def apply_adjoint(field, blocks_wide, coeff):
    own = jnp.einsum('xyij,xyir->xyjr', blocks_wide, field.astype(jnp.float32))
    padded = jnp.pad(field, ((1, 1), (1, 1), (0, 0), (0, 0)))
    near = coeff[:, :, 0, :, None] * padded[:-2, 1:-1].astype(jnp.float32)
    near = near + coeff[:, :, 1, :, None] * padded[2:, 1:-1].astype(jnp.float32)
    near = near + coeff[:, :, 2, :, None] * padded[1:-1, :-2].astype(jnp.float32)
    near = near + coeff[:, :, 3, :, None] * padded[1:-1, 2:].astype(jnp.float32)
    return own - near

def coarse_whole(vector, one_hot, coarse_basis, coarse_inv):
    width = vector.shape[-1]
    highest = lax.Precision.HIGHEST
    shaped = vector.reshape(GROUPS, CX, N_GROUP, CY, NS, width)
    summed = jnp.einsum('bxgyk,bxgyjr->bgkjr', one_hot, shaped, precision=highest)
    weight_scale = (AGGS / (CX * CY)) ** 0.5
    residual = jnp.einsum('bgkjr,jc->bgkcr', summed, coarse_basis, precision=highest) * weight_scale
    residual = residual.reshape(GROUPS, NCG, width)
    correct = jnp.einsum('bmn,bnr->bmr', coarse_inv, residual, precision=highest)
    correct = correct.reshape(GROUPS, N_GROUP, AGGS, COMPS, width)
    spread = jnp.einsum('jc,bgkcr->bgkjr', coarse_basis, correct, precision=highest)
    back = jnp.einsum('bxgyk,bgkjr->bxgyjr', one_hot, spread, precision=highest)
    return back.reshape(NX, NY, NS, width)

def givens_solve(hessen_cols, beta_norm):
    cosine_list = []
    sine_list = []
    target = [beta_norm] + [jnp.zeros_like(beta_norm) for _ in range(ITERS)]
    triangle = []
    for section in range(ITERS):
        column = list(hessen_cols[section])
        for earlier in range(section):
            upper = column[earlier]
            lower = column[earlier + 1]
            column[earlier] = cosine_list[earlier] * upper + sine_list[earlier] * lower
            column[earlier + 1] = -sine_list[earlier] * upper + cosine_list[earlier] * lower
        upper = column[section]
        lower = column[section + 1]
        radius = jnp.sqrt(upper * upper + lower * lower)
        cosine = upper / radius
        sine_val = lower / radius
        cosine_list.append(cosine)
        sine_list.append(sine_val)
        column[section] = radius
        carried = target[section]
        target[section] = cosine * carried
        target[section + 1] = -sine_val * carried
        triangle.append(column[:section + 1])
    solution = [None] * ITERS
    for section in reversed(range(ITERS)):
        accumulated = target[section]
        for later in range(section + 1, ITERS):
            accumulated = accumulated - triangle[later][section] * solution[later]
        solution[section] = accumulated / triangle[section][section]
    return solution

def reference(rhs, diag_blocks, precond_blocks, coupling, face_open, agg_id, coarse_basis, coarse_inv):
    diag_wide = diag_blocks.astype(jnp.float32)
    precond_wide = precond_blocks.astype(jnp.float32)
    coeff = coupling.reshape(NX, NY, 4, NS) * face_open.astype(jnp.float32)[..., None]
    one_hot = (agg_id[..., None] == jnp.arange(AGGS, dtype=jnp.int32)[None, None, :]).astype(jnp.float32)
    one_hot = one_hot.reshape(GROUPS, CX, N_GROUP, CY, AGGS)

    def precondition(vector):
        rounded = lax.optimization_barrier(vector.astype(jnp.bfloat16))
        local = jnp.einsum('xyij,xyjr->xyir', precond_wide, rounded.astype(jnp.float32))
        return (local + coarse_whole(vector, one_hot, coarse_basis, coarse_inv)).astype(jnp.bfloat16)

    def solve(columns):
        start = columns.astype(jnp.float32)
        beta_norm = jnp.sqrt(lax.optimization_barrier(jnp.sum(start * start, axis=(0, 1, 2))) + tiny_eps)
        inv_beta = 1.0 / beta_norm
        krylov = [start]
        factors = [inv_beta]
        precond_vecs = []
        hessen_cols = []
        for section in range(ITERS):
            scale_now = factors[section]
            zvec = precondition(krylov[section])
            precond_vecs.append(zvec)
            image = apply_adjoint(zvec, diag_wide, coeff)
            projected = [lax.optimization_barrier(jnp.sum(krylov[i] * image, axis=(0, 1, 2))) * factors[i] * scale_now for i in range(section + 1)]
            image = image * scale_now
            for earlier in range(section + 1):
                image = image - projected[earlier] * (krylov[earlier] * factors[earlier])
            next_norm = jnp.sqrt(lax.optimization_barrier(jnp.sum(image * image, axis=(0, 1, 2))) + tiny_eps)
            hessen_cols.append(projected + [next_norm])
            if section + 1 < ITERS:
                krylov.append(image / next_norm)
                factors.append(jnp.ones_like(inv_beta))
        solution = givens_solve(hessen_cols, beta_norm)
        total = jnp.zeros(columns.shape, jnp.float32)
        for section in range(ITERS):
            total = total + solution[section] * factors[section] * precond_vecs[section].astype(jnp.float32)
        return total.astype(jnp.bfloat16)
    blocks = jnp.moveaxis(rhs.reshape(NX, NY, NS, COLS // column_block, column_block), 3, 0)
    result = lax.map(solve, blocks)
    return jnp.moveaxis(result, 0, 3).reshape(NX, NY, NS, COLS)
```

```python
import functools

import jax
import jax.numpy as jnp
from jax import lax
from jax.experimental import pallas as pl
from jax.experimental.pallas import tpu as pltpu
from jax.sharding import PartitionSpec as P

NS = 64
COLS = 64
CX = 2
CY = 16
AGGS = 4
COMPS = 8
ITERS = 3
HALF = CY // 2
PAIRS = CX * HALF
LANES = 2 * COLS

tiny_eps = 1e-06
f32 = jnp.float32
bf16 = jnp.bfloat16


def split_hi_lo(value):
    high = value.astype(bf16)
    low = (value - high.astype(f32)).astype(bf16)
    return high, low


def mm(left, right):
    return jnp.dot(left, right, preferred_element_type=f32)


def low_half(shape):
    return lax.broadcasted_iota(jnp.int32, shape, 1) < COLS


def givens_solve(hessen_cols, beta_norm):
    cosine_list = []
    sine_list = []
    target = [beta_norm] + [jnp.zeros_like(beta_norm) for _ in range(ITERS)]
    triangle = []
    for section in range(ITERS):
        column = list(hessen_cols[section])
        for earlier in range(section):
            upper = column[earlier]
            lower = column[earlier + 1]
            column[earlier] = cosine_list[earlier] * upper + sine_list[earlier] * lower
            column[earlier + 1] = -sine_list[earlier] * upper + cosine_list[earlier] * lower
        upper = column[section]
        lower = column[section + 1]
        radius = jnp.sqrt(upper * upper + lower * lower)
        cosine = upper / radius
        sine_val = lower / radius
        cosine_list.append(cosine)
        sine_list.append(sine_val)
        column[section] = radius
        carried = target[section]
        target[section] = cosine * carried
        target[section + 1] = -sine_val * carried
        triangle.append(column[: section + 1])
    result = [None] * ITERS
    for section in reversed(range(ITERS)):
        accumulated = target[section]
        for later in range(section + 1, ITERS):
            accumulated = accumulated - triangle[later][section] * result[later]
        result[section] = accumulated / triangle[section][section]
    return result


def kernel(
    nb,
    ng,
    rhs_hbm,
    diag_hbm,
    prec_hbm,
    coup_ref,
    face_ref,
    agg_ref,
    basis_ref,
    inv_hbm,
    out_ref,
    rhs_raw,
    prec,
    diag_raw,
    diag_t,
    inv_raw,
    inv_rows,
    coef,
    wtab,
    bas_t,
    bas_w,
    k0,
    k1,
    w0,
    w1,
    acc,
    local_y,
    zs,
    spread,
    res_send,
    res_buf,
    halo_x,
    halo_y,
    edge,
    sum_send,
    sum_group,
    tot_send,
    sum_bulk,
    load_sem,
    res_ssem,
    res_rsem,
    hx_ssem,
    hx_rsem,
    hy_ssem,
    hy_rsem,
    g_ssem,
    g_rsem,
    b_ssem,
    b_rsem,
):
    bulk = lax.axis_index("bulk")
    group = lax.axis_index("group")

    loads = [pltpu.make_async_copy(rhs_hbm, rhs_raw, load_sem.at[0])]
    prec_loads = []
    diag_loads = []
    for x in range(CX):
        for yh in range(2):
            n = x * 2 + yh
            src = (x, pl.ds(yh * HALF, HALF))
            dst = (pl.ds(x * HALF, HALF), pl.ds(yh * NS, NS))
            prec_loads.append(
                pltpu.make_async_copy(prec_hbm.at[src], prec.at[dst], load_sem.at[1 + n])
            )
            diag_loads.append(
                pltpu.make_async_copy(diag_hbm.at[src], diag_raw.at[dst], load_sem.at[5 + n])
            )
    inv_loads = [
        pltpu.make_async_copy(inv_hbm.at[:, kh], inv_raw.at[kh], load_sem.at[9 + kh])
        for kh in range(2)
    ]
    for copy in loads + prec_loads + inv_loads + diag_loads:
        copy.start()

    barrier = pltpu.get_barrier_semaphore()

    def greet_group(d, carry):
        pl.semaphore_signal(
            barrier,
            inc=1,
            device_id={"group": lax.rem(group + d, ng)},
            device_id_type=pl.DeviceIdType.MESH,
        )
        return carry

    def greet_bulk(d, carry):
        pl.semaphore_signal(
            barrier,
            inc=1,
            device_id={"bulk": lax.rem(bulk + d, nb)},
            device_id_type=pl.DeviceIdType.MESH,
        )
        return carry

    lax.fori_loop(1, ng, greet_group, 0)
    lax.fori_loop(1, nb, greet_bulk, 0)

    low8 = low_half((8, LANES))
    low64 = low_half((NS, LANES))

    def make_weights(p, carry):
        x = p // HALF
        yy = p % HALF
        first = agg_ref[x, yy]
        second = agg_ref[x, yy + HALF]
        for k in range(AGGS):
            wtab[p, k] = jnp.where(
                low8,
                jnp.where(first == k, 1.0, 0.0).astype(f32),
                jnp.where(second == k, 1.0, 0.0).astype(f32),
            )
        return carry

    lax.fori_loop(0, PAIRS, make_weights, 0)

    weight_scale = (AGGS / (CX * CY)) ** 0.5
    basis = basis_ref[...]
    turned = jnp.transpose(basis)
    high, low = split_hi_lo(turned)
    stacked = jnp.concatenate([high.astype(f32), high.astype(f32), low.astype(f32)], axis=0)
    bas_w[...] = jnp.transpose(stacked).astype(bf16)
    high, low = split_hi_lo(turned * weight_scale)
    bas_t[0] = jnp.concatenate([high, high], axis=0)
    bas_t[1] = jnp.concatenate([low, low], axis=0)

    loads[0].wait()

    def make_start(p, carry):
        x = p // HALF
        yy = p % HALF
        first = rhs_raw[x, yy].astype(f32)
        second = rhs_raw[x, yy + HALF].astype(f32)
        k0[p] = jnp.concatenate([first, second], axis=1)
        return carry

    lax.fori_loop(0, PAIRS, make_start, 0)

    def coarse_send(step, field):
        def add(p, sums):
            value = field[p].reshape(8, 8, LANES)
            return tuple(sums[k] + wtab[p, k] * value for k in range(AGGS))

        zero = jnp.zeros((8, 8, LANES), f32)
        sums = lax.fori_loop(0, PAIRS, add, (zero,) * AGGS)
        sums = [s.reshape(NS, LANES) for s in sums]
        parts = []
        for kl in range(2):
            keep = jnp.where(low64, sums[kl], sums[kl + 2])
            move = jnp.where(low64, sums[kl + 2], sums[kl])
            total = keep + pltpu.roll(move, COLS, 1)
            high, low = split_hi_lo(total)
            part = mm(bas_t[0], high) + mm(bas_t[0], low) + mm(bas_t[1], high)
            parts.append(part[:COMPS])
        res = jnp.concatenate(parts, axis=0).astype(bf16)
        res_send[step] = res
        res_buf[step, group] = res

        def push(d, carry):
            pltpu.make_async_remote_copy(
                src_ref=res_send.at[step],
                dst_ref=res_buf.at[step, group],
                send_sem=res_ssem.at[step],
                recv_sem=res_rsem.at[step],
                device_id={"group": lax.rem(group + d, ng)},
                device_id_type=pl.DeviceIdType.MESH,
            ).start()
            return carry

        lax.fori_loop(1, ng, push, 0)

    def all_but_one(buf, count, sem):
        return pltpu.make_async_copy(buf.at[pl.ds(0, count - 1)], buf.at[pl.ds(0, count - 1)], sem)

    def pair_product(mats, p, value):
        both = mm(mats[p], value)
        return jnp.where(low64, both[:NS], both[NS:])

    def local_part(field):
        def one(p, carry):
            local_y[p] = pair_product(prec, p, field[p].astype(bf16))
            return carry

        lax.fori_loop(0, PAIRS, one, 0)

    def halo_copies(step):
        left = lax.rem(bulk + nb - 1, nb)
        right = lax.rem(bulk + 1, nb)
        before = lax.rem(group + ng - 1, ng)
        after = lax.rem(group + 1, ng)
        copies = []
        for x, axis, target in ((0, "bulk", left), (1, "bulk", right)):
            copies.append(
                pltpu.make_async_remote_copy(
                    src_ref=zs.at[step, pl.ds(x * HALF, HALF)],
                    dst_ref=halo_x.at[step, 1 - x],
                    send_sem=hx_ssem.at[step, x],
                    recv_sem=hx_rsem.at[step, 1 - x],
                    device_id={axis: target},
                    device_id_type=pl.DeviceIdType.MESH,
                )
            )
        for x in range(CX):
            for side, row, target in ((0, HALF - 1, after), (1, 0, before)):
                copies.append(
                    pltpu.make_async_remote_copy(
                        src_ref=zs.at[step, x * HALF + row],
                        dst_ref=halo_y.at[step, x, side],
                        send_sem=hy_ssem.at[step, x, side],
                        recv_sem=hy_rsem.at[step, x, side],
                        device_id={"group": target},
                        device_id_type=pl.DeviceIdType.MESH,
                    )
                )
        return copies

    def finish_z(step):
        all_but_one(res_buf.at[step], ng, res_rsem.at[step]).wait()
        gathered = res_buf[step].reshape(ng * 16, LANES)
        both = mm(inv_rows[...], gathered)
        rows = AGGS * COMPS
        both = both[: 2 * rows] + both[2 * rows :]
        mixed = jnp.where(low_half((rows, LANES)), both[:rows], both[rows:])
        cor = mixed + pltpu.roll(mixed, COLS, 1)
        wide = jnp.concatenate([cor[k * COMPS : (k + 1) * COMPS] for k in range(AGGS)], axis=1)
        high, low = split_hi_lo(wide)
        wide = jnp.concatenate([high.astype(f32), low.astype(f32), high.astype(f32)], axis=0)
        wide = mm(bas_w[...], wide.astype(bf16))
        for k in range(AGGS):
            spread[k] = wide[:, k * LANES : (k + 1) * LANES]
        copies = halo_copies(step)

        def one(p, carry):
            x = p // HALF
            yy = p % HALF
            first = spread[agg_ref[x, yy]]
            second = spread[agg_ref[x, yy + HALF]]
            zs[step, p] = (local_y[p] + jnp.where(low64, first, second)).astype(bf16)
            return carry

        for x in range(CX):
            lax.fori_loop(x * HALF, (x + 1) * HALF, one, 0)
            copies[x].start()
            copies[2 + 2 * x].start()
            copies[3 + 2 * x].start()
        return copies

    def own_image(step):
        for x in range(CX):

            def one(yy, carry):
                p = x * HALF + yy
                own = pair_product(diag_t, p, zs[step, p])
                other = zs[step, (1 - x) * HALF + yy].astype(f32)
                acc[p] = own - coef[p, 1 - x] * other
                return carry

            lax.fori_loop(0, HALF, one, 0)

    def wait_halo(step, copies):
        for n in (2, 3, 4, 5, 0, 1):
            copies[n].wait_recv()
        for x in range(CX):
            base = x * HALF
            last = zs[step, base + HALF - 1].astype(f32)
            first = zs[step, base].astype(f32)
            got = halo_y[step, x, 0].astype(f32)
            edge[x, 0] = pltpu.roll(jnp.where(low64, last, got), COLS, 1)
            got = halo_y[step, x, 1].astype(f32)
            edge[x, 1] = pltpu.roll(jnp.where(low64, got, first), COLS, 1)

    def image(step, x, yy, prev, following):
        p = x * HALF + yy
        value = acc[p] - coef[p, x] * halo_x[step, x, yy].astype(f32)
        return value - coef[p, 2] * prev - coef[p, 3] * following

    def sweep(step, tail, count):
        def run(x, yy, prev, following, sums):
            p = x * HALF + yy
            terms = tail(p, image(step, x, yy, prev, following))
            return tuple(
                s + jnp.sum((a * b).reshape(8, 8, LANES), axis=0) for s, (a, b) in zip(sums, terms)
            )

        sums = (jnp.zeros((8, LANES), f32),) * count
        for x in range(CX):
            base = x * HALF

            def one(yy, sums):
                prev = zs[step, base + yy - 1].astype(f32)
                following = zs[step, base + yy + 1].astype(f32)
                return run(x, yy, prev, following, sums)

            sums = run(x, 0, edge[x, 0], zs[step, base + 1].astype(f32), sums)
            sums = lax.fori_loop(1, HALF - 1, one, sums)
            sums = run(x, HALF - 1, zs[step, base + HALF - 2].astype(f32), edge[x, 1], sums)
        rows = [jnp.sum(s, axis=0, keepdims=True) for s in sums]
        rows += [jnp.zeros((1, LANES), f32)] * (8 - count)
        return jnp.concatenate(rows, axis=0)

    def sum_start(step, payload):
        sum_send[step] = payload
        sum_group[step, group] = payload

        def push(d, carry):
            pltpu.make_async_remote_copy(
                src_ref=sum_send.at[step],
                dst_ref=sum_group.at[step, group],
                send_sem=g_ssem.at[step],
                recv_sem=g_rsem.at[step],
                device_id={"group": lax.rem(group + d, ng)},
                device_id_type=pl.DeviceIdType.MESH,
            ).start()
            return carry

        lax.fori_loop(1, ng, push, 0)

    def sum_middle(step):
        all_but_one(sum_group.at[step], ng, g_rsem.at[step]).wait()
        partial = jnp.sum(sum_group[step], axis=0)
        tot_send[step] = partial
        sum_bulk[step, bulk] = partial

        def push(d, carry):
            pltpu.make_async_remote_copy(
                src_ref=tot_send.at[step],
                dst_ref=sum_bulk.at[step, bulk],
                send_sem=b_ssem.at[step],
                recv_sem=b_rsem.at[step],
                device_id={"bulk": lax.rem(bulk + d, nb)},
                device_id_type=pl.DeviceIdType.MESH,
            ).start()
            return carry

        lax.fori_loop(1, nb, push, 0)

    def sum_finish(step, count):
        all_but_one(sum_bulk.at[step], nb, b_rsem.at[step]).wait()
        total = jnp.sum(sum_bulk[step], axis=0)
        total = total + pltpu.roll(total, COLS, 1)
        return [jnp.broadcast_to(total[i : i + 1], (8, LANES)) for i in range(count)]

    def scaled(factor, value):
        return (factor * value.reshape(8, 8, LANES)).reshape(NS, LANES)

    pl.semaphore_wait(barrier, ng + nb - 2)
    coarse_send(0, k0)

    for copy in prec_loads:
        copy.wait()
    local_part(k0)

    for copy in inv_loads:
        copy.wait()
    turned = [jnp.transpose(inv_raw[kh].reshape(ng * 16, AGGS * COMPS)) for kh in range(2)]
    high, low = split_hi_lo(jnp.concatenate(turned, axis=0))
    inv_rows[0 : 2 * AGGS * COMPS] = high
    inv_rows[2 * AGGS * COMPS :] = low

    for copy in diag_loads:
        copy.wait()

    def turn_diag(p, carry):
        both = diag_raw[p].astype(f32)
        diag_t[p, 0:NS] = jnp.transpose(both[:NS]).astype(bf16)
        diag_t[p, NS : 2 * NS] = jnp.transpose(both[NS:]).astype(bf16)
        return carry

    lax.fori_loop(0, PAIRS, turn_diag, 0)

    copies0 = finish_z(0)

    face_of = lax.broadcasted_iota(jnp.int32, (CY, 4 * NS), 1) // NS
    cell_y = lax.broadcasted_iota(jnp.int32, (CY, 4 * NS), 0)
    for x in range(CX):
        opened = face_ref[x].astype(f32)
        mask = jnp.zeros((CY, 4 * NS), f32)
        for f in range(4):
            mask = jnp.where(face_of == f, opened[:, f : f + 1], mask)
        if x == 0:
            mask = jnp.where((face_of == 0) & (bulk == 0), 0.0, mask)
        if x == CX - 1:
            mask = jnp.where((face_of == 1) & (bulk == nb - 1), 0.0, mask)
        mask = jnp.where((face_of == 2) & (cell_y == 0) & (group == 0), 0.0, mask)
        mask = jnp.where((face_of == 3) & (cell_y == CY - 1) & (group == ng - 1), 0.0, mask)
        value = coup_ref[x] * mask
        first = value.astype(bf16).astype(f32)
        second = (value - first).astype(bf16).astype(f32)
        third = value - first - second
        spread_rows = jnp.transpose(jnp.concatenate([first, second, third], axis=0)).astype(bf16)

        def expand(yy, carry):
            row = lax.broadcasted_iota(jnp.int32, (3 * CY, LANES), 0) & (CY - 1)
            lane = lax.broadcasted_iota(jnp.int32, (3 * CY, LANES), 1)
            pick = jnp.where(row == yy + jnp.where(lane < COLS, 0, HALF), 1.0, 0.0).astype(bf16)
            wide = mm(spread_rows, pick)
            for f in range(4):
                coef[x * HALF + yy, f] = wide[f * NS : (f + 1) * NS]
            return carry

        lax.fori_loop(0, HALF, expand, 0)

    own_image(0)
    wait_halo(0, copies0)

    def tail0(p, value):
        w0[p] = value
        start = k0[p]
        return ((start, start), (start, value), (value, value))

    payload = sweep(0, tail0, 3)

    coarse_send(1, w0)
    sum_start(0, payload)
    local_part(w0)
    sum_middle(0)
    copies1 = finish_z(1)
    own_image(1)
    wait_halo(1, copies1)
    sum_kk, sum_kw, sum_ww = sum_finish(0, 3)
    beta = jnp.sqrt(sum_kk + tiny_eps)
    s0 = 1.0 / beta
    h00 = sum_kw * s0 * s0
    g00 = sum_kk * s0 * s0
    left_sq = sum_ww * s0 * s0 - h00 * h00 * (2.0 - g00)
    h10u = jnp.sqrt(jnp.maximum(left_sq, 0.0) + tiny_eps)
    c1 = s0 / h10u
    c2 = h00 * s0 / h10u

    def tail1(p, value):
        image0 = w0[p]
        start = k0[p]
        vec = scaled(c1, image0) - scaled(c2, start)
        value = scaled(c1, value) - scaled(c2, image0)
        k1[p] = vec
        w1[p] = value
        return ((start, value), (vec, value), (value, value), (start, vec), (vec, vec))

    payload = sweep(1, tail1, 5)

    coarse_send(2, w1)
    sum_start(1, payload)
    local_part(w1)
    sum_middle(1)
    copies2 = finish_z(2)
    own_image(2)
    wait_halo(2, copies2)
    d_0w, d_1w, d_ww, d_01, d_11 = sum_finish(1, 5)
    h10 = jnp.sqrt(h10u * h10u * d_11 + tiny_eps)
    t1 = h10u / h10
    h01 = d_0w * s0 * t1
    h11 = d_1w * t1 * t1
    g01 = d_01 * s0 * t1
    g11 = d_11 * t1 * t1
    left_sq = (
        d_ww * t1 * t1
        - h01 * h01 * (2.0 - g00)
        - h11 * h11 * (2.0 - g11)
        + 2.0 * h01 * h11 * g01
    )
    h21u = jnp.sqrt(jnp.maximum(left_sq, 0.0) + tiny_eps)
    e1 = t1 / h21u
    e2 = h01 * s0 / h21u
    e3 = h11 * t1 / h21u

    def tail2(p, value):
        start = k0[p]
        vec1 = k1[p]
        image1 = w1[p]
        vec2 = scaled(e1, image1) - scaled(e2, start) - scaled(e3, vec1)
        value = scaled(e1, value) - scaled(e2, w0[p]) - scaled(e3, image1)
        return (
            (start, value),
            (vec1, value),
            (vec2, value),
            (value, value),
            (start, vec2),
            (vec1, vec2),
            (vec2, vec2),
        )

    payload = sweep(2, tail2, 7)
    sum_start(2, payload)
    sum_middle(2)
    q_0w, q_1w, q_2w, q_ww, q_02, q_12, q_22 = sum_finish(2, 7)
    h21 = jnp.sqrt(h21u * h21u * q_22 + tiny_eps)
    t2 = h21u / h21
    h02 = q_0w * s0 * t2
    h12 = q_1w * t1 * t2
    h22 = q_2w * t2 * t2
    g02 = q_02 * s0 * t2
    g12 = q_12 * t1 * t2
    g22 = q_22 * t2 * t2
    left_sq = (
        q_ww * t2 * t2
        - h02 * h02 * (2.0 - g00)
        - h12 * h12 * (2.0 - g11)
        - h22 * h22 * (2.0 - g22)
        + 2.0 * (h02 * h12 * g01 + h02 * h22 * g02 + h12 * h22 * g12)
    )
    h32 = jnp.sqrt(jnp.maximum(left_sq, 0.0) + tiny_eps)
    y0, y1, y2 = givens_solve([[h00, h10], [h01, h11, h21], [h02, h12, h22, h32]], beta)

    over = y2 * t2 / h21u
    a2 = over * t1
    on1 = y1 - over * h11
    a1 = on1 * t1 * c1
    a0 = y0 * s0 - over * h01 * s0 - on1 * t1 * c2

    def finish(p, carry):
        x = p // HALF
        yy = p % HALF
        total = (
            scaled(a0, zs[0, p].astype(f32))
            + scaled(a1, zs[1, p].astype(f32))
            + scaled(a2, zs[2, p].astype(f32))
        )
        out_ref[x, yy] = total[:, :COLS].astype(bf16)
        out_ref[x, yy + HALF] = pltpu.roll(total, COLS, 1)[:, :COLS].astype(bf16)
        return carry

    lax.fori_loop(0, PAIRS, finish, 0)

    for step, copies in enumerate((copies0, copies1, copies2)):
        all_but_one(res_buf.at[step], ng, res_ssem.at[step]).wait()
        all_but_one(sum_group.at[step], ng, g_ssem.at[step]).wait()
        all_but_one(sum_bulk.at[step], nb, b_ssem.at[step]).wait()
        for copy in copies:
            copy.wait_send()


def body(nb, ng, rhs, diag_blocks, precond_blocks, coupling, face_open, agg_id, coarse_basis, coarse_inv):
    rows = AGGS * COMPS
    inverse = coarse_inv.reshape(ng, 2, rows // 2, rows)
    any_spec = pl.BlockSpec(memory_space=pl.ANY)
    vmem_spec = pl.BlockSpec(memory_space=pltpu.VMEM)
    smem_spec = pl.BlockSpec(memory_space=pltpu.SMEM)
    field = pltpu.VMEM((PAIRS, NS, LANES), f32)
    dma = pltpu.SemaphoreType.DMA
    return pl.pallas_call(
        functools.partial(kernel, nb, ng),
        out_shape=jax.ShapeDtypeStruct(rhs.shape, bf16),
        in_specs=[any_spec, any_spec, any_spec, vmem_spec, vmem_spec, smem_spec, vmem_spec, any_spec],
        out_specs=vmem_spec,
        scratch_shapes=[
            pltpu.VMEM((CX, CY, NS, COLS), bf16),
            pltpu.VMEM((PAIRS, 2 * NS, NS), bf16),
            pltpu.VMEM((PAIRS, 2 * NS, NS), bf16),
            pltpu.VMEM((PAIRS, 2 * NS, NS), bf16),
            pltpu.VMEM((2, ng, rows // 2, rows), f32),
            pltpu.VMEM((4 * rows, ng * rows // 2), bf16),
            pltpu.VMEM((PAIRS, 4, NS, LANES), f32),
            pltpu.VMEM((PAIRS, AGGS, 8, LANES), f32),
            pltpu.VMEM((2, 2 * COMPS, NS), bf16),
            pltpu.VMEM((NS, 3 * COMPS), bf16),
            field,
            field,
            field,
            field,
            field,
            field,
            pltpu.VMEM((ITERS, PAIRS, NS, LANES), bf16),
            pltpu.VMEM((AGGS, NS, LANES), f32),
            pltpu.VMEM((ITERS, rows // 2, LANES), bf16),
            pltpu.VMEM((ITERS, ng, rows // 2, LANES), bf16),
            pltpu.VMEM((ITERS, CX, HALF, NS, LANES), bf16),
            pltpu.VMEM((ITERS, CX, 2, NS, LANES), bf16),
            pltpu.VMEM((CX, 2, NS, LANES), f32),
            pltpu.VMEM((ITERS, 8, LANES), f32),
            pltpu.VMEM((ITERS, ng, 8, LANES), f32),
            pltpu.VMEM((ITERS, 8, LANES), f32),
            pltpu.VMEM((ITERS, nb, 8, LANES), f32),
            dma((11,)),
            dma((ITERS,)),
            dma((ITERS,)),
            dma((ITERS, CX)),
            dma((ITERS, CX)),
            dma((ITERS, CX, 2)),
            dma((ITERS, CX, 2)),
            dma((ITERS,)),
            dma((ITERS,)),
            dma((ITERS,)),
            dma((ITERS,)),
        ],
        compiler_params=pltpu.CompilerParams(
            collective_id=0, has_side_effects=True, vmem_limit_bytes=40 * 1024 * 1024
        ),
        cost_estimate=pl.CostEstimate(flops=200_000_000, bytes_accessed=3_000_000, transcendentals=0),
    )(
        rhs,
        diag_blocks,
        precond_blocks,
        coupling,
        face_open,
        agg_id,
        coarse_basis,
        inverse,
    )


def solution(mesh):
    in_specs = (
        P("bulk", "group", None, None),
        P("bulk", "group", None, None),
        P("bulk", "group", None, None),
        P("bulk", "group", None),
        P("bulk", "group", None),
        P("bulk", "group"),
        P(),
        P("bulk", None, "group"),
    )
    out_specs = P("bulk", "group", None, None)
    return jax.shard_map(
        functools.partial(body, mesh.shape["bulk"], mesh.shape["group"]),
        mesh=mesh,
        in_specs=in_specs,
        out_specs=out_specs,
        check_vma=False,
    )
```

```python
import functools

import jax
import jax.numpy as jnp
from jax import lax
from jax.experimental import pallas as pl
from jax.experimental.pallas import tpu as pltpu
from jax.sharding import PartitionSpec as P

NS = 64
COLS = 64
CX = 2
CY = 16
AGGS = 4
COMPS = 8
ITERS = 3
HALF = CY // 2
PAIRS = CX * HALF
LANES = 2 * COLS
UNROLL = 16

tiny_eps = 1e-06
f32 = jnp.float32
bf16 = jnp.bfloat16


def split_hi_lo(value):
    high = value.astype(bf16)
    low = (value - high.astype(f32)).astype(bf16)
    return high, low


def mm(left, right):
    return jnp.dot(left, right, preferred_element_type=f32)


def loop(count, step, carry=0, unroll=UNROLL):
    unroll = min(unroll, count)

    def several(start, carry):
        for i in range(unroll):
            carry = step(start * unroll + i, carry)
        return carry

    if unroll == count:
        return several(0, carry)
    return lax.fori_loop(0, count // unroll, several, carry)


def low_half(shape):
    return lax.broadcasted_iota(jnp.int32, shape, 1) < COLS


def givens_solve(hessen_cols, beta_norm):
    cosine_list = []
    sine_list = []
    target = [beta_norm] + [jnp.zeros_like(beta_norm) for _ in range(ITERS)]
    triangle = []
    for section in range(ITERS):
        column = list(hessen_cols[section])
        for earlier in range(section):
            upper = column[earlier]
            lower = column[earlier + 1]
            column[earlier] = cosine_list[earlier] * upper + sine_list[earlier] * lower
            column[earlier + 1] = -sine_list[earlier] * upper + cosine_list[earlier] * lower
        upper = column[section]
        lower = column[section + 1]
        radius = jnp.sqrt(upper * upper + lower * lower)
        cosine = upper / radius
        sine_val = lower / radius
        cosine_list.append(cosine)
        sine_list.append(sine_val)
        column[section] = radius
        carried = target[section]
        target[section] = cosine * carried
        target[section + 1] = -sine_val * carried
        triangle.append(column[: section + 1])
    result = [None] * ITERS
    for section in reversed(range(ITERS)):
        accumulated = target[section]
        for later in range(section + 1, ITERS):
            accumulated = accumulated - triangle[later][section] * result[later]
        result[section] = accumulated / triangle[section][section]
    return result


def kernel(
    nb,
    ng,
    rhs_hbm,
    diag_hbm,
    prec_hbm,
    coup_hbm,
    face_hbm,
    agg_ref,
    basis_hbm,
    inv_hbm,
    out_ref,
    coup_ref,
    face_ref,
    basis_ref,
    rhs_raw,
    prec,
    diag_raw,
    diag_t,
    inv_raw,
    inv_rows,
    coef,
    wtab,
    bas_t,
    bas_w,
    k0,
    k1,
    w0,
    w1,
    acc,
    local_y,
    zs,
    spread,
    res_send,
    res_buf,
    halo_x,
    halo_y,
    edge,
    sum_send,
    sum_group,
    tot_send,
    sum_bulk,
    load_sem,
    res_ssem,
    res_rsem,
    hx_ssem,
    hx_rsem,
    hy_ssem,
    hy_rsem,
    g_ssem,
    g_rsem,
    b_ssem,
    b_rsem,
):
    bulk = lax.axis_index("bulk")
    group = lax.axis_index("group")

    loads = [pltpu.make_async_copy(rhs_hbm, rhs_raw, load_sem.at[0])]
    prec_loads = []
    diag_loads = []
    for x in range(CX):
        for yh in range(2):
            n = x * 2 + yh
            src = (x, pl.ds(yh * HALF, HALF))
            dst = (pl.ds(x * HALF, HALF), pl.ds(yh * NS, NS))
            prec_loads.append(
                pltpu.make_async_copy(prec_hbm.at[src], prec.at[dst], load_sem.at[1 + n])
            )
            diag_loads.append(
                pltpu.make_async_copy(diag_hbm.at[src], diag_raw.at[dst], load_sem.at[5 + n])
            )
    inv_loads = [pltpu.make_async_copy(inv_hbm, inv_raw, load_sem.at[9])]
    small_loads = [
        pltpu.make_async_copy(basis_hbm, basis_ref, load_sem.at[10]),
        pltpu.make_async_copy(face_hbm, face_ref, load_sem.at[11]),
        pltpu.make_async_copy(coup_hbm, coup_ref, load_sem.at[12]),
    ]
    for copy in loads + small_loads + prec_loads + inv_loads + diag_loads:
        copy.start()

    barrier = pltpu.get_barrier_semaphore()

    def greet_group(d, carry):
        pl.semaphore_signal(
            barrier,
            inc=1,
            device_id={"group": lax.rem(group + d, ng)},
            device_id_type=pl.DeviceIdType.MESH,
        )
        return carry

    def greet_bulk(d, carry):
        pl.semaphore_signal(
            barrier,
            inc=1,
            device_id={"bulk": lax.rem(bulk + d, nb)},
            device_id_type=pl.DeviceIdType.MESH,
        )
        return carry

    lax.fori_loop(1, ng, greet_group, 0)
    lax.fori_loop(1, nb, greet_bulk, 0)

    low8 = low_half((8, LANES))
    low64 = low_half((NS, LANES))

    def make_weights(p, carry):
        x = p // HALF
        yy = p % HALF
        first = agg_ref[x, yy]
        second = agg_ref[x, yy + HALF]
        for k in range(AGGS):
            wtab[p, k] = jnp.where(
                low8,
                jnp.where(first == k, 1.0, 0.0).astype(f32),
                jnp.where(second == k, 1.0, 0.0).astype(f32),
            )
        return carry

    loop(PAIRS, make_weights)

    weight_scale = (AGGS / (CX * CY)) ** 0.5
    small_loads[0].wait()
    turned = basis_ref[...]
    high, low = split_hi_lo(turned)
    stacked = jnp.concatenate([high.astype(f32), high.astype(f32), low.astype(f32)], axis=0)
    bas_w[...] = jnp.transpose(stacked).astype(bf16)
    high, low = split_hi_lo(turned * weight_scale)
    bas_t[0] = jnp.concatenate([high, high], axis=0)
    bas_t[1] = jnp.concatenate([low, low], axis=0)

    loads[0].wait()

    def make_start(p, carry):
        x = p // HALF
        yy = p % HALF
        first = rhs_raw[x, yy].astype(f32)
        second = rhs_raw[x, yy + HALF].astype(f32)
        k0[p] = jnp.concatenate([first, second], axis=1)
        return carry

    loop(PAIRS, make_start)

    def coarse_send(step, field):
        def add(p, sums):
            value = field[p].reshape(8, 8, LANES)
            return tuple(sums[k] + wtab[p, k] * value for k in range(AGGS))

        zero = jnp.zeros((8, 8, LANES), f32)
        sums = loop(PAIRS, add, (zero,) * AGGS)
        sums = [s.reshape(NS, LANES) for s in sums]
        parts = []
        for kl in range(2):
            keep = jnp.where(low64, sums[kl], sums[kl + 2])
            move = jnp.where(low64, sums[kl + 2], sums[kl])
            total = keep + pltpu.roll(move, COLS, 1)
            high, low = split_hi_lo(total)
            part = mm(bas_t[0], high) + mm(bas_t[0], low) + mm(bas_t[1], high)
            parts.append(part[:COMPS])
        res = jnp.concatenate(parts, axis=0).astype(bf16)
        res_send[step] = res
        res_buf[step, group] = res

        def push(d, carry):
            pltpu.make_async_remote_copy(
                src_ref=res_send.at[step],
                dst_ref=res_buf.at[step, group],
                send_sem=res_ssem.at[step],
                recv_sem=res_rsem.at[step],
                device_id={"group": lax.rem(group + d, ng)},
                device_id_type=pl.DeviceIdType.MESH,
            ).start()
            return carry

        lax.fori_loop(1, ng, push, 0)

    def all_but_one(buf, count, sem):
        return pltpu.make_async_copy(buf.at[pl.ds(0, count - 1)], buf.at[pl.ds(0, count - 1)], sem)

    def pair_product(mats, p, value):
        both = mm(mats[p], value)
        return jnp.where(low64, both[:NS], both[NS:])

    def local_part(field):
        def one(p, carry):
            local_y[p] = pair_product(prec, p, field[p].astype(bf16))
            return carry

        loop(PAIRS, one)

    def halo_copies(step):
        left = lax.rem(bulk + nb - 1, nb)
        right = lax.rem(bulk + 1, nb)
        before = lax.rem(group + ng - 1, ng)
        after = lax.rem(group + 1, ng)
        copies = []
        for x, axis, target in ((0, "bulk", left), (1, "bulk", right)):
            copies.append(
                pltpu.make_async_remote_copy(
                    src_ref=zs.at[step, pl.ds(x * HALF, HALF)],
                    dst_ref=halo_x.at[step, 1 - x],
                    send_sem=hx_ssem.at[step, x],
                    recv_sem=hx_rsem.at[step, 1 - x],
                    device_id={axis: target},
                    device_id_type=pl.DeviceIdType.MESH,
                )
            )
        for x in range(CX):
            for side, row, target in ((0, HALF - 1, after), (1, 0, before)):
                copies.append(
                    pltpu.make_async_remote_copy(
                        src_ref=zs.at[step, x * HALF + row],
                        dst_ref=halo_y.at[step, x, side],
                        send_sem=hy_ssem.at[step, x, side],
                        recv_sem=hy_rsem.at[step, x, side],
                        device_id={"group": target},
                        device_id_type=pl.DeviceIdType.MESH,
                    )
                )
        return copies

    def finish_z(step):
        all_but_one(res_buf.at[step], ng, res_rsem.at[step]).wait()
        rows = AGGS * COMPS
        gathered = res_buf[step]
        gathered = jnp.concatenate([gathered, gathered], axis=1).reshape(ng * rows, LANES)
        both = mm(inv_rows[...], gathered)
        both = both[: 2 * rows] + both[2 * rows :]
        mixed = jnp.where(low_half((rows, LANES)), both[:rows], both[rows:])
        cor = mixed + pltpu.roll(mixed, COLS, 1)
        wide = jnp.concatenate([cor[k * COMPS : (k + 1) * COMPS] for k in range(AGGS)], axis=1)
        high, low = split_hi_lo(wide)
        wide = jnp.concatenate([high.astype(f32), low.astype(f32), high.astype(f32)], axis=0)
        wide = mm(bas_w[...], wide.astype(bf16))
        for k in range(AGGS):
            spread[k] = wide[:, k * LANES : (k + 1) * LANES]
        copies = halo_copies(step)

        def one(x, yy, carry):
            p = x * HALF + yy
            first = spread[agg_ref[x, yy]]
            second = spread[agg_ref[x, yy + HALF]]
            zs[step, p] = (local_y[p] + jnp.where(low64, first, second)).astype(bf16)
            return carry

        for x in range(CX):
            loop(HALF, functools.partial(one, x))
            copies[x].start()
            copies[2 + 2 * x].start()
            copies[3 + 2 * x].start()
        return copies

    def own_image(step):
        for x in range(CX):

            def one(yy, carry):
                p = x * HALF + yy
                own = pair_product(diag_t, p, zs[step, p])
                other = zs[step, (1 - x) * HALF + yy].astype(f32)
                acc[p] = own - coef[p, 1 - x] * other
                return carry

            loop(HALF, one)

    def wait_halo(step, copies):
        for n in (2, 3, 4, 5, 0, 1):
            copies[n].wait_recv()
        for x in range(CX):
            base = x * HALF
            last = zs[step, base + HALF - 1].astype(f32)
            first = zs[step, base].astype(f32)
            got = halo_y[step, x, 0].astype(f32)
            edge[x, 0] = pltpu.roll(jnp.where(low64, last, got), COLS, 1)
            got = halo_y[step, x, 1].astype(f32)
            edge[x, 1] = pltpu.roll(jnp.where(low64, got, first), COLS, 1)

    def image(step, x, yy, prev, following):
        p = x * HALF + yy
        value = acc[p] - coef[p, x] * halo_x[step, x, yy].astype(f32)
        return value - coef[p, 2] * prev - coef[p, 3] * following

    def sweep(step, tail, count):
        def run(x, yy, prev, following, sums):
            p = x * HALF + yy
            terms = tail(p, image(step, x, yy, prev, following))
            return tuple(
                s + jnp.sum((a * b).reshape(8, 8, LANES), axis=0) for s, (a, b) in zip(sums, terms)
            )

        sums = (jnp.zeros((8, LANES), f32),) * count
        for x in range(CX):
            base = x * HALF

            def one(row, sums):
                yy = row + 1
                prev = zs[step, base + yy - 1].astype(f32)
                following = zs[step, base + yy + 1].astype(f32)
                return run(x, yy, prev, following, sums)

            sums = run(x, 0, edge[x, 0], zs[step, base + 1].astype(f32), sums)
            sums = loop(HALF - 2, one, sums)
            sums = run(x, HALF - 1, zs[step, base + HALF - 2].astype(f32), edge[x, 1], sums)
        rows = [jnp.sum(s, axis=0, keepdims=True) for s in sums]
        rows += [jnp.zeros((1, LANES), f32)] * (8 - count)
        return jnp.concatenate(rows, axis=0)

    def sum_start(step, payload):
        sum_send[step] = payload
        sum_group[step, group] = payload

        def push(d, carry):
            pltpu.make_async_remote_copy(
                src_ref=sum_send.at[step],
                dst_ref=sum_group.at[step, group],
                send_sem=g_ssem.at[step],
                recv_sem=g_rsem.at[step],
                device_id={"group": lax.rem(group + d, ng)},
                device_id_type=pl.DeviceIdType.MESH,
            ).start()
            return carry

        lax.fori_loop(1, ng, push, 0)

    def sum_middle(step):
        all_but_one(sum_group.at[step], ng, g_rsem.at[step]).wait()
        partial = jnp.sum(sum_group[step], axis=0)
        tot_send[step] = partial
        sum_bulk[step, bulk] = partial

        def push(d, carry):
            pltpu.make_async_remote_copy(
                src_ref=tot_send.at[step],
                dst_ref=sum_bulk.at[step, bulk],
                send_sem=b_ssem.at[step],
                recv_sem=b_rsem.at[step],
                device_id={"bulk": lax.rem(bulk + d, nb)},
                device_id_type=pl.DeviceIdType.MESH,
            ).start()
            return carry

        lax.fori_loop(1, nb, push, 0)

    def sum_finish(step, count):
        all_but_one(sum_bulk.at[step], nb, b_rsem.at[step]).wait()
        total = jnp.sum(sum_bulk[step], axis=0)
        total = total + pltpu.roll(total, COLS, 1)
        return [jnp.broadcast_to(total[i : i + 1], (8, LANES)) for i in range(count)]

    def scaled(factor, value):
        return (factor * value.reshape(8, 8, LANES)).reshape(NS, LANES)

    pl.semaphore_wait(barrier, ng + nb - 2)
    coarse_send(0, k0)

    for copy in prec_loads:
        copy.wait()
    local_part(k0)

    for copy in inv_loads:
        copy.wait()
    rows = AGGS * COMPS
    turned = inv_raw[...]
    in_half = (lax.broadcasted_iota(jnp.int32, turned.shape, 1) & (rows - 1)) < rows // 2
    turned = jnp.concatenate(
        [jnp.where(in_half, turned, 0.0), jnp.where(in_half, 0.0, turned)], axis=0
    )
    high, low = split_hi_lo(turned)
    inv_rows[0 : 2 * rows] = high
    inv_rows[2 * rows :] = low

    for copy in diag_loads:
        copy.wait()

    def turn_diag(p, carry):
        both = diag_raw[p].astype(f32)
        diag_t[p, 0:NS] = jnp.transpose(both[:NS]).astype(bf16)
        diag_t[p, NS : 2 * NS] = jnp.transpose(both[NS:]).astype(bf16)
        return carry

    loop(PAIRS, turn_diag)

    copies0 = finish_z(0)

    small_loads[1].wait()
    small_loads[2].wait()
    face_of = lax.broadcasted_iota(jnp.int32, (CY, 4 * NS), 1) // NS
    cell_y = lax.broadcasted_iota(jnp.int32, (CY, 4 * NS), 0)
    for x in range(CX):
        opened = jnp.transpose(face_ref[x].astype(f32))
        mask = jnp.zeros((CY, 4 * NS), f32)
        for f in range(4):
            mask = jnp.where(face_of == f, opened[:, f : f + 1], mask)
        if x == 0:
            mask = jnp.where((face_of == 0) & (bulk == 0), 0.0, mask)
        if x == CX - 1:
            mask = jnp.where((face_of == 1) & (bulk == nb - 1), 0.0, mask)
        mask = jnp.where((face_of == 2) & (cell_y == 0) & (group == 0), 0.0, mask)
        mask = jnp.where((face_of == 3) & (cell_y == CY - 1) & (group == ng - 1), 0.0, mask)
        value = coup_ref[x] * mask
        first = value.astype(bf16).astype(f32)
        second = (value - first).astype(bf16).astype(f32)
        third = value - first - second
        spread_rows = jnp.transpose(jnp.concatenate([first, second, third], axis=0)).astype(bf16)

        def expand(yy, carry):
            row = lax.broadcasted_iota(jnp.int32, (3 * CY, LANES), 0) & (CY - 1)
            lane = lax.broadcasted_iota(jnp.int32, (3 * CY, LANES), 1)
            pick = jnp.where(row == yy + jnp.where(lane < COLS, 0, HALF), 1.0, 0.0).astype(bf16)
            wide = mm(spread_rows, pick)
            for f in range(4):
                coef[x * HALF + yy, f] = wide[f * NS : (f + 1) * NS]
            return carry

        loop(HALF, expand)

    own_image(0)
    wait_halo(0, copies0)

    def tail0(p, value):
        w0[p] = value
        start = k0[p]
        return ((start, start), (start, value), (value, value))

    payload = sweep(0, tail0, 3)

    coarse_send(1, w0)
    sum_start(0, payload)
    local_part(w0)
    sum_middle(0)
    copies1 = finish_z(1)
    own_image(1)
    wait_halo(1, copies1)
    sum_kk, sum_kw, sum_ww = sum_finish(0, 3)
    beta = jnp.sqrt(sum_kk + tiny_eps)
    s0 = 1.0 / beta
    h00 = sum_kw * s0 * s0
    g00 = sum_kk * s0 * s0
    left_sq = sum_ww * s0 * s0 - h00 * h00 * (2.0 - g00)
    h10u = jnp.sqrt(jnp.maximum(left_sq, 0.0) + tiny_eps)
    c1 = s0 / h10u
    c2 = h00 * s0 / h10u

    def tail1(p, value):
        image0 = w0[p]
        start = k0[p]
        vec = scaled(c1, image0) - scaled(c2, start)
        value = scaled(c1, value) - scaled(c2, image0)
        k1[p] = vec
        w1[p] = value
        return ((start, value), (vec, value), (value, value), (start, vec), (vec, vec))

    payload = sweep(1, tail1, 5)

    coarse_send(2, w1)
    sum_start(1, payload)
    local_part(w1)
    sum_middle(1)
    copies2 = finish_z(2)
    own_image(2)
    wait_halo(2, copies2)
    d_0w, d_1w, d_ww, d_01, d_11 = sum_finish(1, 5)
    h10 = jnp.sqrt(h10u * h10u * d_11 + tiny_eps)
    t1 = h10u / h10
    h01 = d_0w * s0 * t1
    h11 = d_1w * t1 * t1
    g01 = d_01 * s0 * t1
    g11 = d_11 * t1 * t1
    left_sq = (
        d_ww * t1 * t1
        - h01 * h01 * (2.0 - g00)
        - h11 * h11 * (2.0 - g11)
        + 2.0 * h01 * h11 * g01
    )
    h21u = jnp.sqrt(jnp.maximum(left_sq, 0.0) + tiny_eps)
    e1 = t1 / h21u
    e2 = h01 * s0 / h21u
    e3 = h11 * t1 / h21u

    def tail2(p, value):
        start = k0[p]
        vec1 = k1[p]
        image1 = w1[p]
        vec2 = scaled(e1, image1) - scaled(e2, start) - scaled(e3, vec1)
        value = scaled(e1, value) - scaled(e2, w0[p]) - scaled(e3, image1)
        return (
            (start, value),
            (vec1, value),
            (vec2, value),
            (value, value),
            (start, vec2),
            (vec1, vec2),
            (vec2, vec2),
        )

    payload = sweep(2, tail2, 7)
    sum_start(2, payload)
    sum_middle(2)
    q_0w, q_1w, q_2w, q_ww, q_02, q_12, q_22 = sum_finish(2, 7)
    h21 = jnp.sqrt(h21u * h21u * q_22 + tiny_eps)
    t2 = h21u / h21
    h02 = q_0w * s0 * t2
    h12 = q_1w * t1 * t2
    h22 = q_2w * t2 * t2
    g02 = q_02 * s0 * t2
    g12 = q_12 * t1 * t2
    g22 = q_22 * t2 * t2
    left_sq = (
        q_ww * t2 * t2
        - h02 * h02 * (2.0 - g00)
        - h12 * h12 * (2.0 - g11)
        - h22 * h22 * (2.0 - g22)
        + 2.0 * (h02 * h12 * g01 + h02 * h22 * g02 + h12 * h22 * g12)
    )
    h32 = jnp.sqrt(jnp.maximum(left_sq, 0.0) + tiny_eps)
    y0, y1, y2 = givens_solve([[h00, h10], [h01, h11, h21], [h02, h12, h22, h32]], beta)

    over = y2 * t2 / h21u
    a2 = over * t1
    on1 = y1 - over * h11
    a1 = on1 * t1 * c1
    a0 = y0 * s0 - over * h01 * s0 - on1 * t1 * c2

    def finish(p, carry):
        x = p // HALF
        yy = p % HALF
        total = (
            scaled(a0, zs[0, p].astype(f32))
            + scaled(a1, zs[1, p].astype(f32))
            + scaled(a2, zs[2, p].astype(f32))
        )
        out_ref[x, yy] = total[:, :COLS].astype(bf16)
        out_ref[x, yy + HALF] = pltpu.roll(total, COLS, 1)[:, :COLS].astype(bf16)
        return carry

    loop(PAIRS, finish)

    for step, copies in enumerate((copies0, copies1, copies2)):
        all_but_one(res_buf.at[step], ng, res_ssem.at[step]).wait()
        all_but_one(sum_group.at[step], ng, g_ssem.at[step]).wait()
        all_but_one(sum_bulk.at[step], nb, b_ssem.at[step]).wait()
        for copy in copies:
            copy.wait_send()


def body(nb, ng, rhs, diag_blocks, precond_blocks, coupling, face_open, agg_id, coarse_basis, coarse_inv):
    rows = AGGS * COMPS
    inverse = jnp.swapaxes(coarse_inv[0], 0, 1)
    any_spec = pl.BlockSpec(memory_space=pl.ANY)
    vmem_spec = pl.BlockSpec(memory_space=pltpu.VMEM)
    smem_spec = pl.BlockSpec(memory_space=pltpu.SMEM)
    field = pltpu.VMEM((PAIRS, NS, LANES), f32)
    dma = pltpu.SemaphoreType.DMA
    return pl.pallas_call(
        functools.partial(kernel, nb, ng),
        out_shape=jax.ShapeDtypeStruct(rhs.shape, bf16),
        in_specs=[any_spec, any_spec, any_spec, any_spec, any_spec, smem_spec, any_spec, any_spec],
        out_specs=vmem_spec,
        scratch_shapes=[
            pltpu.VMEM((CX, CY, 4 * NS), f32),
            pltpu.VMEM((CX, 4, CY), jnp.int32),
            pltpu.VMEM((COMPS, NS), f32),
            pltpu.VMEM((CX, CY, NS, COLS), bf16),
            pltpu.VMEM((PAIRS, 2 * NS, NS), bf16),
            pltpu.VMEM((PAIRS, 2 * NS, NS), bf16),
            pltpu.VMEM((PAIRS, 2 * NS, NS), bf16),
            pltpu.VMEM((rows, ng * rows), f32),
            pltpu.VMEM((4 * rows, ng * rows), bf16),
            pltpu.VMEM((PAIRS, 4, NS, LANES), f32),
            pltpu.VMEM((PAIRS, AGGS, 8, LANES), f32),
            pltpu.VMEM((2, 2 * COMPS, NS), bf16),
            pltpu.VMEM((NS, 3 * COMPS), bf16),
            field,
            field,
            field,
            field,
            field,
            field,
            pltpu.VMEM((ITERS, PAIRS, NS, LANES), bf16),
            pltpu.VMEM((AGGS, NS, LANES), f32),
            pltpu.VMEM((ITERS, rows // 2, LANES), bf16),
            pltpu.VMEM((ITERS, ng, rows // 2, LANES), bf16),
            pltpu.VMEM((ITERS, CX, HALF, NS, LANES), bf16),
            pltpu.VMEM((ITERS, CX, 2, NS, LANES), bf16),
            pltpu.VMEM((CX, 2, NS, LANES), f32),
            pltpu.VMEM((ITERS, 8, LANES), f32),
            pltpu.VMEM((ITERS, ng, 8, LANES), f32),
            pltpu.VMEM((ITERS, 8, LANES), f32),
            pltpu.VMEM((ITERS, nb, 8, LANES), f32),
            dma((13,)),
            dma((ITERS,)),
            dma((ITERS,)),
            dma((ITERS, CX)),
            dma((ITERS, CX)),
            dma((ITERS, CX, 2)),
            dma((ITERS, CX, 2)),
            dma((ITERS,)),
            dma((ITERS,)),
            dma((ITERS,)),
            dma((ITERS,)),
        ],
        compiler_params=pltpu.CompilerParams(
            collective_id=0, has_side_effects=True, vmem_limit_bytes=60 * 1024 * 1024
        ),
        cost_estimate=pl.CostEstimate(flops=200_000_000, bytes_accessed=3_000_000, transcendentals=0),
    )(
        rhs,
        diag_blocks,
        precond_blocks,
        coupling,
        jnp.swapaxes(face_open, 1, 2),
        agg_id,
        jnp.swapaxes(coarse_basis, 0, 1),
        inverse,
    )


def solution(mesh):
    in_specs = (
        P("bulk", "group", None, None),
        P("bulk", "group", None, None),
        P("bulk", "group", None, None),
        P("bulk", "group", None),
        P("bulk", "group", None),
        P("bulk", "group"),
        P(),
        P("bulk", None, "group"),
    )
    out_specs = P("bulk", "group", None, None)
    return jax.shard_map(
        functools.partial(body, mesh.shape["bulk"], mesh.shape["group"]),
        mesh=mesh,
        in_specs=in_specs,
        out_specs=out_specs,
        check_vma=False,
    )
```

```python
import functools

import jax
import jax.numpy as jnp
from jax import lax
from jax.experimental import pallas as pl
from jax.experimental.pallas import tpu as pltpu
from jax.sharding import PartitionSpec as P

NS = 64
COLS = 64
CX = 2
CY = 16
AGGS = 4
COMPS = 8
ITERS = 3
HALF = CY // 2
PAIRS = CX * HALF
LANES = 2 * COLS
UNROLL = 16

tiny_eps = 1e-06
f32 = jnp.float32
bf16 = jnp.bfloat16


def split_hi_lo(value):
    high = value.astype(bf16)
    low = (value - high.astype(f32)).astype(bf16)
    return high, low


def mm(left, right):
    return jnp.dot(left, right, preferred_element_type=f32)


def loop(count, step, carry=0, unroll=UNROLL):
    unroll = min(unroll, count)

    def several(start, carry):
        for i in range(unroll):
            carry = step(start * unroll + i, carry)
        return carry

    if unroll == count:
        return several(0, carry)
    return lax.fori_loop(0, count // unroll, several, carry)


def far_first(count):
    return sorted(range(1, count), key=lambda d: -min(d, count - d))


def far_targets(nb, bulk):
    along = 8 if nb % 8 == 0 else nb
    across = nb // along

    def hops(d):
        high, low = d // along, d % along
        return min(high, across - high) + min(low, along - low)

    base = (bulk // along) * along
    return [
        {"bulk": lax.rem(base + (d // along) * along, nb) + lax.rem(bulk + d % along, along)}
        for d in sorted(range(1, nb), key=lambda d: -hops(d))
    ]


def low_half(shape):
    return lax.broadcasted_iota(jnp.int32, shape, 1) < COLS


def givens_solve(hessen_cols, beta_norm):
    cosine_list = []
    sine_list = []
    target = [beta_norm] + [jnp.zeros_like(beta_norm) for _ in range(ITERS)]
    triangle = []
    for section in range(ITERS):
        column = list(hessen_cols[section])
        for earlier in range(section):
            upper = column[earlier]
            lower = column[earlier + 1]
            column[earlier] = cosine_list[earlier] * upper + sine_list[earlier] * lower
            column[earlier + 1] = -sine_list[earlier] * upper + cosine_list[earlier] * lower
        upper = column[section]
        lower = column[section + 1]
        radius = jnp.sqrt(upper * upper + lower * lower)
        cosine = upper / radius
        sine_val = lower / radius
        cosine_list.append(cosine)
        sine_list.append(sine_val)
        column[section] = radius
        carried = target[section]
        target[section] = cosine * carried
        target[section + 1] = -sine_val * carried
        triangle.append(column[: section + 1])
    result = [None] * ITERS
    for section in reversed(range(ITERS)):
        accumulated = target[section]
        for later in range(section + 1, ITERS):
            accumulated = accumulated - triangle[later][section] * result[later]
        result[section] = accumulated / triangle[section][section]
    return result


def kernel(
    nb,
    ng,
    rhs_hbm,
    diag_hbm,
    prec_hbm,
    coup_hbm,
    face_hbm,
    agg_ref,
    basis_hbm,
    inv_hbm,
    out_ref,
    coup_ref,
    face_ref,
    basis_ref,
    rhs_raw,
    prec,
    diag_raw,
    diag_t,
    inv_raw,
    inv_rows,
    coef,
    wtab,
    bas_t,
    bas_w,
    k0,
    w0,
    w1,
    acc,
    yb,
    zs,
    spread,
    res_send,
    res_buf,
    cor_send,
    cor_buf,
    halo_x,
    halo_y,
    wnb_x,
    wnb_y,
    sum_send,
    sum_group,
    tot_send,
    sum_bulk,
    load_sem,
    res_ssem,
    res_rsem,
    cor_ssem,
    cor_rsem,
    hx_ssem,
    hx_rsem,
    hy_ssem,
    hy_rsem,
    g_ssem,
    g_rsem,
    b_ssem,
    b_rsem,
):
    bulk = lax.axis_index("bulk")
    group = lax.axis_index("group")

    loads = [pltpu.make_async_copy(rhs_hbm, rhs_raw, load_sem.at[0])]
    prec_loads = []
    diag_loads = []
    for x in range(CX):
        for yh in range(2):
            n = x * 2 + yh
            src = (x, pl.ds(yh * HALF, HALF))
            dst = (pl.ds(x * HALF, HALF), pl.ds(yh * NS, NS))
            prec_loads.append(
                pltpu.make_async_copy(prec_hbm.at[src], prec.at[dst], load_sem.at[1 + n])
            )
            diag_loads.append(
                pltpu.make_async_copy(diag_hbm.at[src], diag_raw.at[dst], load_sem.at[5 + n])
            )
    inv_loads = [pltpu.make_async_copy(inv_hbm, inv_raw, load_sem.at[9])]
    small_loads = [
        pltpu.make_async_copy(basis_hbm, basis_ref, load_sem.at[10]),
        pltpu.make_async_copy(face_hbm, face_ref, load_sem.at[11]),
        pltpu.make_async_copy(coup_hbm, coup_ref, load_sem.at[12]),
    ]
    for copy in loads + small_loads + prec_loads + inv_loads + diag_loads:
        copy.start()

    barrier = pltpu.get_barrier_semaphore()

    near_group = [{"group": lax.rem(group + d, ng)} for d in far_first(ng)]
    far_bulk = far_targets(nb, bulk)
    for target in near_group + far_bulk:
        pl.semaphore_signal(barrier, inc=1, device_id=target, device_id_type=pl.DeviceIdType.MESH)

    rows = AGGS * COMPS
    low8 = low_half((8, LANES))
    low16 = low_half((rows // 2, LANES))
    low32 = low_half((rows, LANES))
    low64 = low_half((NS, LANES))
    row8 = lax.broadcasted_iota(jnp.int32, (8, LANES), 0)

    def make_weights(p, carry):
        x = p // HALF
        yy = p % HALF
        cell = jnp.where(low8, agg_ref[x, yy], agg_ref[x, yy + HALF])
        wtab[p] = jnp.where(cell == row8, 1.0, 0.0).astype(f32)
        return carry

    loop(PAIRS, make_weights)

    weight_scale = (AGGS / (CX * CY)) ** 0.5
    small_loads[0].wait()
    turned = basis_ref[...]
    high, low = split_hi_lo(turned)
    stacked = jnp.concatenate([high.astype(f32), high.astype(f32), low.astype(f32)], axis=0)
    bas_w[...] = jnp.transpose(stacked).astype(bf16)
    high, low = split_hi_lo(turned * weight_scale)
    bas_t[0] = jnp.concatenate([high, high], axis=0)
    bas_t[1] = jnp.concatenate([low, low], axis=0)

    loads[0].wait()

    def make_start(p, carry):
        x = p // HALF
        yy = p % HALF
        first = rhs_raw[x, yy].astype(f32)
        second = rhs_raw[x, yy + HALF].astype(f32)
        k0[p] = jnp.concatenate([first, second], axis=1)
        return carry

    loop(PAIRS, make_start)

    def remote(src, dst, ssem, rsem, target):
        return pltpu.make_async_remote_copy(
            src_ref=src,
            dst_ref=dst,
            send_sem=ssem,
            recv_sem=rsem,
            device_id=target,
            device_id_type=pl.DeviceIdType.MESH,
        )

    def all_but_one(buf, count, sem):
        return pltpu.make_async_copy(buf.at[pl.ds(0, count - 1)], buf.at[pl.ds(0, count - 1)], sem)

    def coarse_residual(step, field):
        def add(p, sums):
            value = field[p].reshape(8, 8, LANES)
            return tuple(sums[k] + wtab[p, k : k + 1] * value for k in range(AGGS))

        zero = jnp.zeros((8, 8, LANES), f32)
        sums = loop(PAIRS, add, (zero,) * AGGS)
        sums = [s.reshape(NS, LANES) for s in sums]
        parts = []
        for kl in range(2):
            keep = jnp.where(low64, sums[kl], sums[kl + 2])
            move = jnp.where(low64, sums[kl + 2], sums[kl])
            total = keep + pltpu.roll(move, COLS, 1)
            high, low = split_hi_lo(total)
            part = mm(bas_t[0], high) + mm(bas_t[0], low) + mm(bas_t[1], high)
            parts.append(part[:COMPS])
        res = jnp.concatenate(parts, axis=0).astype(bf16)
        res_send[step] = res
        res_buf[step, group] = res

    def coarse_push(step):
        for target in near_group:
            remote(
                res_send.at[step], res_buf.at[step, group], res_ssem.at[step], res_rsem.at[step], target
            ).start()

    def pair_product(mats, p, value):
        both = mm(mats[p], value)
        return jnp.where(low64, both[:NS], both[NS:])

    left = {"bulk": lax.rem(bulk + nb - 1, nb)}
    right = {"bulk": lax.rem(bulk + 1, nb)}
    before = {"group": lax.rem(group + ng - 1, ng)}
    after = {"group": lax.rem(group + 1, ng)}

    def edge_copies(src, dst_x, dst_y, n):
        copies = []
        for x, side in ((0, left), (1, right)):
            copies.append(
                remote(
                    src.at[pl.ds(x * HALF, HALF)],
                    dst_x.at[1 - x],
                    hx_ssem.at[n, x],
                    hx_rsem.at[n, 1 - x],
                    side,
                )
            )
        for x in range(CX):
            for end, row, side in ((0, HALF - 1, after), (1, 0, before)):
                copies.append(
                    remote(
                        src.at[x * HALF + row],
                        dst_y.at[x, end],
                        hy_ssem.at[n, x, end],
                        hy_rsem.at[n, x, end],
                        side,
                    )
                )
        return copies

    def local_part(step, field):
        copies = edge_copies(yb.at[step], halo_x.at[step], halo_y.at[step], step)

        def one(x, yy, carry):
            p = x * HALF + yy
            yb[step, p] = pair_product(prec, p, field[p].astype(bf16)).astype(bf16)
            return carry

        for x in range(CX):
            loop(HALF, functools.partial(one, x))
            copies[x].start()
            copies[2 + 2 * x].start()
            copies[3 + 2 * x].start()
        return copies

    def make_spread(n, cor):
        wide = jnp.concatenate([cor[k * COMPS : (k + 1) * COMPS] for k in range(AGGS)], axis=1)
        high, low = split_hi_lo(wide)
        wide = jnp.concatenate([high.astype(f32), low.astype(f32), high.astype(f32)], axis=0)
        wide = mm(bas_w[...], wide.astype(bf16))
        for k in range(AGGS):
            spread[n, k] = wide[:, k * LANES : (k + 1) * LANES]

    def cor_copies(step):
        return [
            remote(
                cor_send.at[step],
                cor_buf.at[step, slot],
                cor_ssem.at[step, slot],
                cor_rsem.at[step, slot],
                side,
            )
            for slot, side in ((0, right), (1, left), (2, after), (3, before))
        ]

    def coarse_solve(step):
        all_but_one(res_buf.at[step], ng, res_rsem.at[step]).wait()
        gathered = res_buf[step]
        gathered = jnp.concatenate([gathered, gathered], axis=1).reshape(ng * rows, LANES)
        both = mm(inv_rows[...], gathered)
        both = both[: 2 * rows] + both[2 * rows :]
        mixed = jnp.where(low32, both[:rows], both[rows:])
        cor = mixed + pltpu.roll(mixed, COLS, 1)
        cor_send[step] = jnp.where(low16, cor[: rows // 2], cor[rows // 2 :])
        copies = cor_copies(step)
        for copy in copies:
            copy.start()
        make_spread(4, cor)
        return copies

    def joined(n, weights, local):
        total = local.astype(f32).reshape(8, 8, LANES)
        for k in range(AGGS):
            total = total + weights[k : k + 1] * spread[n, k].reshape(8, 8, LANES)
        return total.reshape(NS, LANES).astype(bf16)

    def own_z(step):
        def one(p, carry):
            zs[step, p] = joined(4, wtab[p], yb[step, p])
            return carry

        loop(PAIRS, one)

    def own_image(step):
        def one(p, carry):
            x = p // HALF
            yy = p % HALF
            value = pair_product(diag_t, p, zs[step, p])
            value = value - coef[p, 1 - x] * zs[step, (1 - x) * HALF + yy].astype(f32)
            if yy > 0:
                value = value - coef[p, 2] * zs[step, p - 1].astype(f32)
            if yy < HALF - 1:
                value = value - coef[p, 3] * zs[step, p + 1].astype(f32)
            acc[p] = value
            return carry

        loop(PAIRS, one)

    def wait_edges(step, halos, cors):
        for n in range(4):
            cors[n].wait_recv()
        for n in range(4):
            got = cor_buf[step, n]
            swapped = pltpu.roll(got, COLS, 1)
            make_spread(
                n,
                jnp.concatenate(
                    [jnp.where(low16, got, swapped), jnp.where(low16, swapped, got)], axis=0
                ),
            )
        for copy in halos:
            copy.wait_recv()

    def sweep(step, tail, count):
        sums = [jnp.zeros((8, LANES), f32)] * count
        for p in range(PAIRS):
            x = p // HALF
            yy = p % HALF
            beside = joined(x, wnb_x[x, yy], halo_x[step, x, yy]).astype(f32)
            value = acc[p] - coef[p, x] * beside
            if yy == 0:
                got = joined(2, wnb_y[x, 0], halo_y[step, x, 0]).astype(f32)
                own = zs[step, p + HALF - 1].astype(f32)
                value = value - coef[p, 2] * pltpu.roll(jnp.where(low64, own, got), COLS, 1)
            if yy == HALF - 1:
                got = joined(3, wnb_y[x, 1], halo_y[step, x, 1]).astype(f32)
                own = zs[step, p - HALF + 1].astype(f32)
                value = value - coef[p, 3] * pltpu.roll(jnp.where(low64, got, own), COLS, 1)
            terms = tail(p, value)
            sums = [
                s + jnp.sum((a * b).reshape(8, 8, LANES), axis=0) for s, (a, b) in zip(sums, terms)
            ]
        if not sums:
            return None
        sums = [jnp.sum(s, axis=0, keepdims=True) for s in sums]
        sums += [sums[-1]] * (count % 2)
        first = jnp.concatenate(sums[0::2], axis=0)
        second = jnp.concatenate(sums[1::2], axis=0)
        low = low_half(first.shape)
        packed = jnp.where(low, first, second)
        packed = packed + pltpu.roll(jnp.where(low, second, first), COLS, 1)
        return jnp.concatenate([packed, jnp.zeros((8 - packed.shape[0], LANES), f32)], axis=0)

    def sum_start(n, payload):
        sum_send[n] = payload
        sum_group[n, group] = payload
        for target in near_group:
            remote(
                sum_send.at[n], sum_group.at[n, group], g_ssem.at[n], g_rsem.at[n], target
            ).start()

    def sum_middle(n):
        all_but_one(sum_group.at[n], ng, g_rsem.at[n]).wait()
        partial = jnp.sum(sum_group[n], axis=0)
        tot_send[n] = partial
        sum_bulk[n, bulk] = partial
        for target in far_bulk:
            remote(tot_send.at[n], sum_bulk.at[n, bulk], b_ssem.at[n], b_rsem.at[n], target).start()

    def sum_finish(n, count):
        all_but_one(sum_bulk.at[n], nb, b_rsem.at[n]).wait()
        total = jnp.sum(sum_bulk[n], axis=0)
        swapped = pltpu.roll(total, COLS, 1)
        halves = (jnp.where(low8, total, swapped), jnp.where(low8, swapped, total))
        return [
            jnp.broadcast_to(halves[i % 2][i // 2 : i // 2 + 1], (8, LANES)) for i in range(count)
        ]

    def scaled(factor, value):
        return (factor * value.reshape(8, 8, LANES)).reshape(NS, LANES)

    coarse_residual(0, k0)
    pl.semaphore_wait(barrier, ng + nb - 2)
    coarse_push(0)
    weight_copies = edge_copies(wtab, wnb_x, wnb_y, ITERS)
    for copy in weight_copies:
        copy.start()

    for copy in prec_loads:
        copy.wait()
    halos0 = local_part(0, k0)

    for copy in inv_loads:
        copy.wait()
    turned = inv_raw[...]
    in_half = (lax.broadcasted_iota(jnp.int32, turned.shape, 1) & (rows - 1)) < rows // 2
    turned = jnp.concatenate(
        [jnp.where(in_half, turned, 0.0), jnp.where(in_half, 0.0, turned)], axis=0
    )
    high, low = split_hi_lo(turned)
    inv_rows[0 : 2 * rows] = high
    inv_rows[2 * rows :] = low

    for copy in diag_loads:
        copy.wait()

    def turn_diag(p, carry):
        both = diag_raw[p].astype(f32)
        diag_t[p, 0:NS] = jnp.transpose(both[:NS]).astype(bf16)
        diag_t[p, NS : 2 * NS] = jnp.transpose(both[NS:]).astype(bf16)
        return carry

    loop(PAIRS, turn_diag)

    small_loads[1].wait()
    small_loads[2].wait()
    face_of = lax.broadcasted_iota(jnp.int32, (CY, 4 * NS), 1) // NS
    cell_y = lax.broadcasted_iota(jnp.int32, (CY, 4 * NS), 0)
    for x in range(CX):
        opened = jnp.transpose(face_ref[x].astype(f32))
        mask = jnp.zeros((CY, 4 * NS), f32)
        for f in range(4):
            mask = jnp.where(face_of == f, opened[:, f : f + 1], mask)
        if x == 0:
            mask = jnp.where((face_of == 0) & (bulk == 0), 0.0, mask)
        if x == CX - 1:
            mask = jnp.where((face_of == 1) & (bulk == nb - 1), 0.0, mask)
        mask = jnp.where((face_of == 2) & (cell_y == 0) & (group == 0), 0.0, mask)
        mask = jnp.where((face_of == 3) & (cell_y == CY - 1) & (group == ng - 1), 0.0, mask)
        value = coup_ref[x] * mask
        first = value.astype(bf16).astype(f32)
        second = (value - first).astype(bf16).astype(f32)
        third = value - first - second
        spread_rows = jnp.transpose(jnp.concatenate([first, second, third], axis=0)).astype(bf16)

        def expand(yy, carry):
            row = lax.broadcasted_iota(jnp.int32, (3 * CY, LANES), 0) & (CY - 1)
            lane = lax.broadcasted_iota(jnp.int32, (3 * CY, LANES), 1)
            pick = jnp.where(row == yy + jnp.where(lane < COLS, 0, HALF), 1.0, 0.0).astype(bf16)
            wide = mm(spread_rows, pick)
            for f in range(4):
                coef[x * HALF + yy, f] = wide[f * NS : (f + 1) * NS]
            return carry

        loop(HALF, expand)

    cors0 = coarse_solve(0)
    own_z(0)
    own_image(0)
    for copy in weight_copies:
        copy.wait_recv()
    wait_edges(0, halos0, cors0)

    def tail0(p, value):
        w0[p] = value
        start = k0[p]
        return ((start, start), (start, value), (value, value))

    payload = sweep(0, tail0, 3)

    coarse_residual(1, w0)
    coarse_push(1)
    halos1 = local_part(1, w0)
    sum_start(0, payload)
    cors1 = coarse_solve(1)
    own_z(1)
    own_image(1)
    wait_edges(1, halos1, cors1)

    def tail1(p, value):
        w1[p] = value
        return ()

    sweep(1, tail1, 0)

    coarse_residual(2, w1)
    coarse_push(2)
    halos2 = local_part(2, w1)
    sum_middle(0)
    cors2 = coarse_solve(2)
    own_z(2)
    own_image(2)
    sum_kk, sum_kw, sum_ww = sum_finish(0, 3)
    beta = jnp.sqrt(sum_kk + tiny_eps)
    s0 = 1.0 / beta
    h00 = sum_kw * s0 * s0
    g00 = sum_kk * s0 * s0
    ww0 = sum_ww * s0 * s0
    h10u = jnp.sqrt(jnp.maximum(ww0 - h00 * h00 * (2.0 - g00), 0.0) + tiny_eps)
    c1 = s0 / h10u
    c2 = h00 * c1
    wait_edges(2, halos2, cors2)

    def tail2(p, value):
        start = k0[p]
        raw0 = w0[p]
        raw1 = w1[p]
        vec1 = scaled(c1, raw0) - scaled(c2, start)
        image1 = scaled(c1, raw1) - scaled(c2, raw0)
        image2 = scaled(c1, value) - scaled(c2, raw1)
        return (
            (start, vec1),
            (vec1, vec1),
            (start, image1),
            (vec1, image1),
            (image1, image1),
            (start, image2),
            (vec1, image2),
            (image1, image2),
            (image2, image2),
        )

    payload = sweep(2, tail2, 9)
    sum_start(1, payload)
    sum_middle(1)
    d_01, d_11, d_0w, d_1w, d_ww, d_0v, d_1v, d_wv, d_vv = sum_finish(1, 9)

    h10 = jnp.sqrt(h10u * h10u * d_11 + tiny_eps)
    t1 = h10u / h10
    t1s = t1 * t1
    g01 = d_01 * s0 * t1
    g11 = d_11 * t1s
    h01 = d_0w * s0 * t1
    h11 = d_1w * t1s
    ww1 = d_ww * t1s
    n1 = ww1 - h01 * h01 * (2.0 - g00) - h11 * h11 * (2.0 - g11) + 2.0 * h01 * h11 * g01
    n1 = jnp.maximum(n1, 0.0)
    h21 = jnp.sqrt(n1 + tiny_eps)
    i21 = 1.0 / h21
    v0 = d_0v * s0 * t1
    v1 = d_1v * t1s
    vw = d_wv * t1s
    vv = d_vv * t1s
    k1w0 = h00 * g01 + h10 * g11
    w1w0 = h00 * h01 + h10 * h11
    vw0 = h00 * v0 + h10 * v1
    h02 = (v0 - h01 * h00 - h11 * h01) * i21
    h12 = (v1 - h01 * k1w0 - h11 * h11) * i21
    w1w2 = (vw - h01 * w1w0 - h11 * ww1) * i21
    h22 = (w1w2 - h01 * h02 - h11 * h12) * i21
    ww2 = vv + h01 * h01 * ww0 + h11 * h11 * ww1
    ww2 = (ww2 - 2.0 * (h01 * vw0 + h11 * vw - h01 * h11 * w1w0)) * i21 * i21
    g02 = (h01 - h01 * g00 - h11 * g01) * i21
    g12 = (h11 - h01 * g01 - h11 * g11) * i21
    g22 = n1 * i21 * i21
    n2 = ww2 - h02 * h02 * (2.0 - g00) - h12 * h12 * (2.0 - g11) - h22 * h22 * (2.0 - g22)
    n2 = n2 + 2.0 * (h02 * h12 * g01 + h02 * h22 * g02 + h12 * h22 * g12)
    h32 = jnp.sqrt(jnp.maximum(n2, 0.0) + tiny_eps)
    y0, y1, y2 = givens_solve([[h00, h10], [h01, h11, h21], [h02, h12, h22, h32]], beta)

    over = y2 * i21
    on1 = y1 - over * h11
    a2 = over * t1 * c1
    a1 = on1 * t1 * c1 - over * t1 * c2
    a0 = y0 * s0 - over * h01 * s0 - on1 * t1 * c2

    def finish(p, carry):
        x = p // HALF
        yy = p % HALF
        total = (
            scaled(a0, zs[0, p].astype(f32))
            + scaled(a1, zs[1, p].astype(f32))
            + scaled(a2, zs[2, p].astype(f32))
        )
        out_ref[x, yy] = total[:, :COLS].astype(bf16)
        out_ref[x, yy + HALF] = pltpu.roll(total, COLS, 1)[:, :COLS].astype(bf16)
        return carry

    loop(PAIRS, finish)

    for step, copies in enumerate((halos0 + cors0, halos1 + cors1, halos2 + cors2)):
        all_but_one(res_buf.at[step], ng, res_ssem.at[step]).wait()
        for copy in copies:
            copy.wait_send()
    for copy in weight_copies:
        copy.wait_send()
    for n in range(2):
        all_but_one(sum_group.at[n], ng, g_ssem.at[n]).wait()
        all_but_one(sum_bulk.at[n], nb, b_ssem.at[n]).wait()


def body(nb, ng, rhs, diag_blocks, precond_blocks, coupling, face_open, agg_id, coarse_basis, coarse_inv):
    rows = AGGS * COMPS
    inverse = jnp.swapaxes(coarse_inv[0], 0, 1)
    any_spec = pl.BlockSpec(memory_space=pl.ANY)
    vmem_spec = pl.BlockSpec(memory_space=pltpu.VMEM)
    smem_spec = pl.BlockSpec(memory_space=pltpu.SMEM)
    field = pltpu.VMEM((PAIRS, NS, LANES), f32)
    dma = pltpu.SemaphoreType.DMA
    return pl.pallas_call(
        functools.partial(kernel, nb, ng),
        out_shape=jax.ShapeDtypeStruct(rhs.shape, bf16),
        in_specs=[any_spec, any_spec, any_spec, any_spec, any_spec, smem_spec, any_spec, any_spec],
        out_specs=vmem_spec,
        scratch_shapes=[
            pltpu.VMEM((CX, CY, 4 * NS), f32),
            pltpu.VMEM((CX, 4, CY), jnp.int32),
            pltpu.VMEM((COMPS, NS), f32),
            pltpu.VMEM((CX, CY, NS, COLS), bf16),
            pltpu.VMEM((PAIRS, 2 * NS, NS), bf16),
            pltpu.VMEM((PAIRS, 2 * NS, NS), bf16),
            pltpu.VMEM((PAIRS, 2 * NS, NS), bf16),
            pltpu.VMEM((rows, ng * rows), f32),
            pltpu.VMEM((4 * rows, ng * rows), bf16),
            pltpu.VMEM((PAIRS, 4, NS, LANES), f32),
            pltpu.VMEM((PAIRS, 8, LANES), f32),
            pltpu.VMEM((2, 2 * COMPS, NS), bf16),
            pltpu.VMEM((NS, 3 * COMPS), bf16),
            field,
            field,
            field,
            field,
            pltpu.VMEM((ITERS, PAIRS, NS, LANES), bf16),
            pltpu.VMEM((ITERS, PAIRS, NS, LANES), bf16),
            pltpu.VMEM((5, AGGS, NS, LANES), f32),
            pltpu.VMEM((ITERS, rows // 2, LANES), bf16),
            pltpu.VMEM((ITERS, ng, rows // 2, LANES), bf16),
            pltpu.VMEM((ITERS, rows // 2, LANES), f32),
            pltpu.VMEM((ITERS, 4, rows // 2, LANES), f32),
            pltpu.VMEM((ITERS, CX, HALF, NS, LANES), bf16),
            pltpu.VMEM((ITERS, CX, 2, NS, LANES), bf16),
            pltpu.VMEM((CX, HALF, 8, LANES), f32),
            pltpu.VMEM((CX, 2, 8, LANES), f32),
            pltpu.VMEM((2, 8, LANES), f32),
            pltpu.VMEM((2, ng, 8, LANES), f32),
            pltpu.VMEM((2, 8, LANES), f32),
            pltpu.VMEM((2, nb, 8, LANES), f32),
            dma((13,)),
            dma((ITERS,)),
            dma((ITERS,)),
            dma((ITERS, 4)),
            dma((ITERS, 4)),
            dma((ITERS + 1, CX)),
            dma((ITERS + 1, CX)),
            dma((ITERS + 1, CX, 2)),
            dma((ITERS + 1, CX, 2)),
            dma((2,)),
            dma((2,)),
            dma((2,)),
            dma((2,)),
        ],
        compiler_params=pltpu.CompilerParams(
            collective_id=0, has_side_effects=True, vmem_limit_bytes=60 * 1024 * 1024
        ),
        cost_estimate=pl.CostEstimate(flops=200_000_000, bytes_accessed=3_000_000, transcendentals=0),
    )(
        rhs,
        diag_blocks,
        precond_blocks,
        coupling,
        jnp.swapaxes(face_open, 1, 2),
        agg_id,
        jnp.swapaxes(coarse_basis, 0, 1),
        inverse,
    )


def solution(mesh):
    in_specs = (
        P("bulk", "group", None, None),
        P("bulk", "group", None, None),
        P("bulk", "group", None, None),
        P("bulk", "group", None),
        P("bulk", "group", None),
        P("bulk", "group"),
        P(),
        P("bulk", None, "group"),
    )
    out_specs = P("bulk", "group", None, None)
    return jax.shard_map(
        functools.partial(body, mesh.shape["bulk"], mesh.shape["group"]),
        mesh=mesh,
        in_specs=in_specs,
        out_specs=out_specs,
        check_vma=False,
    )
```

```python
import functools

import jax
import jax.numpy as jnp
from jax import lax
from jax.experimental import pallas as pl
from jax.experimental.pallas import tpu as pltpu
from jax.sharding import PartitionSpec as P

NS = 64
COLS = 64
CX = 2
CY = 16
AGGS = 4
COMPS = 8
ITERS = 3
HALF = CY // 2
PAIRS = CX * HALF
LANES = 2 * COLS
UNROLL = 16

tiny_eps = 1e-06
f32 = jnp.float32
bf16 = jnp.bfloat16


def split_hi_lo(value):
    high = value.astype(bf16)
    low = (value - high.astype(f32)).astype(bf16)
    return high, low


def mm(left, right):
    return jnp.dot(left, right, preferred_element_type=f32)


def loop(count, step, carry=0, unroll=UNROLL):
    unroll = min(unroll, count)

    def several(start, carry):
        for i in range(unroll):
            carry = step(start * unroll + i, carry)
        return carry

    if unroll == count:
        return several(0, carry)
    return lax.fori_loop(0, count // unroll, several, carry)


def far_first(count):
    return sorted(range(1, count), key=lambda d: -min(d, count - d))


def far_targets(nb, bulk):
    along = 8 if nb % 8 == 0 else nb
    across = nb // along

    def hops(d):
        high, low = d // along, d % along
        return min(high, across - high) + min(low, along - low)

    base = (bulk // along) * along
    return [
        {"bulk": lax.rem(base + (d // along) * along, nb) + lax.rem(bulk + d % along, along)}
        for d in sorted(range(1, nb), key=lambda d: -hops(d))
    ]


def low_half(shape):
    return lax.broadcasted_iota(jnp.int32, shape, 1) < COLS


def givens_solve(hessen_cols, beta_norm):
    cosine_list = []
    sine_list = []
    target = [beta_norm] + [jnp.zeros_like(beta_norm) for _ in range(ITERS)]
    triangle = []
    for section in range(ITERS):
        column = list(hessen_cols[section])
        for earlier in range(section):
            upper = column[earlier]
            lower = column[earlier + 1]
            column[earlier] = cosine_list[earlier] * upper + sine_list[earlier] * lower
            column[earlier + 1] = -sine_list[earlier] * upper + cosine_list[earlier] * lower
        upper = column[section]
        lower = column[section + 1]
        radius = jnp.sqrt(upper * upper + lower * lower)
        cosine = upper / radius
        sine_val = lower / radius
        cosine_list.append(cosine)
        sine_list.append(sine_val)
        column[section] = radius
        carried = target[section]
        target[section] = cosine * carried
        target[section + 1] = -sine_val * carried
        triangle.append(column[: section + 1])
    result = [None] * ITERS
    for section in reversed(range(ITERS)):
        accumulated = target[section]
        for later in range(section + 1, ITERS):
            accumulated = accumulated - triangle[later][section] * result[later]
        result[section] = accumulated / triangle[section][section]
    return result


def kernel(
    nb,
    ng,
    rhs_hbm,
    diag_hbm,
    prec_hbm,
    coup_hbm,
    face_hbm,
    agg_hbm,
    basis_hbm,
    inv_hbm,
    out_ref,
    coup_ref,
    face_ref,
    agg_ref,
    basis_ref,
    rhs_raw,
    prec,
    diag_raw,
    diag_t,
    inv_raw,
    inv_rows,
    coef,
    wtab,
    bas_t,
    bas_w,
    k0,
    w0,
    w1,
    acc,
    yb,
    zs,
    spread,
    res_send,
    res_buf,
    cor_send,
    cor_buf,
    halo_x,
    halo_y,
    wnb_x,
    wnb_y,
    sum_send,
    sum_group,
    tot_send,
    sum_bulk,
    load_sem,
    res_ssem,
    res_rsem,
    cor_ssem,
    cor_rsem,
    hx_ssem,
    hx_rsem,
    hy_ssem,
    hy_rsem,
    g_ssem,
    g_rsem,
    b_ssem,
    b_rsem,
):
    bulk = lax.axis_index("bulk")
    group = lax.axis_index("group")

    loads = [pltpu.make_async_copy(rhs_hbm, rhs_raw, load_sem.at[0])]
    prec_loads = []
    diag_loads = []
    for x in range(CX):
        for yh in range(2):
            n = x * 2 + yh
            src = (x, pl.ds(yh * HALF, HALF))
            dst = (pl.ds(x * HALF, HALF), pl.ds(yh * NS, NS))
            prec_loads.append(
                pltpu.make_async_copy(prec_hbm.at[src], prec.at[dst], load_sem.at[1 + n])
            )
            diag_loads.append(
                pltpu.make_async_copy(diag_hbm.at[src], diag_raw.at[dst], load_sem.at[5 + n])
            )
    inv_loads = [pltpu.make_async_copy(inv_hbm, inv_raw, load_sem.at[9])]
    small_loads = [
        pltpu.make_async_copy(basis_hbm, basis_ref, load_sem.at[10]),
        pltpu.make_async_copy(face_hbm, face_ref, load_sem.at[11]),
        pltpu.make_async_copy(coup_hbm, coup_ref, load_sem.at[12]),
        pltpu.make_async_copy(agg_hbm, agg_ref, load_sem.at[13]),
    ]
    for copy in loads + small_loads + prec_loads + inv_loads + diag_loads:
        copy.start()

    barrier = pltpu.get_barrier_semaphore()

    near_group = [{"group": lax.rem(group + d, ng)} for d in far_first(ng)]
    far_bulk = far_targets(nb, bulk)
    for target in near_group + far_bulk:
        pl.semaphore_signal(barrier, inc=1, device_id=target, device_id_type=pl.DeviceIdType.MESH)

    rows = AGGS * COMPS
    low8 = low_half((8, LANES))
    low16 = low_half((rows // 2, LANES))
    low32 = low_half((rows, LANES))
    low64 = low_half((NS, LANES))
    row8 = lax.broadcasted_iota(jnp.int32, (8, LANES), 0)

    def make_weights(p, carry):
        x = p // HALF
        yy = p % HALF
        cell = jnp.where(low8, agg_ref[x, yy], agg_ref[x, yy + HALF])
        wtab[p] = jnp.where(cell == row8, 1.0, 0.0).astype(f32)
        return carry

    small_loads[3].wait()
    loop(PAIRS, make_weights)

    weight_scale = (AGGS / (CX * CY)) ** 0.5
    small_loads[0].wait()
    turned = basis_ref[...]
    high, low = split_hi_lo(turned)
    stacked = jnp.concatenate([high.astype(f32), high.astype(f32), low.astype(f32)], axis=0)
    bas_w[...] = jnp.transpose(stacked).astype(bf16)
    high, low = split_hi_lo(turned * weight_scale)
    bas_t[0] = jnp.concatenate([high, high], axis=0)
    bas_t[1] = jnp.concatenate([low, low], axis=0)

    loads[0].wait()

    def make_start(p, carry):
        x = p // HALF
        yy = p % HALF
        first = rhs_raw[x, yy].astype(f32)
        second = rhs_raw[x, yy + HALF].astype(f32)
        k0[p] = jnp.concatenate([first, second], axis=1)
        return carry

    loop(PAIRS, make_start)

    def remote(src, dst, ssem, rsem, target):
        return pltpu.make_async_remote_copy(
            src_ref=src,
            dst_ref=dst,
            send_sem=ssem,
            recv_sem=rsem,
            device_id=target,
            device_id_type=pl.DeviceIdType.MESH,
        )

    def all_but_one(buf, count, sem):
        return pltpu.make_async_copy(buf.at[pl.ds(0, count - 1)], buf.at[pl.ds(0, count - 1)], sem)

    def coarse_residual(step, field):
        def add(p, sums):
            value = field[p].reshape(8, 8, LANES)
            return tuple(sums[k] + wtab[p, k : k + 1] * value for k in range(AGGS))

        zero = jnp.zeros((8, 8, LANES), f32)
        sums = loop(PAIRS, add, (zero,) * AGGS)
        sums = [s.reshape(NS, LANES) for s in sums]
        parts = []
        for kl in range(2):
            keep = jnp.where(low64, sums[kl], sums[kl + 2])
            move = jnp.where(low64, sums[kl + 2], sums[kl])
            total = keep + pltpu.roll(move, COLS, 1)
            high, low = split_hi_lo(total)
            part = mm(bas_t[0], high) + mm(bas_t[0], low) + mm(bas_t[1], high)
            parts.append(part[:COMPS])
        res = jnp.concatenate(parts, axis=0).astype(bf16)
        res_send[step] = res
        res_buf[step, group] = res

    def coarse_push(step):
        for target in near_group:
            remote(
                res_send.at[step], res_buf.at[step, group], res_ssem.at[step], res_rsem.at[step], target
            ).start()

    def pair_product(mats, p, value):
        both = mm(mats[p], value)
        return jnp.where(low64, both[:NS], both[NS:])

    left = {"bulk": lax.rem(bulk + nb - 1, nb)}
    right = {"bulk": lax.rem(bulk + 1, nb)}
    before = {"group": lax.rem(group + ng - 1, ng)}
    after = {"group": lax.rem(group + 1, ng)}

    def edge_copies(src, dst_x, dst_y, n):
        copies = []
        for x, side in ((0, left), (1, right)):
            copies.append(
                remote(
                    src.at[pl.ds(x * HALF, HALF)],
                    dst_x.at[1 - x],
                    hx_ssem.at[n, x],
                    hx_rsem.at[n, 1 - x],
                    side,
                )
            )
        for x in range(CX):
            for end, row, side in ((0, HALF - 1, after), (1, 0, before)):
                copies.append(
                    remote(
                        src.at[x * HALF + row],
                        dst_y.at[x, end],
                        hy_ssem.at[n, x, end],
                        hy_rsem.at[n, x, end],
                        side,
                    )
                )
        return copies

    def local_part(step, field):
        copies = edge_copies(yb.at[step], halo_x.at[step], halo_y.at[step], step)

        def one(x, yy, carry):
            p = x * HALF + yy
            yb[step, p] = pair_product(prec, p, field[p].astype(bf16)).astype(bf16)
            return carry

        for x in range(CX):
            loop(HALF, functools.partial(one, x))
            copies[x].start()
            copies[2 + 2 * x].start()
            copies[3 + 2 * x].start()
        return copies

    def make_spread(n, cor):
        wide = jnp.concatenate([cor[k * COMPS : (k + 1) * COMPS] for k in range(AGGS)], axis=1)
        high, low = split_hi_lo(wide)
        wide = jnp.concatenate([high.astype(f32), low.astype(f32), high.astype(f32)], axis=0)
        wide = mm(bas_w[...], wide.astype(bf16))
        for k in range(AGGS):
            spread[n, k] = wide[:, k * LANES : (k + 1) * LANES]

    def cor_copies(step):
        return [
            remote(
                cor_send.at[step],
                cor_buf.at[step, slot],
                cor_ssem.at[step, slot],
                cor_rsem.at[step, slot],
                side,
            )
            for slot, side in ((0, right), (1, left), (2, after), (3, before))
        ]

    def coarse_solve(step):
        all_but_one(res_buf.at[step], ng, res_rsem.at[step]).wait()
        gathered = res_buf[step]
        gathered = jnp.concatenate([gathered, gathered], axis=1).reshape(ng * rows, LANES)
        both = mm(inv_rows[...], gathered)
        both = both[: 2 * rows] + both[2 * rows :]
        mixed = jnp.where(low32, both[:rows], both[rows:])
        cor = mixed + pltpu.roll(mixed, COLS, 1)
        cor_send[step] = jnp.where(low16, cor[: rows // 2], cor[rows // 2 :])
        copies = cor_copies(step)
        for copy in copies:
            copy.start()
        make_spread(4, cor)
        return copies

    def joined(n, weights, local):
        total = local.astype(f32).reshape(8, 8, LANES)
        for k in range(AGGS):
            total = total + weights[k : k + 1] * spread[n, k].reshape(8, 8, LANES)
        return total.reshape(NS, LANES).astype(bf16)

    def own_z(step):
        def one(p, carry):
            zs[step, p] = joined(4, wtab[p], yb[step, p])
            return carry

        loop(PAIRS, one)

    def own_image(step):
        def one(p, carry):
            x = p // HALF
            yy = p % HALF
            value = pair_product(diag_t, p, zs[step, p])
            value = value - coef[p, 1 - x] * zs[step, (1 - x) * HALF + yy].astype(f32)
            if yy > 0:
                value = value - coef[p, 2] * zs[step, p - 1].astype(f32)
            if yy < HALF - 1:
                value = value - coef[p, 3] * zs[step, p + 1].astype(f32)
            acc[p] = value
            return carry

        loop(PAIRS, one)

    def wait_edges(step, halos, cors):
        for n in range(4):
            cors[n].wait_recv()
        for n in range(4):
            got = cor_buf[step, n]
            swapped = pltpu.roll(got, COLS, 1)
            make_spread(
                n,
                jnp.concatenate(
                    [jnp.where(low16, got, swapped), jnp.where(low16, swapped, got)], axis=0
                ),
            )
        for copy in halos:
            copy.wait_recv()

    def sweep(step, tail, count):
        sums = [jnp.zeros((8, LANES), f32)] * count
        for p in range(PAIRS):
            x = p // HALF
            yy = p % HALF
            beside = joined(x, wnb_x[x, yy], halo_x[step, x, yy]).astype(f32)
            value = acc[p] - coef[p, x] * beside
            if yy == 0:
                got = joined(2, wnb_y[x, 0], halo_y[step, x, 0]).astype(f32)
                own = zs[step, p + HALF - 1].astype(f32)
                value = value - coef[p, 2] * pltpu.roll(jnp.where(low64, own, got), COLS, 1)
            if yy == HALF - 1:
                got = joined(3, wnb_y[x, 1], halo_y[step, x, 1]).astype(f32)
                own = zs[step, p - HALF + 1].astype(f32)
                value = value - coef[p, 3] * pltpu.roll(jnp.where(low64, got, own), COLS, 1)
            terms = tail(p, value)
            sums = [
                s + jnp.sum((a * b).reshape(8, 8, LANES), axis=0) for s, (a, b) in zip(sums, terms)
            ]
        if not sums:
            return None
        sums = [jnp.sum(s, axis=0, keepdims=True) for s in sums]
        sums += [sums[-1]] * (count % 2)
        first = jnp.concatenate(sums[0::2], axis=0)
        second = jnp.concatenate(sums[1::2], axis=0)
        low = low_half(first.shape)
        packed = jnp.where(low, first, second)
        packed = packed + pltpu.roll(jnp.where(low, second, first), COLS, 1)
        return jnp.concatenate([packed, jnp.zeros((8 - packed.shape[0], LANES), f32)], axis=0)

    def sum_start(n, payload):
        sum_send[n] = payload
        sum_group[n, group] = payload
        for target in near_group:
            remote(
                sum_send.at[n], sum_group.at[n, group], g_ssem.at[n], g_rsem.at[n], target
            ).start()

    def sum_middle(n):
        all_but_one(sum_group.at[n], ng, g_rsem.at[n]).wait()
        partial = jnp.sum(sum_group[n], axis=0)
        tot_send[n] = partial
        sum_bulk[n, bulk] = partial
        for target in far_bulk:
            remote(tot_send.at[n], sum_bulk.at[n, bulk], b_ssem.at[n], b_rsem.at[n], target).start()

    def sum_finish(n, count):
        all_but_one(sum_bulk.at[n], nb, b_rsem.at[n]).wait()
        total = jnp.sum(sum_bulk[n], axis=0)
        swapped = pltpu.roll(total, COLS, 1)
        halves = (jnp.where(low8, total, swapped), jnp.where(low8, swapped, total))
        return [
            jnp.broadcast_to(halves[i % 2][i // 2 : i // 2 + 1], (8, LANES)) for i in range(count)
        ]

    def scaled(factor, value):
        return (factor * value.reshape(8, 8, LANES)).reshape(NS, LANES)

    coarse_residual(0, k0)
    pl.semaphore_wait(barrier, ng + nb - 2)
    coarse_push(0)
    weight_copies = edge_copies(wtab, wnb_x, wnb_y, ITERS)
    for copy in weight_copies:
        copy.start()

    for copy in prec_loads:
        copy.wait()
    halos0 = local_part(0, k0)

    for copy in inv_loads:
        copy.wait()
    turned = inv_raw[...]
    in_half = (lax.broadcasted_iota(jnp.int32, turned.shape, 1) & (rows - 1)) < rows // 2
    turned = jnp.concatenate(
        [jnp.where(in_half, turned, 0.0), jnp.where(in_half, 0.0, turned)], axis=0
    )
    high, low = split_hi_lo(turned)
    inv_rows[0 : 2 * rows] = high
    inv_rows[2 * rows :] = low

    for copy in diag_loads:
        copy.wait()

    def turn_diag(p, carry):
        both = diag_raw[p].astype(f32)
        diag_t[p, 0:NS] = jnp.transpose(both[:NS]).astype(bf16)
        diag_t[p, NS : 2 * NS] = jnp.transpose(both[NS:]).astype(bf16)
        return carry

    loop(PAIRS, turn_diag)

    small_loads[1].wait()
    small_loads[2].wait()
    face_of = lax.broadcasted_iota(jnp.int32, (CY, 4 * NS), 1) // NS
    cell_y = lax.broadcasted_iota(jnp.int32, (CY, 4 * NS), 0)
    for x in range(CX):
        opened = jnp.transpose(face_ref[x].astype(f32))
        mask = jnp.zeros((CY, 4 * NS), f32)
        for f in range(4):
            mask = jnp.where(face_of == f, opened[:, f : f + 1], mask)
        if x == 0:
            mask = jnp.where((face_of == 0) & (bulk == 0), 0.0, mask)
        if x == CX - 1:
            mask = jnp.where((face_of == 1) & (bulk == nb - 1), 0.0, mask)
        mask = jnp.where((face_of == 2) & (cell_y == 0) & (group == 0), 0.0, mask)
        mask = jnp.where((face_of == 3) & (cell_y == CY - 1) & (group == ng - 1), 0.0, mask)
        value = coup_ref[x] * mask
        first = value.astype(bf16).astype(f32)
        second = (value - first).astype(bf16).astype(f32)
        third = value - first - second
        spread_rows = jnp.transpose(jnp.concatenate([first, second, third], axis=0)).astype(bf16)

        def expand(yy, carry):
            row = lax.broadcasted_iota(jnp.int32, (3 * CY, LANES), 0) & (CY - 1)
            lane = lax.broadcasted_iota(jnp.int32, (3 * CY, LANES), 1)
            pick = jnp.where(row == yy + jnp.where(lane < COLS, 0, HALF), 1.0, 0.0).astype(bf16)
            wide = mm(spread_rows, pick)
            for f in range(4):
                coef[x * HALF + yy, f] = wide[f * NS : (f + 1) * NS]
            return carry

        loop(HALF, expand)

    cors0 = coarse_solve(0)
    own_z(0)
    own_image(0)
    for copy in weight_copies:
        copy.wait_recv()
    wait_edges(0, halos0, cors0)

    def tail0(p, value):
        w0[p] = value
        start = k0[p]
        return ((start, start), (start, value), (value, value))

    payload = sweep(0, tail0, 3)

    coarse_residual(1, w0)
    coarse_push(1)
    halos1 = local_part(1, w0)
    sum_start(0, payload)
    cors1 = coarse_solve(1)
    own_z(1)
    own_image(1)
    sum_middle(0)
    wait_edges(1, halos1, cors1)

    def tail1(p, value):
        w1[p] = value
        return ()

    sweep(1, tail1, 0)

    coarse_residual(2, w1)
    coarse_push(2)
    halos2 = local_part(2, w1)
    cors2 = coarse_solve(2)
    own_z(2)
    own_image(2)
    sum_kk, sum_kw, sum_ww = sum_finish(0, 3)
    beta = jnp.sqrt(sum_kk + tiny_eps)
    s0 = 1.0 / beta
    h00 = sum_kw * s0 * s0
    g00 = sum_kk * s0 * s0
    ww0 = sum_ww * s0 * s0
    h10u = jnp.sqrt(jnp.maximum(ww0 - h00 * h00 * (2.0 - g00), 0.0) + tiny_eps)
    c1 = s0 / h10u
    c2 = h00 * c1
    wait_edges(2, halos2, cors2)

    def tail2(p, value):
        start = k0[p]
        raw0 = w0[p]
        raw1 = w1[p]
        vec1 = scaled(c1, raw0) - scaled(c2, start)
        image1 = scaled(c1, raw1) - scaled(c2, raw0)
        image2 = scaled(c1, value) - scaled(c2, raw1)
        return (
            (start, vec1),
            (vec1, vec1),
            (start, image1),
            (vec1, image1),
            (image1, image1),
            (start, image2),
            (vec1, image2),
            (image1, image2),
            (image2, image2),
        )

    payload = sweep(2, tail2, 9)
    sum_start(1, payload)
    sum_middle(1)
    d_01, d_11, d_0w, d_1w, d_ww, d_0v, d_1v, d_wv, d_vv = sum_finish(1, 9)

    h10 = jnp.sqrt(h10u * h10u * d_11 + tiny_eps)
    t1 = h10u / h10
    t1s = t1 * t1
    g01 = d_01 * s0 * t1
    g11 = d_11 * t1s
    h01 = d_0w * s0 * t1
    h11 = d_1w * t1s
    ww1 = d_ww * t1s
    n1 = ww1 - h01 * h01 * (2.0 - g00) - h11 * h11 * (2.0 - g11) + 2.0 * h01 * h11 * g01
    n1 = jnp.maximum(n1, 0.0)
    h21 = jnp.sqrt(n1 + tiny_eps)
    i21 = 1.0 / h21
    v0 = d_0v * s0 * t1
    v1 = d_1v * t1s
    vw = d_wv * t1s
    vv = d_vv * t1s
    k1w0 = h00 * g01 + h10 * g11
    w1w0 = h00 * h01 + h10 * h11
    vw0 = h00 * v0 + h10 * v1
    h02 = (v0 - h01 * h00 - h11 * h01) * i21
    h12 = (v1 - h01 * k1w0 - h11 * h11) * i21
    w1w2 = (vw - h01 * w1w0 - h11 * ww1) * i21
    h22 = (w1w2 - h01 * h02 - h11 * h12) * i21
    ww2 = vv + h01 * h01 * ww0 + h11 * h11 * ww1
    ww2 = (ww2 - 2.0 * (h01 * vw0 + h11 * vw - h01 * h11 * w1w0)) * i21 * i21
    g02 = (h01 - h01 * g00 - h11 * g01) * i21
    g12 = (h11 - h01 * g01 - h11 * g11) * i21
    g22 = n1 * i21 * i21
    n2 = ww2 - h02 * h02 * (2.0 - g00) - h12 * h12 * (2.0 - g11) - h22 * h22 * (2.0 - g22)
    n2 = n2 + 2.0 * (h02 * h12 * g01 + h02 * h22 * g02 + h12 * h22 * g12)
    h32 = jnp.sqrt(jnp.maximum(n2, 0.0) + tiny_eps)
    y0, y1, y2 = givens_solve([[h00, h10], [h01, h11, h21], [h02, h12, h22, h32]], beta)

    over = y2 * i21
    on1 = y1 - over * h11
    a2 = over * t1 * c1
    a1 = on1 * t1 * c1 - over * t1 * c2
    a0 = y0 * s0 - over * h01 * s0 - on1 * t1 * c2

    def finish(p, carry):
        x = p // HALF
        yy = p % HALF
        total = (
            scaled(a0, zs[0, p].astype(f32))
            + scaled(a1, zs[1, p].astype(f32))
            + scaled(a2, zs[2, p].astype(f32))
        )
        out_ref[x, yy] = total[:, :COLS].astype(bf16)
        out_ref[x, yy + HALF] = pltpu.roll(total, COLS, 1)[:, :COLS].astype(bf16)
        return carry

    loop(PAIRS, finish)

    for step, copies in enumerate((halos0 + cors0, halos1 + cors1, halos2 + cors2)):
        all_but_one(res_buf.at[step], ng, res_ssem.at[step]).wait()
        for copy in copies:
            copy.wait_send()
    for copy in weight_copies:
        copy.wait_send()
    for n in range(2):
        all_but_one(sum_group.at[n], ng, g_ssem.at[n]).wait()
        all_but_one(sum_bulk.at[n], nb, b_ssem.at[n]).wait()


def body(nb, ng, rhs, diag_blocks, precond_blocks, coupling, face_open, agg_id, coarse_basis, coarse_inv):
    rows = AGGS * COMPS
    inverse = jnp.swapaxes(coarse_inv[0], 0, 1)
    hbm_spec = pl.BlockSpec(memory_space=pltpu.HBM)
    vmem_spec = pl.BlockSpec(memory_space=pltpu.VMEM)
    field = pltpu.VMEM((PAIRS, NS, LANES), f32)
    dma = pltpu.SemaphoreType.DMA
    call = pl.pallas_call(
        functools.partial(kernel, nb, ng),
        out_shape=jax.ShapeDtypeStruct(rhs.shape, bf16),
        in_specs=[hbm_spec] * 8,
        out_specs=vmem_spec,
        scratch_shapes=[
            pltpu.VMEM((CX, CY, 4 * NS), f32),
            pltpu.VMEM((CX, 4, CY), jnp.int32),
            pltpu.SMEM((CX, CY), jnp.int32),
            pltpu.VMEM((COMPS, NS), f32),
            pltpu.VMEM((CX, CY, NS, COLS), bf16),
            pltpu.VMEM((PAIRS, 2 * NS, NS), bf16),
            pltpu.VMEM((PAIRS, 2 * NS, NS), bf16),
            pltpu.VMEM((PAIRS, 2 * NS, NS), bf16),
            pltpu.VMEM((rows, ng * rows), f32),
            pltpu.VMEM((4 * rows, ng * rows), bf16),
            pltpu.VMEM((PAIRS, 4, NS, LANES), f32),
            pltpu.VMEM((PAIRS, 8, LANES), f32),
            pltpu.VMEM((2, 2 * COMPS, NS), bf16),
            pltpu.VMEM((NS, 3 * COMPS), bf16),
            field,
            field,
            field,
            field,
            pltpu.VMEM((ITERS, PAIRS, NS, LANES), bf16),
            pltpu.VMEM((ITERS, PAIRS, NS, LANES), bf16),
            pltpu.VMEM((5, AGGS, NS, LANES), f32),
            pltpu.VMEM((ITERS, rows // 2, LANES), bf16),
            pltpu.VMEM((ITERS, ng, rows // 2, LANES), bf16),
            pltpu.VMEM((ITERS, rows // 2, LANES), f32),
            pltpu.VMEM((ITERS, 4, rows // 2, LANES), f32),
            pltpu.VMEM((ITERS, CX, HALF, NS, LANES), bf16),
            pltpu.VMEM((ITERS, CX, 2, NS, LANES), bf16),
            pltpu.VMEM((CX, HALF, 8, LANES), f32),
            pltpu.VMEM((CX, 2, 8, LANES), f32),
            pltpu.VMEM((2, 8, LANES), f32),
            pltpu.VMEM((2, ng, 8, LANES), f32),
            pltpu.VMEM((2, 8, LANES), f32),
            pltpu.VMEM((2, nb, 8, LANES), f32),
            dma((14,)),
            dma((ITERS,)),
            dma((ITERS,)),
            dma((ITERS, 4)),
            dma((ITERS, 4)),
            dma((ITERS + 1, CX)),
            dma((ITERS + 1, CX)),
            dma((ITERS + 1, CX, 2)),
            dma((ITERS + 1, CX, 2)),
            dma((2,)),
            dma((2,)),
            dma((2,)),
            dma((2,)),
        ],
        compiler_params=pltpu.CompilerParams(
            collective_id=0, has_side_effects=True, vmem_limit_bytes=32 * 1024 * 1024
        ),
        cost_estimate=pl.CostEstimate(flops=200_000_000, bytes_accessed=3_000_000, transcendentals=0),
    )
    operands = (
        rhs,
        diag_blocks,
        precond_blocks,
        coupling,
        jnp.swapaxes(face_open, 1, 2),
        agg_id,
        jnp.swapaxes(coarse_basis, 0, 1),
        inverse,
    )
    return call(*[pltpu.with_memory_space_constraint(x, pltpu.HBM) for x in operands])


def solution(mesh):
    in_specs = (
        P("bulk", "group", None, None),
        P("bulk", "group", None, None),
        P("bulk", "group", None, None),
        P("bulk", "group", None),
        P("bulk", "group", None),
        P("bulk", "group"),
        P(),
        P("bulk", None, "group"),
    )
    out_specs = P("bulk", "group", None, None)
    return jax.shard_map(
        functools.partial(body, mesh.shape["bulk"], mesh.shape["group"]),
        mesh=mesh,
        in_specs=in_specs,
        out_specs=out_specs,
        check_vma=False,
    )
```

```python
import functools

import jax
import jax.numpy as jnp
from jax import lax
from jax.experimental import pallas as pl
from jax.experimental.pallas import tpu as pltpu
from jax.sharding import PartitionSpec as P

NS = 64
COLS = 64
CX = 2
CY = 16
AGGS = 4
COMPS = 8
ITERS = 3
HALF = CY // 2
PAIRS = CX * HALF
LANES = 2 * COLS
UNROLL = 16

tiny_eps = 1e-06
f32 = jnp.float32
bf16 = jnp.bfloat16


def split_hi_lo(value):
    high = value.astype(bf16)
    low = (value - high.astype(f32)).astype(bf16)
    return high, low


def mm(left, right):
    return jnp.dot(left, right, preferred_element_type=f32)


def loop(count, step, carry=0, unroll=UNROLL):
    unroll = min(unroll, count)

    def several(start, carry):
        for i in range(unroll):
            carry = step(start * unroll + i, carry)
        return carry

    if unroll == count:
        return several(0, carry)
    return lax.fori_loop(0, count // unroll, several, carry)


def far_first(count):
    return sorted(range(1, count), key=lambda d: -min(d, count - d))


def far_targets(nb, bulk):
    along = 8 if nb % 8 == 0 else nb
    across = nb // along

    def hops(d):
        high, low = d // along, d % along
        return min(high, across - high) + min(low, along - low)

    base = (bulk // along) * along
    return [
        {"bulk": lax.rem(base + (d // along) * along, nb) + lax.rem(bulk + d % along, along)}
        for d in sorted(range(1, nb), key=lambda d: -hops(d))
    ]


def low_half(shape):
    return lax.broadcasted_iota(jnp.int32, shape, 1) < COLS


def givens_solve(hessen_cols, beta_norm):
    rotations = []
    target = [beta_norm] + [jnp.zeros_like(beta_norm) for _ in range(ITERS)]
    triangle = []
    for section in range(ITERS):
        column = list(hessen_cols[section])
        for earlier, (cosine, sine, _) in enumerate(rotations):
            upper = column[earlier]
            lower = column[earlier + 1]
            column[earlier] = cosine * upper + sine * lower
            column[earlier + 1] = cosine * lower - sine * upper
        upper = column[section]
        lower = column[section + 1]
        inverse = lax.rsqrt(upper * upper + lower * lower)
        rotations.append((upper * inverse, lower * inverse, inverse))
        carried = target[section]
        target[section] = rotations[-1][0] * carried
        target[section + 1] = -rotations[-1][1] * carried
        triangle.append(column[:section])
    result = [None] * ITERS
    for section in reversed(range(ITERS)):
        accumulated = target[section]
        for later in range(section + 1, ITERS):
            accumulated = accumulated - triangle[later][section] * result[later]
        result[section] = accumulated * rotations[section][2]
    return result


def kernel(
    nb,
    ng,
    rhs_hbm,
    diag_hbm,
    prec_hbm,
    coup_hbm,
    face_hbm,
    agg_hbm,
    basis_hbm,
    inv_hbm,
    out_ref,
    coup_ref,
    face_ref,
    agg_ref,
    basis_ref,
    rhs_raw,
    prec,
    diag_raw,
    diag_t,
    inv_raw,
    inv_rows,
    coef,
    wtab,
    bas_t,
    bas_w,
    k0,
    w0,
    w1,
    acc,
    yb,
    zs,
    spread,
    res_send,
    res_buf,
    cor_send,
    cor_buf,
    halo_x,
    halo_y,
    wnb_x,
    wnb_y,
    sum_send,
    sum_group,
    tot_send,
    sum_bulk,
    load_sem,
    res_ssem,
    res_rsem,
    cor_ssem,
    cor_rsem,
    hx_ssem,
    hx_rsem,
    hy_ssem,
    hy_rsem,
    g_ssem,
    g_rsem,
    b_ssem,
    b_rsem,
):
    bulk = lax.axis_index("bulk")
    group = lax.axis_index("group")

    loads = [pltpu.make_async_copy(rhs_hbm, rhs_raw, load_sem.at[0])]
    prec_loads = []
    diag_loads = []
    for x in range(CX):
        for yh in range(2):
            n = x * 2 + yh
            src = (x, pl.ds(yh * HALF, HALF))
            dst = (pl.ds(x * HALF, HALF), pl.ds(yh * NS, NS))
            prec_loads.append(
                pltpu.make_async_copy(prec_hbm.at[src], prec.at[dst], load_sem.at[1 + n])
            )
            diag_loads.append(
                pltpu.make_async_copy(diag_hbm.at[src], diag_raw.at[dst], load_sem.at[5 + n])
            )
    inv_loads = [pltpu.make_async_copy(inv_hbm, inv_raw, load_sem.at[9])]
    small_loads = [
        pltpu.make_async_copy(basis_hbm, basis_ref, load_sem.at[10]),
        pltpu.make_async_copy(face_hbm, face_ref, load_sem.at[11]),
        pltpu.make_async_copy(coup_hbm, coup_ref, load_sem.at[12]),
        pltpu.make_async_copy(agg_hbm, agg_ref, load_sem.at[13]),
    ]
    loads[0].start()

    barrier = pltpu.get_barrier_semaphore()

    near_group = [{"group": lax.rem(group + d, ng)} for d in far_first(ng)]
    far_bulk = far_targets(nb, bulk)
    for target in near_group + far_bulk:
        pl.semaphore_signal(barrier, inc=1, device_id=target, device_id_type=pl.DeviceIdType.MESH)
    for copy in small_loads + prec_loads + inv_loads + diag_loads:
        copy.start()

    rows = AGGS * COMPS
    low8 = low_half((8, LANES))
    low16 = low_half((rows // 2, LANES))
    low32 = low_half((rows, LANES))
    low64 = low_half((NS, LANES))
    row8 = lax.broadcasted_iota(jnp.int32, (8, LANES), 0)

    def make_weights(p, carry):
        x = p // HALF
        yy = p % HALF
        cell = jnp.where(low8, agg_ref[x, yy], agg_ref[x, yy + HALF])
        wtab[p] = jnp.where(cell == row8, 1.0, 0.0).astype(f32)
        return carry

    small_loads[3].wait()
    loop(PAIRS, make_weights)

    weight_scale = (AGGS / (CX * CY)) ** 0.5
    small_loads[0].wait()
    turned = basis_ref[...]
    high, low = split_hi_lo(turned)
    stacked = jnp.concatenate([high.astype(f32), high.astype(f32), low.astype(f32)], axis=0)
    bas_w[...] = jnp.transpose(stacked).astype(bf16)
    high, low = split_hi_lo(turned * weight_scale)
    stacked = jnp.concatenate([high.astype(f32), high.astype(f32), low.astype(f32)], axis=1)
    bas_t[...] = jnp.concatenate([stacked, stacked], axis=0).astype(bf16)

    loads[0].wait()

    def make_start(p, carry):
        x = p // HALF
        yy = p % HALF
        first = rhs_raw[x, yy].astype(f32)
        second = rhs_raw[x, yy + HALF].astype(f32)
        k0[p] = jnp.concatenate([first, second], axis=1)
        return carry

    loop(PAIRS, make_start)

    def remote(src, dst, ssem, rsem, target):
        return pltpu.make_async_remote_copy(
            src_ref=src,
            dst_ref=dst,
            send_sem=ssem,
            recv_sem=rsem,
            device_id=target,
            device_id_type=pl.DeviceIdType.MESH,
        )

    def all_but_one(buf, count, sem):
        return pltpu.make_async_copy(buf.at[pl.ds(0, count - 1)], buf.at[pl.ds(0, count - 1)], sem)

    def coarse_residual(step, field):
        def add(p, sums):
            value = field[p].reshape(8, 8, LANES)
            return tuple(sums[k] + wtab[p, k : k + 1] * value for k in range(AGGS))

        zero = jnp.zeros((8, 8, LANES), f32)
        sums = loop(PAIRS, add, (zero,) * AGGS)
        project(step, [s.reshape(NS, LANES) for s in sums])

    def project(step, sums):
        totals = []
        for kl in range(2):
            keep = jnp.where(low64, sums[kl], sums[kl + 2])
            move = jnp.where(low64, sums[kl + 2], sums[kl])
            totals.append(keep + pltpu.roll(move, COLS, 1))
        high, low = split_hi_lo(jnp.concatenate(totals, axis=1))
        part = mm(bas_t[...], jnp.concatenate([high, low, high], axis=0))[:COMPS]
        res = jnp.concatenate([part[:, :LANES], part[:, LANES:]], axis=0).astype(bf16)
        res_send[step] = res
        res_buf[step, group] = res

    def coarse_push(step):
        for target in near_group:
            remote(
                res_send.at[step], res_buf.at[step, group], res_ssem.at[step], res_rsem.at[step], target
            ).start()

    def pair_product(mats, p, value):
        both = mm(mats[p], value)
        return jnp.where(low64, both[:NS], both[NS:])

    left = {"bulk": lax.rem(bulk + nb - 1, nb)}
    right = {"bulk": lax.rem(bulk + 1, nb)}
    before = {"group": lax.rem(group + ng - 1, ng)}
    after = {"group": lax.rem(group + 1, ng)}

    def edge_copies(src, dst_x, dst_y, n):
        copies = []
        for x, side in ((0, left), (1, right)):
            copies.append(
                remote(
                    src.at[pl.ds(x * HALF, HALF)],
                    dst_x.at[1 - x],
                    hx_ssem.at[n, x],
                    hx_rsem.at[n, 1 - x],
                    side,
                )
            )
        for x in range(CX):
            for end, row, side in ((0, HALF - 1, after), (1, 0, before)):
                copies.append(
                    remote(
                        src.at[x * HALF + row],
                        dst_y.at[x, end],
                        hy_ssem.at[n, x, end],
                        hy_rsem.at[n, x, end],
                        side,
                    )
                )
        return copies

    def local_part(step, field):
        copies = edge_copies(yb.at[step], halo_x.at[step], halo_y.at[step], step)

        def one(x, yy, carry):
            p = x * HALF + yy
            yb[step, p] = pair_product(prec, p, field[p].astype(bf16)).astype(bf16)
            return carry

        for x in range(CX):
            loop(HALF, functools.partial(one, x))
            copies[x].start()
            copies[2 + 2 * x].start()
            copies[3 + 2 * x].start()
        return copies

    def make_spread(n, cor):
        wide = jnp.concatenate([cor[k * COMPS : (k + 1) * COMPS] for k in range(AGGS)], axis=1)
        high, low = split_hi_lo(wide)
        wide = jnp.concatenate([high.astype(f32), low.astype(f32), high.astype(f32)], axis=0)
        wide = mm(bas_w[...], wide.astype(bf16))
        for k in range(AGGS):
            spread[n, k] = wide[:, k * LANES : (k + 1) * LANES]

    def cor_copies(step):
        return [
            remote(
                cor_send.at[step],
                cor_buf.at[step, slot],
                cor_ssem.at[step, slot],
                cor_rsem.at[step, slot],
                side,
            )
            for slot, side in ((0, right), (1, left), (2, after), (3, before))
        ]

    def coarse_solve(step):
        all_but_one(res_buf.at[step], ng, res_rsem.at[step]).wait()
        gathered = res_buf[step]
        gathered = jnp.concatenate([gathered, gathered], axis=1).reshape(ng * rows, LANES)
        both = mm(inv_rows[...], gathered)
        both = both[: 2 * rows] + both[2 * rows :]
        mixed = jnp.where(low32, both[:rows], both[rows:])
        cor = mixed + pltpu.roll(mixed, COLS, 1)
        cor_send[step] = jnp.where(low16, cor[: rows // 2], cor[rows // 2 :])
        copies = cor_copies(step)
        for copy in copies:
            copy.start()
        make_spread(4, cor)
        return copies

    def joined(n, weights, local):
        total = local.astype(f32).reshape(8, 8, LANES)
        for k in range(AGGS):
            total = total + weights[k : k + 1] * spread[n, k].reshape(8, 8, LANES)
        return total.reshape(NS, LANES).astype(bf16)

    def own_z(step):
        def one(p, carry):
            zs[step, p] = joined(4, wtab[p], yb[step, p])
            return carry

        loop(PAIRS, one)

    def own_image(step):
        def one(p, carry):
            x = p // HALF
            yy = p % HALF
            value = pair_product(diag_t, p, zs[step, p])
            value = value - coef[p, 1 - x] * zs[step, (1 - x) * HALF + yy].astype(f32)
            if yy > 0:
                value = value - coef[p, 2] * zs[step, p - 1].astype(f32)
            if yy < HALF - 1:
                value = value - coef[p, 3] * zs[step, p + 1].astype(f32)
            acc[p] = value
            return carry

        loop(PAIRS, one)

    def wait_edges(step, halos, cors):
        for copy in halos:
            copy.wait_recv()
        for n in (2, 3, 0, 1):
            cors[n].wait_recv()
            got = cor_buf[step, n]
            swapped = pltpu.roll(got, COLS, 1)
            make_spread(
                n,
                jnp.concatenate(
                    [jnp.where(low16, got, swapped), jnp.where(low16, swapped, got)], axis=0
                ),
            )

    def add_terms(sums, terms):
        return [
            s + jnp.sum((a * b).reshape(-1, 8, LANES), axis=0) for s, (a, b) in zip(sums, terms)
        ]

    def sweep(step, tail, count, weight=None, next_step=None):
        sums = [jnp.zeros((8, LANES), f32)] * count
        chunk = 16
        low = low_half((chunk, LANES))
        chunks = []
        for start in range(0, NS, chunk):
            part = pl.ds(start, chunk)
            held = [[spread[n, k, part] for k in range(AGGS)] for n in range(2)]
            cells = [jnp.zeros((chunk, LANES), f32)] * AGGS

            def whole(n, weights, local):
                total = local.astype(f32)
                for k in range(AGGS):
                    total = total + weights[k : k + 1] * (held[n][k] if n < 2 else spread[n, k, part])
                return total.astype(bf16).astype(f32)

            for p in range(PAIRS):
                x = p // HALF
                yy = p % HALF
                value = coef[p, x, part] * whole(x, wnb_x[x, yy], halo_x[step, x, yy, part])
                if yy == 0:
                    got = whole(2, wnb_y[x, 0], halo_y[step, x, 0, part])
                    own = zs[step, p + HALF - 1, part].astype(f32)
                    moved = pltpu.roll(jnp.where(low, own, got), COLS, 1)
                    value = value + coef[p, 2, part] * moved
                if yy == HALF - 1:
                    got = whole(3, wnb_y[x, 1], halo_y[step, x, 1, part])
                    own = zs[step, p - HALF + 1, part].astype(f32)
                    moved = pltpu.roll(jnp.where(low, got, own), COLS, 1)
                    value = value + coef[p, 3, part] * moved
                if weight is not None:
                    value = scaled(weight, value)
                value = acc[p, part] - value
                sums = add_terms(sums, tail(p, part, value))
                if next_step is not None:
                    cells = [cells[k] + wtab[p, k : k + 1] * value for k in range(AGGS)]
            chunks.append(cells)
        if next_step is not None:
            project(
                next_step,
                [jnp.concatenate([c[k] for c in chunks], axis=0) for k in range(AGGS)],
            )
        return sums

    def pack_sums(sums):
        count = len(sums)
        sums = [jnp.sum(s, axis=0, keepdims=True) for s in sums]
        sums += [sums[-1]] * (count % 2)
        first = jnp.concatenate(sums[0::2], axis=0)
        second = jnp.concatenate(sums[1::2], axis=0)
        low = low_half(first.shape)
        packed = jnp.where(low, first, second)
        packed = packed + pltpu.roll(jnp.where(low, second, first), COLS, 1)
        return jnp.concatenate([packed, jnp.zeros((8 - packed.shape[0], LANES), f32)], axis=0)

    def sum_start(n, payload):
        sum_send[n] = payload
        sum_group[n, group] = payload
        for target in near_group:
            remote(
                sum_send.at[n], sum_group.at[n, group], g_ssem.at[n], g_rsem.at[n], target
            ).start()

    def sum_middle(n):
        all_but_one(sum_group.at[n], ng, g_rsem.at[n]).wait()
        partial = jnp.sum(sum_group[n], axis=0)
        tot_send[n] = partial
        sum_bulk[n, bulk] = partial
        for target in far_bulk:
            remote(tot_send.at[n], sum_bulk.at[n, bulk], b_ssem.at[n], b_rsem.at[n], target).start()

    def sum_finish(n, count):
        all_but_one(sum_bulk.at[n], nb, b_rsem.at[n]).wait()
        total = jnp.sum(sum_bulk[n], axis=0)
        swapped = pltpu.roll(total, COLS, 1)
        halves = (jnp.where(low8, total, swapped), jnp.where(low8, swapped, total))
        return [
            jnp.broadcast_to(halves[i % 2][i // 2 : i // 2 + 1], (8, LANES)) for i in range(count)
        ]

    def scaled(factor, value):
        return (factor * value.reshape(-1, 8, LANES)).reshape(value.shape)

    coarse_residual(0, k0)
    pl.semaphore_wait(barrier, ng + nb - 2)
    coarse_push(0)
    weight_copies = edge_copies(wtab, wnb_x, wnb_y, ITERS)
    for copy in weight_copies:
        copy.start()

    for copy in prec_loads:
        copy.wait()
    halos0 = local_part(0, k0)

    for copy in inv_loads:
        copy.wait()
    turned = inv_raw[...]
    in_half = (lax.broadcasted_iota(jnp.int32, turned.shape, 1) & (rows - 1)) < rows // 2
    turned = jnp.concatenate(
        [jnp.where(in_half, turned, 0.0), jnp.where(in_half, 0.0, turned)], axis=0
    )
    high, low = split_hi_lo(turned)
    inv_rows[0 : 2 * rows] = high
    inv_rows[2 * rows :] = low

    for copy in diag_loads:
        copy.wait()

    def turn_diag(p, carry):
        both = diag_raw[p].astype(f32)
        diag_t[p, 0:NS] = jnp.transpose(both[:NS]).astype(bf16)
        diag_t[p, NS : 2 * NS] = jnp.transpose(both[NS:]).astype(bf16)
        return carry

    loop(PAIRS, turn_diag)

    small_loads[1].wait()
    small_loads[2].wait()
    face_of = lax.broadcasted_iota(jnp.int32, (CY, 4 * NS), 1) // NS
    cell_y = lax.broadcasted_iota(jnp.int32, (CY, 4 * NS), 0)
    for x in range(CX):
        opened = jnp.transpose(face_ref[x].astype(f32))
        mask = jnp.zeros((CY, 4 * NS), f32)
        for f in range(4):
            mask = jnp.where(face_of == f, opened[:, f : f + 1], mask)
        if x == 0:
            mask = jnp.where((face_of == 0) & (bulk == 0), 0.0, mask)
        if x == CX - 1:
            mask = jnp.where((face_of == 1) & (bulk == nb - 1), 0.0, mask)
        mask = jnp.where((face_of == 2) & (cell_y == 0) & (group == 0), 0.0, mask)
        mask = jnp.where((face_of == 3) & (cell_y == CY - 1) & (group == ng - 1), 0.0, mask)
        value = coup_ref[x] * mask
        first = value.astype(bf16).astype(f32)
        second = (value - first).astype(bf16).astype(f32)
        third = value - first - second
        spread_rows = jnp.transpose(jnp.concatenate([first, second, third], axis=0)).astype(bf16)

        def expand(yy, carry):
            row = lax.broadcasted_iota(jnp.int32, (3 * CY, LANES), 0) & (CY - 1)
            lane = lax.broadcasted_iota(jnp.int32, (3 * CY, LANES), 1)
            pick = jnp.where(row == yy + jnp.where(lane < COLS, 0, HALF), 1.0, 0.0).astype(bf16)
            wide = mm(spread_rows, pick)
            for f in range(4):
                coef[x * HALF + yy, f] = wide[f * NS : (f + 1) * NS]
            return carry

        loop(HALF, expand)

    cors0 = coarse_solve(0)
    own_z(0)
    own_image(0)
    for copy in weight_copies:
        copy.wait_recv()
    wait_edges(0, halos0, cors0)

    def tail0(p, part, value):
        w0[p, part] = value
        start = k0[p, part]
        return ((start, start), (start, value), (value, value))

    sums = sweep(0, tail0, 3, next_step=1)

    coarse_push(1)
    payload = pack_sums(sums)
    halos1 = local_part(1, w0)
    sum_start(0, payload)
    cors1 = coarse_solve(1)
    own_z(1)
    own_image(1)
    sum_middle(0)
    wait_edges(1, halos1, cors1)

    def tail1(p, part, value):
        w1[p, part] = value
        return ()

    sweep(1, tail1, 0, next_step=2)

    coarse_push(2)
    halos2 = local_part(2, w1)
    cors2 = coarse_solve(2)
    own_z(2)
    own_image(2)
    sum_kk, sum_kw, sum_ww = sum_finish(0, 3)
    beta = jnp.sqrt(sum_kk + tiny_eps)
    s0 = 1.0 / beta
    h00 = sum_kw * s0 * s0
    g00 = sum_kk * s0 * s0
    ww0 = sum_ww * s0 * s0
    h10u = jnp.sqrt(jnp.maximum(ww0 - h00 * h00 * (2.0 - g00), 0.0) + tiny_eps)
    c1 = s0 / h10u
    c2 = h00 * c1

    early = [jnp.zeros((8, LANES), f32)] * 5
    for p in range(PAIRS):
        start = k0[p]
        raw0 = w0[p]
        raw1 = w1[p]
        vec1 = scaled(c1, raw0) - scaled(c2, start)
        image1 = scaled(c1, raw1) - scaled(c2, raw0)
        acc[p] = scaled(c1, acc[p]) - scaled(c2, raw1)
        w0[p] = vec1
        w1[p] = image1
        early = add_terms(
            early,
            ((start, vec1), (vec1, vec1), (start, image1), (vec1, image1), (image1, image1)),
        )
    wait_edges(2, halos2, cors2)

    def tail2(p, part, image2):
        return (
            (k0[p, part], image2),
            (w0[p, part], image2),
            (w1[p, part], image2),
            (image2, image2),
        )

    late = sweep(2, tail2, 4, c1)
    sum_start(1, pack_sums(early + late))

    for copies in (weight_copies, halos0 + cors0, halos1 + cors1, halos2 + cors2):
        for copy in copies:
            copy.wait_send()
    for step in range(ITERS):
        all_but_one(res_buf.at[step], ng, res_ssem.at[step]).wait()
    all_but_one(sum_group.at[0], ng, g_ssem.at[0]).wait()
    all_but_one(sum_bulk.at[0], nb, b_ssem.at[0]).wait()

    sum_middle(1)
    all_but_one(sum_group.at[1], ng, g_ssem.at[1]).wait()
    d_01, d_11, d_0w, d_1w, d_ww, d_0v, d_1v, d_wv, d_vv = sum_finish(1, 9)

    h10_sq = h10u * h10u * d_11 + tiny_eps
    i10 = lax.rsqrt(h10_sq)
    h10 = h10_sq * i10
    t1 = h10u * i10
    t1s = t1 * t1
    g01 = d_01 * s0 * t1
    g11 = d_11 * t1s
    h01 = d_0w * s0 * t1
    h11 = d_1w * t1s
    ww1 = d_ww * t1s
    n1 = ww1 - h01 * h01 * (2.0 - g00) - h11 * h11 * (2.0 - g11) + 2.0 * h01 * h11 * g01
    n1 = jnp.maximum(n1, 0.0)
    i21 = lax.rsqrt(n1 + tiny_eps)
    h21 = (n1 + tiny_eps) * i21
    v0 = d_0v * s0 * t1
    v1 = d_1v * t1s
    vw = d_wv * t1s
    vv = d_vv * t1s
    k1w0 = h00 * g01 + h10 * g11
    w1w0 = h00 * h01 + h10 * h11
    vw0 = h00 * v0 + h10 * v1
    h02 = (v0 - h01 * h00 - h11 * h01) * i21
    h12 = (v1 - h01 * k1w0 - h11 * h11) * i21
    w1w2 = (vw - h01 * w1w0 - h11 * ww1) * i21
    h22 = (w1w2 - h01 * h02 - h11 * h12) * i21
    ww2 = vv + h01 * h01 * ww0 + h11 * h11 * ww1
    ww2 = (ww2 - 2.0 * (h01 * vw0 + h11 * vw - h01 * h11 * w1w0)) * i21 * i21
    g02 = (h01 - h01 * g00 - h11 * g01) * i21
    g12 = (h11 - h01 * g01 - h11 * g11) * i21
    g22 = n1 * i21 * i21
    n2 = ww2 - h02 * h02 * (2.0 - g00) - h12 * h12 * (2.0 - g11) - h22 * h22 * (2.0 - g22)
    n2 = n2 + 2.0 * (h02 * h12 * g01 + h02 * h22 * g02 + h12 * h22 * g12)
    h32 = jnp.sqrt(jnp.maximum(n2, 0.0) + tiny_eps)
    y0, y1, y2 = givens_solve([[h00, h10], [h01, h11, h21], [h02, h12, h22, h32]], beta)

    over = y2 * i21
    on1 = y1 - over * h11
    a2 = over * t1 * c1
    a1 = on1 * t1 * c1 - over * t1 * c2
    a0 = y0 * s0 - over * h01 * s0 - on1 * t1 * c2

    def finish(p, carry):
        x = p // HALF
        yy = p % HALF
        total = (
            scaled(a0, zs[0, p].astype(f32))
            + scaled(a1, zs[1, p].astype(f32))
            + scaled(a2, zs[2, p].astype(f32))
        )
        out_ref[x, yy] = total[:, :COLS].astype(bf16)
        out_ref[x, yy + HALF] = pltpu.roll(total, COLS, 1)[:, :COLS].astype(bf16)
        return carry

    loop(PAIRS, finish)

    all_but_one(sum_bulk.at[1], nb, b_ssem.at[1]).wait()


def body(nb, ng, rhs, diag_blocks, precond_blocks, coupling, face_open, agg_id, coarse_basis, coarse_inv):
    rows = AGGS * COMPS
    inverse = jnp.swapaxes(coarse_inv[0], 0, 1)
    hbm_spec = pl.BlockSpec(memory_space=pltpu.HBM)
    vmem_spec = pl.BlockSpec(memory_space=pltpu.VMEM)
    field = pltpu.VMEM((PAIRS, NS, LANES), f32)
    dma = pltpu.SemaphoreType.DMA
    call = pl.pallas_call(
        functools.partial(kernel, nb, ng),
        out_shape=jax.ShapeDtypeStruct(rhs.shape, bf16),
        in_specs=[hbm_spec] * 8,
        out_specs=vmem_spec,
        scratch_shapes=[
            pltpu.VMEM((CX, CY, 4 * NS), f32),
            pltpu.VMEM((CX, 4, CY), jnp.int32),
            pltpu.SMEM((CX, CY), jnp.int32),
            pltpu.VMEM((COMPS, NS), f32),
            pltpu.VMEM((CX, CY, NS, COLS), bf16),
            pltpu.VMEM((PAIRS, 2 * NS, NS), bf16),
            pltpu.VMEM((PAIRS, 2 * NS, NS), bf16),
            pltpu.VMEM((PAIRS, 2 * NS, NS), bf16),
            pltpu.VMEM((rows, ng * rows), f32),
            pltpu.VMEM((4 * rows, ng * rows), bf16),
            pltpu.VMEM((PAIRS, 4, NS, LANES), f32),
            pltpu.VMEM((PAIRS, 8, LANES), f32),
            pltpu.VMEM((2 * COMPS, 3 * NS), bf16),
            pltpu.VMEM((NS, 3 * COMPS), bf16),
            field,
            field,
            field,
            field,
            pltpu.VMEM((ITERS, PAIRS, NS, LANES), bf16),
            pltpu.VMEM((ITERS, PAIRS, NS, LANES), bf16),
            pltpu.VMEM((5, AGGS, NS, LANES), f32),
            pltpu.VMEM((ITERS, rows // 2, LANES), bf16),
            pltpu.VMEM((ITERS, ng, rows // 2, LANES), bf16),
            pltpu.VMEM((ITERS, rows // 2, LANES), f32),
            pltpu.VMEM((ITERS, 4, rows // 2, LANES), f32),
            pltpu.VMEM((ITERS, CX, HALF, NS, LANES), bf16),
            pltpu.VMEM((ITERS, CX, 2, NS, LANES), bf16),
            pltpu.VMEM((CX, HALF, 8, LANES), f32),
            pltpu.VMEM((CX, 2, 8, LANES), f32),
            pltpu.VMEM((2, 8, LANES), f32),
            pltpu.VMEM((2, ng, 8, LANES), f32),
            pltpu.VMEM((2, 8, LANES), f32),
            pltpu.VMEM((2, nb, 8, LANES), f32),
            dma((14,)),
            dma((ITERS,)),
            dma((ITERS,)),
            dma((ITERS, 4)),
            dma((ITERS, 4)),
            dma((ITERS + 1, CX)),
            dma((ITERS + 1, CX)),
            dma((ITERS + 1, CX, 2)),
            dma((ITERS + 1, CX, 2)),
            dma((2,)),
            dma((2,)),
            dma((2,)),
            dma((2,)),
        ],
        compiler_params=pltpu.CompilerParams(
            collective_id=0, has_side_effects=True, vmem_limit_bytes=32 * 1024 * 1024
        ),
        cost_estimate=pl.CostEstimate(flops=200_000_000, bytes_accessed=3_000_000, transcendentals=0),
    )
    operands = (
        rhs,
        diag_blocks,
        precond_blocks,
        coupling,
        jnp.swapaxes(face_open, 1, 2),
        agg_id,
        jnp.swapaxes(coarse_basis, 0, 1),
        inverse,
    )
    return call(*[pltpu.with_memory_space_constraint(x, pltpu.HBM) for x in operands])


def solution(mesh):
    in_specs = (
        P("bulk", "group", None, None),
        P("bulk", "group", None, None),
        P("bulk", "group", None, None),
        P("bulk", "group", None),
        P("bulk", "group", None),
        P("bulk", "group"),
        P(),
        P("bulk", None, "group"),
    )
    out_specs = P("bulk", "group", None, None)
    return jax.shard_map(
        functools.partial(body, mesh.shape["bulk"], mesh.shape["group"]),
        mesh=mesh,
        in_specs=in_specs,
        out_specs=out_specs,
        check_vma=False,
    )
```

```python
import functools

import jax
import jax.numpy as jnp
from jax import lax
from jax.experimental import pallas as pl
from jax.experimental.pallas import tpu as pltpu
from jax.sharding import PartitionSpec as P

NS = 64
COLS = 64
CX = 2
CY = 16
AGGS = 4
COMPS = 8
ITERS = 3
HALF = CY // 2
PAIRS = CX * HALF
LANES = 2 * COLS
UNROLL = 16

tiny_eps = 1e-06
f32 = jnp.float32
bf16 = jnp.bfloat16


def split_hi_lo(value):
    high = value.astype(bf16)
    low = (value - high.astype(f32)).astype(bf16)
    return high, low


def mm(left, right):
    return jnp.dot(left, right, preferred_element_type=f32)


def loop(count, step, carry=0, unroll=UNROLL):
    unroll = min(unroll, count)

    def several(start, carry):
        for i in range(unroll):
            carry = step(start * unroll + i, carry)
        return carry

    if unroll == count:
        return several(0, carry)
    return lax.fori_loop(0, count // unroll, several, carry)


def far_first(count):
    return sorted(range(1, count), key=lambda d: -min(d, count - d))


def far_targets(nb, bulk):
    along = 8 if nb % 8 == 0 else nb
    across = nb // along

    def hops(d):
        high, low = d // along, d % along
        return min(high, across - high) + min(low, along - low)

    base = (bulk // along) * along
    return [
        {"bulk": lax.rem(base + (d // along) * along, nb) + lax.rem(bulk + d % along, along)}
        for d in sorted(range(1, nb), key=lambda d: -hops(d))
    ]


def low_half(shape):
    return lax.broadcasted_iota(jnp.int32, shape, 1) < COLS


def givens_solve(hessen_cols, beta_norm):
    rotations = []
    target = [beta_norm] + [jnp.zeros_like(beta_norm) for _ in range(ITERS)]
    triangle = []
    for section in range(ITERS):
        column = list(hessen_cols[section])
        for earlier, (cosine, sine, _) in enumerate(rotations):
            upper = column[earlier]
            lower = column[earlier + 1]
            column[earlier] = cosine * upper + sine * lower
            column[earlier + 1] = cosine * lower - sine * upper
        upper = column[section]
        lower = column[section + 1]
        inverse = lax.rsqrt(upper * upper + lower * lower)
        rotations.append((upper * inverse, lower * inverse, inverse))
        carried = target[section]
        target[section] = rotations[-1][0] * carried
        target[section + 1] = -rotations[-1][1] * carried
        triangle.append(column[:section])
    result = [None] * ITERS
    for section in reversed(range(ITERS)):
        accumulated = target[section]
        for later in range(section + 1, ITERS):
            accumulated = accumulated - triangle[later][section] * result[later]
        result[section] = accumulated * rotations[section][2]
    return result


def kernel(
    nb,
    ng,
    rhs_hbm,
    diag_hbm,
    prec_hbm,
    coup_hbm,
    face_hbm,
    agg_hbm,
    basis_hbm,
    inv_hbm,
    out_ref,
    coup_ref,
    face_ref,
    agg_ref,
    basis_ref,
    rhs_raw,
    prec,
    diag_raw,
    diag_t,
    inv_raw,
    inv_rows,
    coef,
    wtab,
    bas_t,
    bas_w,
    k0,
    w0,
    w1,
    acc,
    yb,
    zs,
    spread,
    answers,
    res_send,
    res_buf,
    cor_send,
    cor_buf,
    halo_x,
    halo_y,
    wnb_x,
    wnb_y,
    sum_send,
    sum_group,
    tot_send,
    sum_bulk,
    load_sem,
    res_ssem,
    res_rsem,
    cor_ssem,
    cor_rsem,
    hx_ssem,
    hx_rsem,
    hy_ssem,
    hy_rsem,
    g_ssem,
    g_rsem,
    b_ssem,
    b_rsem,
):
    bulk = lax.axis_index("bulk")
    group = lax.axis_index("group")

    loads = [pltpu.make_async_copy(rhs_hbm, rhs_raw, load_sem.at[0])]
    prec_loads = []
    diag_loads = []
    for x in range(CX):
        for yh in range(2):
            n = x * 2 + yh
            src = (x, pl.ds(yh * HALF, HALF))
            dst = (pl.ds(x * HALF, HALF), pl.ds(yh * NS, NS))
            prec_loads.append(
                pltpu.make_async_copy(prec_hbm.at[src], prec.at[dst], load_sem.at[1 + n])
            )
            diag_loads.append(
                pltpu.make_async_copy(diag_hbm.at[src], diag_raw.at[dst], load_sem.at[5 + n])
            )
    inv_loads = [pltpu.make_async_copy(inv_hbm, inv_raw, load_sem.at[9])]
    small_loads = [
        pltpu.make_async_copy(basis_hbm, basis_ref, load_sem.at[10]),
        pltpu.make_async_copy(face_hbm, face_ref, load_sem.at[11]),
        pltpu.make_async_copy(coup_hbm, coup_ref, load_sem.at[12]),
        pltpu.make_async_copy(agg_hbm, agg_ref, load_sem.at[13]),
    ]
    loads[0].start()

    barrier = pltpu.get_barrier_semaphore()

    near_group = [{"group": lax.rem(group + d, ng)} for d in far_first(ng)]
    far_bulk = far_targets(nb, bulk)
    for target in near_group + far_bulk:
        pl.semaphore_signal(barrier, inc=1, device_id=target, device_id_type=pl.DeviceIdType.MESH)
    for copy in small_loads + prec_loads + inv_loads + diag_loads:
        copy.start()

    rows = AGGS * COMPS
    low8 = low_half((8, LANES))
    low16 = low_half((rows // 2, LANES))
    low32 = low_half((rows, LANES))
    low64 = low_half((NS, LANES))
    row8 = lax.broadcasted_iota(jnp.int32, (8, LANES), 0)

    def make_weights(p, carry):
        x = p // HALF
        yy = p % HALF
        cell = jnp.where(low8, agg_ref[x, yy], agg_ref[x, yy + HALF])
        wtab[p] = jnp.where(cell == row8, 1.0, 0.0).astype(f32)
        return carry

    small_loads[3].wait()
    loop(PAIRS, make_weights)

    weight_scale = (AGGS / (CX * CY)) ** 0.5
    small_loads[0].wait()
    turned = basis_ref[...]
    high, low = split_hi_lo(turned)
    stacked = jnp.concatenate([high.astype(f32), high.astype(f32), low.astype(f32)], axis=0)
    bas_w[...] = jnp.transpose(stacked).astype(bf16)
    high, low = split_hi_lo(turned * weight_scale)
    stacked = jnp.concatenate([high.astype(f32), high.astype(f32), low.astype(f32)], axis=1)
    bas_t[...] = jnp.concatenate([stacked, stacked], axis=0).astype(bf16)

    loads[0].wait()

    def make_start(p, carry):
        x = p // HALF
        yy = p % HALF
        first = rhs_raw[x, yy].astype(f32)
        second = rhs_raw[x, yy + HALF].astype(f32)
        k0[p] = jnp.concatenate([first, second], axis=1)
        return carry

    loop(PAIRS, make_start)

    def remote(src, dst, ssem, rsem, target):
        return pltpu.make_async_remote_copy(
            src_ref=src,
            dst_ref=dst,
            send_sem=ssem,
            recv_sem=rsem,
            device_id=target,
            device_id_type=pl.DeviceIdType.MESH,
        )

    def all_but_one(buf, count, sem):
        return pltpu.make_async_copy(buf.at[pl.ds(0, count - 1)], buf.at[pl.ds(0, count - 1)], sem)

    def coarse_residual(step, field):
        def add(p, sums):
            value = field[p].reshape(8, 8, LANES)
            return tuple(sums[k] + wtab[p, k : k + 1] * value for k in range(AGGS))

        zero = jnp.zeros((8, 8, LANES), f32)
        sums = loop(PAIRS, add, (zero,) * AGGS)
        keep_residual(step, project([s.reshape(NS, LANES) for s in sums]))

    def keep_residual(step, res):
        res = res.astype(bf16)
        res_send[step] = res
        res_buf[step, group] = res

    def project(sums):
        totals = []
        for kl in range(2):
            keep = jnp.where(low64, sums[kl], sums[kl + 2])
            move = jnp.where(low64, sums[kl + 2], sums[kl])
            totals.append(keep + pltpu.roll(move, COLS, 1))
        high, low = split_hi_lo(jnp.concatenate(totals, axis=1))
        part = mm(bas_t[...], jnp.concatenate([high, low, high], axis=0))[:COMPS]
        return jnp.concatenate([part[:, :LANES], part[:, LANES:]], axis=0)

    def coarse_push(step):
        for target in near_group:
            remote(
                res_send.at[step], res_buf.at[step, group], res_ssem.at[step], res_rsem.at[step], target
            ).start()

    def pair_product(mats, p, value):
        both = mm(mats[p], value)
        return jnp.where(low64, both[:NS], both[NS:])

    left = {"bulk": lax.rem(bulk + nb - 1, nb)}
    right = {"bulk": lax.rem(bulk + 1, nb)}
    before = {"group": lax.rem(group + ng - 1, ng)}
    after = {"group": lax.rem(group + 1, ng)}

    def edge_copies(src, dst_x, dst_y, n):
        copies = []
        for x, side in ((0, left), (1, right)):
            copies.append(
                remote(
                    src.at[pl.ds(x * HALF, HALF)],
                    dst_x.at[1 - x],
                    hx_ssem.at[n, x],
                    hx_rsem.at[n, 1 - x],
                    side,
                )
            )
        for x in range(CX):
            for end, row, side in ((0, HALF - 1, after), (1, 0, before)):
                copies.append(
                    remote(
                        src.at[x * HALF + row],
                        dst_y.at[x, end],
                        hy_ssem.at[n, x, end],
                        hy_rsem.at[n, x, end],
                        side,
                    )
                )
        return copies

    def local_part(step, field):
        copies = edge_copies(yb.at[step], halo_x.at[step], halo_y.at[step], step)

        def one(x, yy, carry):
            p = x * HALF + yy
            yb[step, p] = pair_product(prec, p, field[p].astype(bf16)).astype(bf16)
            return carry

        for x in range(CX):
            loop(HALF, functools.partial(one, x))
            copies[x].start()
            copies[2 + 2 * x].start()
            copies[3 + 2 * x].start()
        return copies

    def make_spread(n, cor):
        wide = jnp.concatenate([cor[k * COMPS : (k + 1) * COMPS] for k in range(AGGS)], axis=1)
        high, low = split_hi_lo(wide)
        wide = jnp.concatenate([high.astype(f32), low.astype(f32), high.astype(f32)], axis=0)
        wide = mm(bas_w[...], wide.astype(bf16))
        for k in range(AGGS):
            spread[n, k] = wide[:, k * LANES : (k + 1) * LANES]

    def cor_copies(step):
        return [
            remote(
                cor_send.at[step],
                cor_buf.at[step, slot],
                cor_ssem.at[step, slot],
                cor_rsem.at[step, slot],
                side,
            )
            for slot, side in ((0, right), (1, left), (2, after), (3, before))
        ]

    def coarse_solve(step):
        all_but_one(res_buf.at[step], ng, res_rsem.at[step]).wait()
        gathered = res_buf[step]
        gathered = jnp.concatenate([gathered, gathered], axis=1).reshape(ng * rows, LANES)
        both = mm(inv_rows[...], gathered)
        both = both[: 2 * rows] + both[2 * rows :]
        mixed = jnp.where(low32, both[:rows], both[rows:])
        cor = mixed + pltpu.roll(mixed, COLS, 1)
        cor_send[step] = jnp.where(low16, cor[: rows // 2], cor[rows // 2 :])
        copies = cor_copies(step)
        for copy in copies:
            copy.start()
        make_spread(4, cor)
        return copies

    def joined(n, weights, local):
        total = local.astype(f32).reshape(8, 8, LANES)
        for k in range(AGGS):
            total = total + weights[k : k + 1] * spread[n, k].reshape(8, 8, LANES)
        return total.reshape(NS, LANES).astype(bf16)

    def own_z(step):
        def one(p, carry):
            zs[step, p] = joined(4, wtab[p], yb[step, p])
            return carry

        loop(PAIRS, one)

    def own_image(step):
        def one(p, carry):
            x = p // HALF
            yy = p % HALF
            value = pair_product(diag_t, p, zs[step, p])
            value = value - coef[p, 1 - x] * zs[step, (1 - x) * HALF + yy].astype(f32)
            if yy > 0:
                value = value - coef[p, 2] * zs[step, p - 1].astype(f32)
            if yy < HALF - 1:
                value = value - coef[p, 3] * zs[step, p + 1].astype(f32)
            acc[p] = value
            return carry

        loop(PAIRS, one)

    def neighbour_cor(step, n):
        got = cor_buf[step, n]
        swapped = pltpu.roll(got, COLS, 1)
        return jnp.concatenate(
            [jnp.where(low16, got, swapped), jnp.where(low16, swapped, got)], axis=0
        )

    def masked_sums(pairs, value_of):
        chunk = 16
        chunks = []
        for start in range(0, NS, chunk):
            part = pl.ds(start, chunk)
            cells = [jnp.zeros((chunk, LANES), f32)] * AGGS
            for p in pairs:
                value = value_of(p, part)
                cells = [cells[k] + wtab[p, k : k + 1] * value for k in range(AGGS)]
            chunks.append(cells)
        return [jnp.concatenate([c[k] for c in chunks], axis=0) for k in range(AGGS)]

    low_chunk = low_half((16, LANES))
    ends = [p for p in range(PAIRS) if p % HALF in (0, HALF - 1)]

    def answer_tables():
        row = lax.broadcasted_iota(jnp.int32, (rows, LANES), 0)
        lane = lax.broadcasted_iota(jnp.int32, (rows, LANES), 1) & (COLS - 1)
        for n in range(4):
            make_spread(n, jnp.where(lane == row + (n % 2) * rows, 1.0, 0.0).astype(f32))

        def only(n, weights, part):
            total = weights[0:1] * spread[n, 0, part]
            for k in range(1, AGGS):
                total = total + weights[k : k + 1] * spread[n, k, part]
            return total

        def across(p, part):
            x = p // HALF
            return -coef[p, x, part] * only(x, wnb_x[x, p % HALF], part)

        def along(p, part):
            x = p // HALF
            if p % HALF == 0:
                got = jnp.where(low_chunk, 0.0, only(2, wnb_y[x, 0], part))
                return -coef[p, 2, part] * pltpu.roll(got, COLS, 1)
            got = jnp.where(low_chunk, only(3, wnb_y[x, 1], part), 0.0)
            return -coef[p, 3, part] * pltpu.roll(got, COLS, 1)

        table = jnp.concatenate(
            [project(masked_sums(range(PAIRS), across)), project(masked_sums(ends, along))], axis=1
        )
        high, low = split_hi_lo(table)
        answers[...] = jnp.concatenate([high, low], axis=0)

    def early_residual(step):
        def value_of(p, part):
            x = p // HALF
            yy = p % HALF
            value = acc[p, part] - coef[p, x, part] * halo_x[step, x, yy, part].astype(f32)
            if yy == 0:
                got = halo_y[step, x, 0, part].astype(f32)
                own = zs[step, p + HALF - 1, part].astype(f32)
                moved = pltpu.roll(jnp.where(low_chunk, own, got), COLS, 1)
                value = value - coef[p, 2, part] * moved
            if yy == HALF - 1:
                got = halo_y[step, x, 1, part].astype(f32)
                own = zs[step, p - HALF + 1, part].astype(f32)
                moved = pltpu.roll(jnp.where(low_chunk, got, own), COLS, 1)
                value = value - coef[p, 3, part] * moved
            return value

        return project(masked_sums(range(PAIRS), value_of))

    def answered_residual(step, res):
        blocks = []
        for n in (0, 2):
            both = jnp.concatenate([neighbour_cor(step, n), neighbour_cor(step, n + 1)], axis=0)
            blocks += [jnp.where(low64, both, 0.0), jnp.where(low64, 0.0, both)]
        added = mm(answers[...], jnp.concatenate(blocks, axis=0).astype(bf16))
        keep_residual(step + 1, res + added[: rows // 2] + added[rows // 2 :])

    def wait_halos(halos):
        for copy in halos:
            copy.wait_recv()

    def wait_cors(cors):
        for n in (2, 3, 0, 1):
            cors[n].wait_recv()

    def spread_neighbours(step):
        for n in (2, 3, 0, 1):
            make_spread(n, neighbour_cor(step, n))

    def add_terms(sums, terms):
        return [
            s + jnp.sum((a * b).reshape(-1, 8, LANES), axis=0) for s, (a, b) in zip(sums, terms)
        ]

    def sweep(step, tail, count, weight=None):
        sums = [jnp.zeros((8, LANES), f32)] * count
        chunk = 16
        low = low_half((chunk, LANES))
        for start in range(0, NS, chunk):
            part = pl.ds(start, chunk)
            held = [[spread[n, k, part] for k in range(AGGS)] for n in range(2)]

            def whole(n, weights, local):
                total = local.astype(f32)
                for k in range(AGGS):
                    total = total + weights[k : k + 1] * (held[n][k] if n < 2 else spread[n, k, part])
                return total.astype(bf16).astype(f32)

            for p in range(PAIRS):
                x = p // HALF
                yy = p % HALF
                value = coef[p, x, part] * whole(x, wnb_x[x, yy], halo_x[step, x, yy, part])
                if yy == 0:
                    got = whole(2, wnb_y[x, 0], halo_y[step, x, 0, part])
                    own = zs[step, p + HALF - 1, part].astype(f32)
                    moved = pltpu.roll(jnp.where(low, own, got), COLS, 1)
                    value = value + coef[p, 2, part] * moved
                if yy == HALF - 1:
                    got = whole(3, wnb_y[x, 1], halo_y[step, x, 1, part])
                    own = zs[step, p - HALF + 1, part].astype(f32)
                    moved = pltpu.roll(jnp.where(low, got, own), COLS, 1)
                    value = value + coef[p, 3, part] * moved
                if weight is not None:
                    value = scaled(weight, value)
                value = acc[p, part] - value
                sums = add_terms(sums, tail(p, part, value))
        return sums

    def pack_sums(sums):
        count = len(sums)
        sums = [jnp.sum(s, axis=0, keepdims=True) for s in sums]
        sums += [sums[-1]] * (count % 2)
        first = jnp.concatenate(sums[0::2], axis=0)
        second = jnp.concatenate(sums[1::2], axis=0)
        low = low_half(first.shape)
        packed = jnp.where(low, first, second)
        packed = packed + pltpu.roll(jnp.where(low, second, first), COLS, 1)
        if packed.shape[0] < 4:
            packed = jnp.concatenate(
                [packed, jnp.zeros((4 - packed.shape[0], LANES), f32)], axis=0
            )
        return packed

    def sum_start(n, payload):
        sum_send[n] = payload
        sum_group[n, group] = payload
        for target in near_group:
            remote(
                sum_send.at[n], sum_group.at[n, group], g_ssem.at[n], g_rsem.at[n], target
            ).start()

    def sum_middle(n):
        all_but_one(sum_group.at[n], ng, g_rsem.at[n]).wait()
        partial = jnp.sum(sum_group[n], axis=0)
        tot_send[n] = partial
        sum_bulk[n, bulk] = partial
        for target in far_bulk:
            remote(tot_send.at[n], sum_bulk.at[n, bulk], b_ssem.at[n], b_rsem.at[n], target).start()

    def sum_finish(n, count):
        all_but_one(sum_bulk.at[n], nb, b_rsem.at[n]).wait()
        total = jnp.sum(sum_bulk[n], axis=0)
        swapped = pltpu.roll(total, COLS, 1)
        low = low_half((4, LANES))
        halves = (jnp.where(low, total, swapped), jnp.where(low, swapped, total))
        return [
            jnp.broadcast_to(halves[i % 2][i // 2 : i // 2 + 1], (8, LANES)) for i in range(count)
        ]

    def scaled(factor, value):
        return (factor * value.reshape(-1, 8, LANES)).reshape(value.shape)

    coarse_residual(0, k0)
    pl.semaphore_wait(barrier, ng + nb - 2)
    coarse_push(0)
    weight_copies = edge_copies(wtab, wnb_x, wnb_y, ITERS)
    for copy in weight_copies:
        copy.start()

    for copy in prec_loads:
        copy.wait()
    halos0 = local_part(0, k0)

    for copy in inv_loads:
        copy.wait()
    turned = inv_raw[...]
    in_half = (lax.broadcasted_iota(jnp.int32, turned.shape, 1) & (rows - 1)) < rows // 2
    turned = jnp.concatenate(
        [jnp.where(in_half, turned, 0.0), jnp.where(in_half, 0.0, turned)], axis=0
    )
    high, low = split_hi_lo(turned)
    inv_rows[0 : 2 * rows] = high
    inv_rows[2 * rows :] = low

    for copy in diag_loads:
        copy.wait()

    def turn_diag(p, carry):
        both = diag_raw[p].astype(f32)
        diag_t[p, 0:NS] = jnp.transpose(both[:NS]).astype(bf16)
        diag_t[p, NS : 2 * NS] = jnp.transpose(both[NS:]).astype(bf16)
        return carry

    loop(PAIRS, turn_diag)

    small_loads[1].wait()
    small_loads[2].wait()
    face_of = lax.broadcasted_iota(jnp.int32, (CY, 4 * NS), 1) // NS
    cell_y = lax.broadcasted_iota(jnp.int32, (CY, 4 * NS), 0)
    for x in range(CX):
        opened = jnp.transpose(face_ref[x].astype(f32))
        mask = jnp.zeros((CY, 4 * NS), f32)
        for f in range(4):
            mask = jnp.where(face_of == f, opened[:, f : f + 1], mask)
        if x == 0:
            mask = jnp.where((face_of == 0) & (bulk == 0), 0.0, mask)
        if x == CX - 1:
            mask = jnp.where((face_of == 1) & (bulk == nb - 1), 0.0, mask)
        mask = jnp.where((face_of == 2) & (cell_y == 0) & (group == 0), 0.0, mask)
        mask = jnp.where((face_of == 3) & (cell_y == CY - 1) & (group == ng - 1), 0.0, mask)
        value = coup_ref[x] * mask
        first = value.astype(bf16).astype(f32)
        second = (value - first).astype(bf16).astype(f32)
        third = value - first - second
        spread_rows = jnp.transpose(jnp.concatenate([first, second, third], axis=0)).astype(bf16)

        def expand(yy, carry):
            row = lax.broadcasted_iota(jnp.int32, (3 * CY, LANES), 0) & (CY - 1)
            lane = lax.broadcasted_iota(jnp.int32, (3 * CY, LANES), 1)
            pick = jnp.where(row == yy + jnp.where(lane < COLS, 0, HALF), 1.0, 0.0).astype(bf16)
            wide = mm(spread_rows, pick)
            for f in range(4):
                coef[x * HALF + yy, f] = wide[f * NS : (f + 1) * NS]
            return carry

        loop(HALF, expand)

    cors0 = coarse_solve(0)
    own_z(0)
    own_image(0)
    for copy in weight_copies:
        copy.wait_recv()
    answer_tables()
    wait_halos(halos0)
    res = early_residual(0)
    wait_cors(cors0)
    answered_residual(0, res)
    coarse_push(1)
    spread_neighbours(0)

    def tail0(p, part, value):
        w0[p, part] = value
        start = k0[p, part]
        return ((start, start), (start, value), (value, value))

    payload = pack_sums(sweep(0, tail0, 3))

    halos1 = local_part(1, w0)
    sum_start(0, payload)
    cors1 = coarse_solve(1)
    own_z(1)
    own_image(1)
    sum_middle(0)
    wait_halos(halos1)
    res = early_residual(1)
    wait_cors(cors1)
    answered_residual(1, res)
    coarse_push(2)
    spread_neighbours(1)

    def tail1(p, part, value):
        w1[p, part] = value
        return ()

    sweep(1, tail1, 0)

    halos2 = local_part(2, w1)
    cors2 = coarse_solve(2)
    own_z(2)
    own_image(2)
    sum_kk, sum_kw, sum_ww = sum_finish(0, 3)
    beta = jnp.sqrt(sum_kk + tiny_eps)
    s0 = 1.0 / beta
    h00 = sum_kw * s0 * s0
    g00 = sum_kk * s0 * s0
    ww0 = sum_ww * s0 * s0
    h10u = jnp.sqrt(jnp.maximum(ww0 - h00 * h00 * (2.0 - g00), 0.0) + tiny_eps)
    c1 = s0 / h10u
    c2 = h00 * c1

    early = [jnp.zeros((8, LANES), f32)] * 4
    for p in range(PAIRS):
        start = k0[p]
        raw0 = w0[p]
        raw1 = w1[p]
        vec1 = scaled(c1, raw0) - scaled(c2, start)
        image1 = scaled(c1, raw1) - scaled(c2, raw0)
        acc[p] = scaled(c1, acc[p]) - scaled(c2, raw1)
        w0[p] = vec1
        w1[p] = image1
        early = add_terms(
            early,
            ((vec1, vec1), (start, image1), (vec1, image1), (image1, image1)),
        )
    wait_halos(halos2)
    wait_cors(cors2)
    spread_neighbours(2)

    def tail2(p, part, image2):
        return (
            (k0[p, part], image2),
            (w0[p, part], image2),
            (w1[p, part], image2),
            (image2, image2),
        )

    late = sweep(2, tail2, 4, c1)
    sum_start(1, pack_sums(early + late))

    for copies in (weight_copies, halos0 + cors0, halos1 + cors1, halos2 + cors2):
        for copy in copies:
            copy.wait_send()
    for step in range(ITERS):
        all_but_one(res_buf.at[step], ng, res_ssem.at[step]).wait()
    all_but_one(sum_group.at[0], ng, g_ssem.at[0]).wait()
    all_but_one(sum_bulk.at[0], nb, b_ssem.at[0]).wait()

    sum_middle(1)
    all_but_one(sum_group.at[1], ng, g_ssem.at[1]).wait()
    d_11, d_0w, d_1w, d_ww, d_0v, d_1v, d_wv, d_vv = sum_finish(1, 8)
    d_01 = c1 * sum_kw * (tiny_eps * s0 * s0)

    h10_sq = h10u * h10u * d_11 + tiny_eps
    i10 = lax.rsqrt(h10_sq)
    h10 = h10_sq * i10
    t1 = h10u * i10
    t1s = t1 * t1
    g01 = d_01 * s0 * t1
    g11 = d_11 * t1s
    h01 = d_0w * s0 * t1
    h11 = d_1w * t1s
    ww1 = d_ww * t1s
    n1 = ww1 - h01 * h01 * (2.0 - g00) - h11 * h11 * (2.0 - g11) + 2.0 * h01 * h11 * g01
    n1 = jnp.maximum(n1, 0.0)
    i21 = lax.rsqrt(n1 + tiny_eps)
    h21 = (n1 + tiny_eps) * i21
    v0 = d_0v * s0 * t1
    v1 = d_1v * t1s
    vw = d_wv * t1s
    vv = d_vv * t1s
    k1w0 = h00 * g01 + h10 * g11
    w1w0 = h00 * h01 + h10 * h11
    vw0 = h00 * v0 + h10 * v1
    h02 = (v0 - h01 * h00 - h11 * h01) * i21
    h12 = (v1 - h01 * k1w0 - h11 * h11) * i21
    w1w2 = (vw - h01 * w1w0 - h11 * ww1) * i21
    h22 = (w1w2 - h01 * h02 - h11 * h12) * i21
    ww2 = vv + h01 * h01 * ww0 + h11 * h11 * ww1
    ww2 = (ww2 - 2.0 * (h01 * vw0 + h11 * vw - h01 * h11 * w1w0)) * i21 * i21
    g02 = (h01 - h01 * g00 - h11 * g01) * i21
    g12 = (h11 - h01 * g01 - h11 * g11) * i21
    g22 = n1 * i21 * i21
    n2 = ww2 - h02 * h02 * (2.0 - g00) - h12 * h12 * (2.0 - g11) - h22 * h22 * (2.0 - g22)
    n2 = n2 + 2.0 * (h02 * h12 * g01 + h02 * h22 * g02 + h12 * h22 * g12)
    h32 = jnp.sqrt(jnp.maximum(n2, 0.0) + tiny_eps)
    y0, y1, y2 = givens_solve([[h00, h10], [h01, h11, h21], [h02, h12, h22, h32]], beta)

    over = y2 * i21
    on1 = y1 - over * h11
    a2 = over * t1 * c1
    a1 = on1 * t1 * c1 - over * t1 * c2
    a0 = y0 * s0 - over * h01 * s0 - on1 * t1 * c2

    def finish(p, carry):
        x = p // HALF
        yy = p % HALF
        total = (
            scaled(a0, zs[0, p].astype(f32))
            + scaled(a1, zs[1, p].astype(f32))
            + scaled(a2, zs[2, p].astype(f32))
        )
        out_ref[x, yy] = total[:, :COLS].astype(bf16)
        out_ref[x, yy + HALF] = pltpu.roll(total, COLS, 1)[:, :COLS].astype(bf16)
        return carry

    loop(PAIRS, finish)

    all_but_one(sum_bulk.at[1], nb, b_ssem.at[1]).wait()


def body(nb, ng, rhs, diag_blocks, precond_blocks, coupling, face_open, agg_id, coarse_basis, coarse_inv):
    rows = AGGS * COMPS
    inverse = jnp.swapaxes(coarse_inv[0], 0, 1)
    hbm_spec = pl.BlockSpec(memory_space=pltpu.HBM)
    vmem_spec = pl.BlockSpec(memory_space=pltpu.VMEM)
    field = pltpu.VMEM((PAIRS, NS, LANES), f32)
    dma = pltpu.SemaphoreType.DMA
    call = pl.pallas_call(
        functools.partial(kernel, nb, ng),
        out_shape=jax.ShapeDtypeStruct(rhs.shape, bf16),
        in_specs=[hbm_spec] * 8,
        out_specs=vmem_spec,
        scratch_shapes=[
            pltpu.VMEM((CX, CY, 4 * NS), f32),
            pltpu.VMEM((CX, 4, CY), jnp.int32),
            pltpu.SMEM((CX, CY), jnp.int32),
            pltpu.VMEM((COMPS, NS), f32),
            pltpu.VMEM((CX, CY, NS, COLS), bf16),
            pltpu.VMEM((PAIRS, 2 * NS, NS), bf16),
            pltpu.VMEM((PAIRS, 2 * NS, NS), bf16),
            pltpu.VMEM((PAIRS, 2 * NS, NS), bf16),
            pltpu.VMEM((rows, ng * rows), f32),
            pltpu.VMEM((4 * rows, ng * rows), bf16),
            pltpu.VMEM((PAIRS, 4, NS, LANES), f32),
            pltpu.VMEM((PAIRS, 8, LANES), f32),
            pltpu.VMEM((2 * COMPS, 3 * NS), bf16),
            pltpu.VMEM((NS, 3 * COMPS), bf16),
            field,
            field,
            field,
            field,
            pltpu.VMEM((ITERS, PAIRS, NS, LANES), bf16),
            pltpu.VMEM((ITERS, PAIRS, NS, LANES), bf16),
            pltpu.VMEM((5, AGGS, NS, LANES), f32),
            pltpu.VMEM((rows, 2 * LANES), bf16),
            pltpu.VMEM((ITERS, rows // 2, LANES), bf16),
            pltpu.VMEM((ITERS, ng, rows // 2, LANES), bf16),
            pltpu.VMEM((ITERS, rows // 2, LANES), f32),
            pltpu.VMEM((ITERS, 4, rows // 2, LANES), f32),
            pltpu.VMEM((ITERS, CX, HALF, NS, LANES), bf16),
            pltpu.VMEM((ITERS, CX, 2, NS, LANES), bf16),
            pltpu.VMEM((CX, HALF, 8, LANES), f32),
            pltpu.VMEM((CX, 2, 8, LANES), f32),
            pltpu.VMEM((2, 4, LANES), f32),
            pltpu.VMEM((2, ng, 4, LANES), f32),
            pltpu.VMEM((2, 4, LANES), f32),
            pltpu.VMEM((2, nb, 4, LANES), f32),
            dma((14,)),
            dma((ITERS,)),
            dma((ITERS,)),
            dma((ITERS, 4)),
            dma((ITERS, 4)),
            dma((ITERS + 1, CX)),
            dma((ITERS + 1, CX)),
            dma((ITERS + 1, CX, 2)),
            dma((ITERS + 1, CX, 2)),
            dma((2,)),
            dma((2,)),
            dma((2,)),
            dma((2,)),
        ],
        compiler_params=pltpu.CompilerParams(
            collective_id=0, has_side_effects=True, vmem_limit_bytes=32 * 1024 * 1024
        ),
        cost_estimate=pl.CostEstimate(flops=200_000_000, bytes_accessed=3_000_000, transcendentals=0),
    )
    operands = (
        rhs,
        diag_blocks,
        precond_blocks,
        coupling,
        jnp.swapaxes(face_open, 1, 2),
        agg_id,
        jnp.swapaxes(coarse_basis, 0, 1),
        inverse,
    )
    return call(*[pltpu.with_memory_space_constraint(x, pltpu.HBM) for x in operands])


def solution(mesh):
    in_specs = (
        P("bulk", "group", None, None),
        P("bulk", "group", None, None),
        P("bulk", "group", None, None),
        P("bulk", "group", None),
        P("bulk", "group", None),
        P("bulk", "group"),
        P(),
        P("bulk", None, "group"),
    )
    out_specs = P("bulk", "group", None, None)
    return jax.shard_map(
        functools.partial(body, mesh.shape["bulk"], mesh.shape["group"]),
        mesh=mesh,
        in_specs=in_specs,
        out_specs=out_specs,
        check_vma=False,
    )
```

```python
import functools

import jax
import jax.numpy as jnp
from jax import lax
from jax.experimental import pallas as pl
from jax.experimental.pallas import tpu as pltpu
from jax.sharding import PartitionSpec as P

NS = 64
COLS = 64
CX = 2
CY = 16
AGGS = 4
COMPS = 8
ITERS = 3
HALF = CY // 2
PAIRS = CX * HALF
LANES = 2 * COLS
UNROLL = 16

tiny_eps = 1e-06
f32 = jnp.float32
bf16 = jnp.bfloat16


def split_hi_lo(value):
    high = value.astype(bf16)
    low = (value - high.astype(f32)).astype(bf16)
    return high, low


def mm(left, right):
    return jnp.dot(left, right, preferred_element_type=f32)


def loop(count, step, carry=0, unroll=UNROLL):
    unroll = min(unroll, count)

    def several(start, carry):
        for i in range(unroll):
            carry = step(start * unroll + i, carry)
        return carry

    if unroll == count:
        return several(0, carry)
    return lax.fori_loop(0, count // unroll, several, carry)


def far_first(count):
    return sorted(range(1, count), key=lambda d: -min(d, count - d))


def along_y(nb):
    return 8 if nb % 8 == 0 else nb


def hops(d, count):
    return min(d, count - d)


def plane_targets(nb, bulk, group):
    count = along_y(nb)
    base = (bulk // count) * count
    return [
        {
            "bulk": base + lax.rem(bulk + d % count, count),
            "group": (group // 2) * 2 + lax.rem(group + d // count, 2),
        }
        for d in sorted(range(1, 2 * count), key=lambda d: -hops(d % count, count))
    ]


def cross_targets(nb, ng, bulk, group):
    count = along_y(nb)
    across = nb // count
    deep = ng // 2
    return [
        {
            "bulk": lax.rem(bulk + (d // deep) * count, nb),
            "group": lax.rem(group + 2 * (d % deep), ng),
        }
        for d in sorted(
            range(1, across * deep), key=lambda d: -hops(d // deep, across) - hops(d % deep, deep)
        )
    ]


def low_half(shape):
    return lax.broadcasted_iota(jnp.int32, shape, 1) < COLS


def givens_solve(hessen_cols, beta_norm):
    rotations = []
    target = [beta_norm] + [jnp.zeros_like(beta_norm) for _ in range(ITERS)]
    triangle = []
    for section in range(ITERS):
        column = list(hessen_cols[section])
        for earlier, (cosine, sine, _) in enumerate(rotations):
            upper = column[earlier]
            lower = column[earlier + 1]
            column[earlier] = cosine * upper + sine * lower
            column[earlier + 1] = cosine * lower - sine * upper
        upper = column[section]
        lower = column[section + 1]
        inverse = lax.rsqrt(upper * upper + lower * lower)
        rotations.append((upper * inverse, lower * inverse, inverse))
        carried = target[section]
        target[section] = rotations[-1][0] * carried
        target[section + 1] = -rotations[-1][1] * carried
        triangle.append(column[:section])
    result = [None] * ITERS
    for section in reversed(range(ITERS)):
        accumulated = target[section]
        for later in range(section + 1, ITERS):
            accumulated = accumulated - triangle[later][section] * result[later]
        result[section] = accumulated * rotations[section][2]
    return result


def kernel(
    nb,
    ng,
    rhs_hbm,
    diag_hbm,
    prec_hbm,
    coup_hbm,
    face_hbm,
    agg_hbm,
    basis_hbm,
    inv_hbm,
    out_ref,
    coup_ref,
    face_ref,
    agg_ref,
    basis_ref,
    rhs_raw,
    prec,
    diag_raw,
    diag_t,
    inv_raw,
    inv_rows,
    coef,
    wtab,
    bas_t,
    bas_w,
    k0,
    w0,
    w1,
    acc,
    yb,
    zs,
    spread,
    answers,
    res_send,
    res_buf,
    cor_send,
    cor_buf,
    halo_x,
    halo_y,
    wnb_x,
    wnb_y,
    sum_send,
    sum_plane,
    tot_send,
    sum_cross,
    load_sem,
    res_ssem,
    res_rsem,
    cor_ssem,
    cor_rsem,
    hx_ssem,
    hx_rsem,
    hy_ssem,
    hy_rsem,
    g_ssem,
    g_rsem,
    b_ssem,
    b_rsem,
):
    bulk = lax.axis_index("bulk")
    group = lax.axis_index("group")

    loads = [pltpu.make_async_copy(rhs_hbm, rhs_raw, load_sem.at[0])]
    prec_loads = []
    diag_loads = []
    for x in range(CX):
        for yh in range(2):
            n = x * 2 + yh
            src = (x, pl.ds(yh * HALF, HALF))
            dst = (pl.ds(x * HALF, HALF), pl.ds(yh * NS, NS))
            prec_loads.append(
                pltpu.make_async_copy(prec_hbm.at[src], prec.at[dst], load_sem.at[1 + n])
            )
            diag_loads.append(
                pltpu.make_async_copy(diag_hbm.at[src], diag_raw.at[dst], load_sem.at[5 + n])
            )
    inv_loads = [pltpu.make_async_copy(inv_hbm, inv_raw, load_sem.at[9])]
    small_loads = [
        pltpu.make_async_copy(basis_hbm, basis_ref, load_sem.at[10]),
        pltpu.make_async_copy(face_hbm, face_ref, load_sem.at[11]),
        pltpu.make_async_copy(coup_hbm, coup_ref, load_sem.at[12]),
        pltpu.make_async_copy(agg_hbm, agg_ref, load_sem.at[13]),
    ]
    loads[0].start()

    barrier = pltpu.get_barrier_semaphore()

    near_group = [{"group": lax.rem(group + d, ng)} for d in far_first(ng)]
    plane = plane_targets(nb, bulk, group)
    cross = cross_targets(nb, ng, bulk, group)
    n_plane = len(plane) + 1
    n_cross = len(cross) + 1
    in_plane = lax.rem(bulk, along_y(nb)) * 2 + lax.rem(group, 2)
    in_cross = (bulk // along_y(nb)) * (ng // 2) + group // 2
    beside = [{"bulk": lax.rem(bulk + d, nb)} for d in (1, nb - 1)]
    greeted = cross + near_group + plane + beside
    for target in greeted:
        pl.semaphore_signal(barrier, inc=1, device_id=target, device_id_type=pl.DeviceIdType.MESH)
    for copy in small_loads + prec_loads + inv_loads + diag_loads:
        copy.start()

    rows = AGGS * COMPS
    low8 = low_half((8, LANES))
    low16 = low_half((rows // 2, LANES))
    low32 = low_half((rows, LANES))
    low64 = low_half((NS, LANES))
    row8 = lax.broadcasted_iota(jnp.int32, (8, LANES), 0)

    def make_weights(p, carry):
        x = p // HALF
        yy = p % HALF
        cell = jnp.where(low8, agg_ref[x, yy], agg_ref[x, yy + HALF])
        wtab[p] = jnp.where(cell == row8, 1.0, 0.0).astype(f32)
        return carry

    small_loads[3].wait()
    loop(PAIRS, make_weights)

    weight_scale = (AGGS / (CX * CY)) ** 0.5
    small_loads[0].wait()
    turned = basis_ref[...]
    high, low = split_hi_lo(turned)
    stacked = jnp.concatenate([high.astype(f32), high.astype(f32), low.astype(f32)], axis=0)
    bas_w[...] = jnp.transpose(stacked).astype(bf16)
    high, low = split_hi_lo(turned * weight_scale)
    stacked = jnp.concatenate([high.astype(f32), high.astype(f32), low.astype(f32)], axis=1)
    bas_t[...] = jnp.concatenate([stacked, stacked], axis=0).astype(bf16)

    loads[0].wait()

    def make_start(p, carry):
        x = p // HALF
        yy = p % HALF
        first = rhs_raw[x, yy].astype(f32)
        second = rhs_raw[x, yy + HALF].astype(f32)
        k0[p] = jnp.concatenate([first, second], axis=1)
        return carry

    loop(PAIRS, make_start)

    def remote(src, dst, ssem, rsem, target):
        return pltpu.make_async_remote_copy(
            src_ref=src,
            dst_ref=dst,
            send_sem=ssem,
            recv_sem=rsem,
            device_id=target,
            device_id_type=pl.DeviceIdType.MESH,
        )

    def all_but_one(buf, count, sem):
        return pltpu.make_async_copy(buf.at[pl.ds(0, count - 1)], buf.at[pl.ds(0, count - 1)], sem)

    def coarse_residual(step, field):
        def add(p, sums):
            value = field[p].reshape(8, 8, LANES)
            return tuple(sums[k] + wtab[p, k : k + 1] * value for k in range(AGGS))

        zero = jnp.zeros((8, 8, LANES), f32)
        sums = loop(PAIRS, add, (zero,) * AGGS)
        keep_residual(step, project([s.reshape(NS, LANES) for s in sums]))

    def keep_residual(step, res):
        res = res.astype(bf16)
        res_send[step] = res
        res_buf[step, group] = res

    def project(sums):
        totals = []
        for kl in range(2):
            keep = jnp.where(low64, sums[kl], sums[kl + 2])
            move = jnp.where(low64, sums[kl + 2], sums[kl])
            totals.append(keep + pltpu.roll(move, COLS, 1))
        high, low = split_hi_lo(jnp.concatenate(totals, axis=1))
        part = mm(bas_t[...], jnp.concatenate([high, low, high], axis=0))[:COMPS]
        return jnp.concatenate([part[:, :LANES], part[:, LANES:]], axis=0)

    def coarse_push(step):
        for target in near_group:
            remote(
                res_send.at[step], res_buf.at[step, group], res_ssem.at[step], res_rsem.at[step], target
            ).start()

    def pair_product(mats, p, value):
        both = mm(mats[p], value)
        return jnp.where(low64, both[:NS], both[NS:])

    left = {"bulk": lax.rem(bulk + nb - 1, nb)}
    right = {"bulk": lax.rem(bulk + 1, nb)}
    before = {"group": lax.rem(group + ng - 1, ng)}
    after = {"group": lax.rem(group + 1, ng)}

    def edge_copies(src, dst_x, dst_y, n):
        copies = []
        for x, side in ((0, left), (1, right)):
            copies.append(
                remote(
                    src.at[pl.ds(x * HALF, HALF)],
                    dst_x.at[1 - x],
                    hx_ssem.at[n, x],
                    hx_rsem.at[n, 1 - x],
                    side,
                )
            )
        for x in range(CX):
            for end, row, side in ((0, HALF - 1, after), (1, 0, before)):
                copies.append(
                    remote(
                        src.at[x * HALF + row],
                        dst_y.at[x, end],
                        hy_ssem.at[n, x, end],
                        hy_rsem.at[n, x, end],
                        side,
                    )
                )
        return copies

    def local_part(step, field):
        copies = edge_copies(yb.at[step], halo_x.at[step], halo_y.at[step], step)

        def one(x, yy, carry):
            p = x * HALF + yy
            yb[step, p] = pair_product(prec, p, field[p].astype(bf16)).astype(bf16)
            return carry

        for x in range(CX):
            loop(HALF, functools.partial(one, x))
            copies[x].start()
            copies[2 + 2 * x].start()
            copies[3 + 2 * x].start()
        return copies

    def make_spread(n, cor):
        wide = jnp.concatenate([cor[k * COMPS : (k + 1) * COMPS] for k in range(AGGS)], axis=1)
        high, low = split_hi_lo(wide)
        wide = jnp.concatenate([high.astype(f32), low.astype(f32), high.astype(f32)], axis=0)
        wide = mm(bas_w[...], wide.astype(bf16))
        for k in range(AGGS):
            spread[n, k] = wide[:, k * LANES : (k + 1) * LANES]

    def cor_copies(step):
        return [
            remote(
                cor_send.at[step],
                cor_buf.at[step, slot],
                cor_ssem.at[step, slot],
                cor_rsem.at[step, slot],
                side,
            )
            for slot, side in ((0, right), (1, left), (2, after), (3, before))
        ]

    def coarse_solve(step):
        all_but_one(res_buf.at[step], ng, res_rsem.at[step]).wait()
        gathered = res_buf[step]
        gathered = jnp.concatenate([gathered, gathered], axis=1).reshape(ng * rows, LANES)
        both = mm(inv_rows[...], gathered)
        both = both[: 2 * rows] + both[2 * rows :]
        mixed = jnp.where(low32, both[:rows], both[rows:])
        cor = mixed + pltpu.roll(mixed, COLS, 1)
        cor_send[step] = jnp.where(low16, cor[: rows // 2], cor[rows // 2 :])
        copies = cor_copies(step)
        for copy in copies:
            copy.start()
        make_spread(4, cor)
        return copies

    def joined(n, weights, local):
        total = local.astype(f32).reshape(8, 8, LANES)
        for k in range(AGGS):
            total = total + weights[k : k + 1] * spread[n, k].reshape(8, 8, LANES)
        return total.reshape(NS, LANES).astype(bf16)

    def own_z(step):
        def one(p, carry):
            zs[step, p] = joined(4, wtab[p], yb[step, p])
            return carry

        loop(PAIRS, one)

    def own_image(step):
        def one(p, carry):
            x = p // HALF
            yy = p % HALF
            value = pair_product(diag_t, p, zs[step, p])
            value = value - coef[p, 1 - x] * zs[step, (1 - x) * HALF + yy].astype(f32)
            if yy > 0:
                value = value - coef[p, 2] * zs[step, p - 1].astype(f32)
            if yy < HALF - 1:
                value = value - coef[p, 3] * zs[step, p + 1].astype(f32)
            acc[p] = value
            return carry

        loop(PAIRS, one)

    def neighbour_cor(step, n):
        got = cor_buf[step, n]
        swapped = pltpu.roll(got, COLS, 1)
        return jnp.concatenate(
            [jnp.where(low16, got, swapped), jnp.where(low16, swapped, got)], axis=0
        )

    def masked_sums(pairs, value_of):
        chunk = 16
        chunks = []
        for start in range(0, NS, chunk):
            part = pl.ds(start, chunk)
            cells = [jnp.zeros((chunk, LANES), f32)] * AGGS
            for p in pairs:
                value = value_of(p, part)
                cells = [cells[k] + wtab[p, k : k + 1] * value for k in range(AGGS)]
            chunks.append(cells)
        return [jnp.concatenate([c[k] for c in chunks], axis=0) for k in range(AGGS)]

    low_chunk = low_half((16, LANES))
    ends = [p for p in range(PAIRS) if p % HALF in (0, HALF - 1)]

    def answer_tables():
        row = lax.broadcasted_iota(jnp.int32, (rows, LANES), 0)
        lane = lax.broadcasted_iota(jnp.int32, (rows, LANES), 1) & (COLS - 1)
        for n in range(4):
            make_spread(n, jnp.where(lane == row + (n % 2) * rows, 1.0, 0.0).astype(f32))

        def only(n, weights, part):
            total = weights[0:1] * spread[n, 0, part]
            for k in range(1, AGGS):
                total = total + weights[k : k + 1] * spread[n, k, part]
            return total

        def across(p, part):
            x = p // HALF
            return -coef[p, x, part] * only(x, wnb_x[x, p % HALF], part)

        def along(p, part):
            x = p // HALF
            if p % HALF == 0:
                got = jnp.where(low_chunk, 0.0, only(2, wnb_y[x, 0], part))
                return -coef[p, 2, part] * pltpu.roll(got, COLS, 1)
            got = jnp.where(low_chunk, only(3, wnb_y[x, 1], part), 0.0)
            return -coef[p, 3, part] * pltpu.roll(got, COLS, 1)

        table = jnp.concatenate(
            [project(masked_sums(range(PAIRS), across)), project(masked_sums(ends, along))], axis=1
        )
        high, low = split_hi_lo(table)
        answers[...] = jnp.concatenate([high, low], axis=0)

    def early_residual(step):
        def value_of(p, part):
            x = p // HALF
            yy = p % HALF
            value = acc[p, part] - coef[p, x, part] * halo_x[step, x, yy, part].astype(f32)
            if yy == 0:
                got = halo_y[step, x, 0, part].astype(f32)
                own = zs[step, p + HALF - 1, part].astype(f32)
                moved = pltpu.roll(jnp.where(low_chunk, own, got), COLS, 1)
                value = value - coef[p, 2, part] * moved
            if yy == HALF - 1:
                got = halo_y[step, x, 1, part].astype(f32)
                own = zs[step, p - HALF + 1, part].astype(f32)
                moved = pltpu.roll(jnp.where(low_chunk, got, own), COLS, 1)
                value = value - coef[p, 3, part] * moved
            return value

        return project(masked_sums(range(PAIRS), value_of))

    def answered_residual(step, res):
        blocks = []
        for n in (0, 2):
            both = jnp.concatenate([neighbour_cor(step, n), neighbour_cor(step, n + 1)], axis=0)
            blocks += [jnp.where(low64, both, 0.0), jnp.where(low64, 0.0, both)]
        added = mm(answers[...], jnp.concatenate(blocks, axis=0).astype(bf16))
        keep_residual(step + 1, res + added[: rows // 2] + added[rows // 2 :])

    def wait_halos(halos):
        for copy in halos:
            copy.wait_recv()

    def wait_cors(cors):
        for n in (2, 3, 0, 1):
            cors[n].wait_recv()

    def spread_neighbours(step):
        for n in (2, 3, 0, 1):
            make_spread(n, neighbour_cor(step, n))

    def add_terms(sums, terms):
        return [
            s + jnp.sum((a * b).reshape(-1, 8, LANES), axis=0) for s, (a, b) in zip(sums, terms)
        ]

    def sweep(step, tail, count, weight=None):
        sums = [jnp.zeros((8, LANES), f32)] * count
        chunk = 16
        low = low_half((chunk, LANES))
        for start in range(0, NS, chunk):
            part = pl.ds(start, chunk)
            held = [[spread[n, k, part] for k in range(AGGS)] for n in range(2)]

            def whole(n, weights, local):
                total = local.astype(f32)
                for k in range(AGGS):
                    total = total + weights[k : k + 1] * (held[n][k] if n < 2 else spread[n, k, part])
                return total.astype(bf16).astype(f32)

            for p in range(PAIRS):
                x = p // HALF
                yy = p % HALF
                value = coef[p, x, part] * whole(x, wnb_x[x, yy], halo_x[step, x, yy, part])
                if yy == 0:
                    got = whole(2, wnb_y[x, 0], halo_y[step, x, 0, part])
                    own = zs[step, p + HALF - 1, part].astype(f32)
                    moved = pltpu.roll(jnp.where(low, own, got), COLS, 1)
                    value = value + coef[p, 2, part] * moved
                if yy == HALF - 1:
                    got = whole(3, wnb_y[x, 1], halo_y[step, x, 1, part])
                    own = zs[step, p - HALF + 1, part].astype(f32)
                    moved = pltpu.roll(jnp.where(low, got, own), COLS, 1)
                    value = value + coef[p, 3, part] * moved
                if weight is not None:
                    value = scaled(weight, value)
                value = acc[p, part] - value
                sums = add_terms(sums, tail(p, part, value))
        return sums

    def pack_sums(sums):
        count = len(sums)
        sums = [jnp.sum(s, axis=0, keepdims=True) for s in sums]
        sums += [sums[-1]] * (count % 2)
        first = jnp.concatenate(sums[0::2], axis=0)
        second = jnp.concatenate(sums[1::2], axis=0)
        low = low_half(first.shape)
        packed = jnp.where(low, first, second)
        packed = packed + pltpu.roll(jnp.where(low, second, first), COLS, 1)
        if packed.shape[0] < 4:
            packed = jnp.concatenate(
                [packed, jnp.zeros((4 - packed.shape[0], LANES), f32)], axis=0
            )
        return packed

    def sum_start(n, payload):
        sum_send[n] = payload
        sum_plane[n, in_plane] = payload
        for target in plane:
            remote(
                sum_send.at[n], sum_plane.at[n, in_plane], g_ssem.at[n], g_rsem.at[n], target
            ).start()

    def sum_middle(n):
        all_but_one(sum_plane.at[n], n_plane, g_rsem.at[n]).wait()
        partial = jnp.sum(sum_plane[n], axis=0)
        tot_send[n] = partial
        sum_cross[n, in_cross] = partial
        for target in cross:
            remote(
                tot_send.at[n], sum_cross.at[n, in_cross], b_ssem.at[n], b_rsem.at[n], target
            ).start()

    def sum_finish(n, count):
        all_but_one(sum_cross.at[n], n_cross, b_rsem.at[n]).wait()
        total = jnp.sum(sum_cross[n], axis=0)
        swapped = pltpu.roll(total, COLS, 1)
        low = low_half((4, LANES))
        halves = (jnp.where(low, total, swapped), jnp.where(low, swapped, total))
        return [
            jnp.broadcast_to(halves[i % 2][i // 2 : i // 2 + 1], (8, LANES)) for i in range(count)
        ]

    def scaled(factor, value):
        return (factor * value.reshape(-1, 8, LANES)).reshape(value.shape)

    coarse_residual(0, k0)
    pl.semaphore_wait(barrier, len(greeted))
    coarse_push(0)
    weight_copies = edge_copies(wtab, wnb_x, wnb_y, ITERS)
    for copy in weight_copies:
        copy.start()

    for copy in prec_loads:
        copy.wait()
    halos0 = local_part(0, k0)

    for copy in inv_loads:
        copy.wait()
    turned = inv_raw[...]
    in_half = (lax.broadcasted_iota(jnp.int32, turned.shape, 1) & (rows - 1)) < rows // 2
    turned = jnp.concatenate(
        [jnp.where(in_half, turned, 0.0), jnp.where(in_half, 0.0, turned)], axis=0
    )
    high, low = split_hi_lo(turned)
    inv_rows[0 : 2 * rows] = high
    inv_rows[2 * rows :] = low

    for copy in diag_loads:
        copy.wait()

    def turn_diag(p, carry):
        both = diag_raw[p].astype(f32)
        diag_t[p, 0:NS] = jnp.transpose(both[:NS]).astype(bf16)
        diag_t[p, NS : 2 * NS] = jnp.transpose(both[NS:]).astype(bf16)
        return carry

    loop(PAIRS, turn_diag)

    small_loads[1].wait()
    small_loads[2].wait()
    face_of = lax.broadcasted_iota(jnp.int32, (CY, 4 * NS), 1) // NS
    cell_y = lax.broadcasted_iota(jnp.int32, (CY, 4 * NS), 0)
    for x in range(CX):
        opened = jnp.transpose(face_ref[x].astype(f32))
        mask = jnp.zeros((CY, 4 * NS), f32)
        for f in range(4):
            mask = jnp.where(face_of == f, opened[:, f : f + 1], mask)
        if x == 0:
            mask = jnp.where((face_of == 0) & (bulk == 0), 0.0, mask)
        if x == CX - 1:
            mask = jnp.where((face_of == 1) & (bulk == nb - 1), 0.0, mask)
        mask = jnp.where((face_of == 2) & (cell_y == 0) & (group == 0), 0.0, mask)
        mask = jnp.where((face_of == 3) & (cell_y == CY - 1) & (group == ng - 1), 0.0, mask)
        value = coup_ref[x] * mask
        first = value.astype(bf16).astype(f32)
        second = (value - first).astype(bf16).astype(f32)
        third = value - first - second
        spread_rows = jnp.transpose(jnp.concatenate([first, second, third], axis=0)).astype(bf16)

        def expand(yy, carry):
            row = lax.broadcasted_iota(jnp.int32, (3 * CY, LANES), 0) & (CY - 1)
            lane = lax.broadcasted_iota(jnp.int32, (3 * CY, LANES), 1)
            pick = jnp.where(row == yy + jnp.where(lane < COLS, 0, HALF), 1.0, 0.0).astype(bf16)
            wide = mm(spread_rows, pick)
            for f in range(4):
                coef[x * HALF + yy, f] = wide[f * NS : (f + 1) * NS]
            return carry

        loop(HALF, expand)

    cors0 = coarse_solve(0)
    own_z(0)
    own_image(0)
    for copy in weight_copies:
        copy.wait_recv()
    answer_tables()
    wait_halos(halos0)
    res = early_residual(0)
    wait_cors(cors0)
    answered_residual(0, res)
    coarse_push(1)
    spread_neighbours(0)

    def tail0(p, part, value):
        w0[p, part] = value
        start = k0[p, part]
        return ((start, start), (start, value), (value, value))

    payload = pack_sums(sweep(0, tail0, 3))

    halos1 = local_part(1, w0)
    sum_start(0, payload)
    cors1 = coarse_solve(1)
    own_z(1)
    own_image(1)
    sum_middle(0)
    wait_halos(halos1)
    res = early_residual(1)
    wait_cors(cors1)
    answered_residual(1, res)
    coarse_push(2)
    spread_neighbours(1)

    def tail1(p, part, value):
        w1[p, part] = value
        return ()

    sweep(1, tail1, 0)

    halos2 = local_part(2, w1)
    cors2 = coarse_solve(2)
    own_z(2)
    own_image(2)
    sum_kk, sum_kw, sum_ww = sum_finish(0, 3)
    beta = jnp.sqrt(sum_kk + tiny_eps)
    s0 = 1.0 / beta
    h00 = sum_kw * s0 * s0
    g00 = sum_kk * s0 * s0
    ww0 = sum_ww * s0 * s0
    h10u = jnp.sqrt(jnp.maximum(ww0 - h00 * h00 * (2.0 - g00), 0.0) + tiny_eps)
    c1 = s0 / h10u
    c2 = h00 * c1

    early = [jnp.zeros((8, LANES), f32)] * 4
    for p in range(PAIRS):
        start = k0[p]
        raw0 = w0[p]
        raw1 = w1[p]
        vec1 = scaled(c1, raw0) - scaled(c2, start)
        image1 = scaled(c1, raw1) - scaled(c2, raw0)
        acc[p] = scaled(c1, acc[p]) - scaled(c2, raw1)
        w0[p] = vec1
        w1[p] = image1
        early = add_terms(
            early,
            ((vec1, vec1), (start, image1), (vec1, image1), (image1, image1)),
        )
    wait_halos(halos2)
    wait_cors(cors2)
    spread_neighbours(2)

    def tail2(p, part, image2):
        return (
            (k0[p, part], image2),
            (w0[p, part], image2),
            (w1[p, part], image2),
            (image2, image2),
        )

    late = sweep(2, tail2, 4, c1)
    sum_start(1, pack_sums(early + late))

    for copies in (weight_copies, halos0 + cors0, halos1 + cors1, halos2 + cors2):
        for copy in copies:
            copy.wait_send()
    for step in range(ITERS):
        all_but_one(res_buf.at[step], ng, res_ssem.at[step]).wait()
    all_but_one(sum_plane.at[0], n_plane, g_ssem.at[0]).wait()
    all_but_one(sum_cross.at[0], n_cross, b_ssem.at[0]).wait()

    sum_middle(1)
    all_but_one(sum_plane.at[1], n_plane, g_ssem.at[1]).wait()
    d_11, d_0w, d_1w, d_ww, d_0v, d_1v, d_wv, d_vv = sum_finish(1, 8)
    d_01 = c1 * sum_kw * (tiny_eps * s0 * s0)

    h10_sq = h10u * h10u * d_11 + tiny_eps
    i10 = lax.rsqrt(h10_sq)
    h10 = h10_sq * i10
    t1 = h10u * i10
    t1s = t1 * t1
    g01 = d_01 * s0 * t1
    g11 = d_11 * t1s
    h01 = d_0w * s0 * t1
    h11 = d_1w * t1s
    ww1 = d_ww * t1s
    n1 = ww1 - h01 * h01 * (2.0 - g00) - h11 * h11 * (2.0 - g11) + 2.0 * h01 * h11 * g01
    n1 = jnp.maximum(n1, 0.0)
    i21 = lax.rsqrt(n1 + tiny_eps)
    h21 = (n1 + tiny_eps) * i21
    v0 = d_0v * s0 * t1
    v1 = d_1v * t1s
    vw = d_wv * t1s
    vv = d_vv * t1s
    k1w0 = h00 * g01 + h10 * g11
    w1w0 = h00 * h01 + h10 * h11
    vw0 = h00 * v0 + h10 * v1
    h02 = (v0 - h01 * h00 - h11 * h01) * i21
    h12 = (v1 - h01 * k1w0 - h11 * h11) * i21
    w1w2 = (vw - h01 * w1w0 - h11 * ww1) * i21
    h22 = (w1w2 - h01 * h02 - h11 * h12) * i21
    ww2 = vv + h01 * h01 * ww0 + h11 * h11 * ww1
    ww2 = (ww2 - 2.0 * (h01 * vw0 + h11 * vw - h01 * h11 * w1w0)) * i21 * i21
    g02 = (h01 - h01 * g00 - h11 * g01) * i21
    g12 = (h11 - h01 * g01 - h11 * g11) * i21
    g22 = n1 * i21 * i21
    n2 = ww2 - h02 * h02 * (2.0 - g00) - h12 * h12 * (2.0 - g11) - h22 * h22 * (2.0 - g22)
    n2 = n2 + 2.0 * (h02 * h12 * g01 + h02 * h22 * g02 + h12 * h22 * g12)
    h32 = jnp.sqrt(jnp.maximum(n2, 0.0) + tiny_eps)
    y0, y1, y2 = givens_solve([[h00, h10], [h01, h11, h21], [h02, h12, h22, h32]], beta)

    over = y2 * i21
    on1 = y1 - over * h11
    a2 = over * t1 * c1
    a1 = on1 * t1 * c1 - over * t1 * c2
    a0 = y0 * s0 - over * h01 * s0 - on1 * t1 * c2

    def finish(p, carry):
        x = p // HALF
        yy = p % HALF
        total = (
            scaled(a0, zs[0, p].astype(f32))
            + scaled(a1, zs[1, p].astype(f32))
            + scaled(a2, zs[2, p].astype(f32))
        )
        out_ref[x, yy] = total[:, :COLS].astype(bf16)
        out_ref[x, yy + HALF] = pltpu.roll(total, COLS, 1)[:, :COLS].astype(bf16)
        return carry

    loop(PAIRS, finish)

    all_but_one(sum_cross.at[1], n_cross, b_ssem.at[1]).wait()


def body(nb, ng, rhs, diag_blocks, precond_blocks, coupling, face_open, agg_id, coarse_basis, coarse_inv):
    rows = AGGS * COMPS
    inverse = jnp.swapaxes(coarse_inv[0], 0, 1)
    hbm_spec = pl.BlockSpec(memory_space=pltpu.HBM)
    vmem_spec = pl.BlockSpec(memory_space=pltpu.VMEM)
    field = pltpu.VMEM((PAIRS, NS, LANES), f32)
    dma = pltpu.SemaphoreType.DMA
    call = pl.pallas_call(
        functools.partial(kernel, nb, ng),
        out_shape=jax.ShapeDtypeStruct(rhs.shape, bf16),
        in_specs=[hbm_spec] * 8,
        out_specs=vmem_spec,
        scratch_shapes=[
            pltpu.VMEM((CX, CY, 4 * NS), f32),
            pltpu.VMEM((CX, 4, CY), jnp.int32),
            pltpu.SMEM((CX, CY), jnp.int32),
            pltpu.VMEM((COMPS, NS), f32),
            pltpu.VMEM((CX, CY, NS, COLS), bf16),
            pltpu.VMEM((PAIRS, 2 * NS, NS), bf16),
            pltpu.VMEM((PAIRS, 2 * NS, NS), bf16),
            pltpu.VMEM((PAIRS, 2 * NS, NS), bf16),
            pltpu.VMEM((rows, ng * rows), f32),
            pltpu.VMEM((4 * rows, ng * rows), bf16),
            pltpu.VMEM((PAIRS, 4, NS, LANES), f32),
            pltpu.VMEM((PAIRS, 8, LANES), f32),
            pltpu.VMEM((2 * COMPS, 3 * NS), bf16),
            pltpu.VMEM((NS, 3 * COMPS), bf16),
            field,
            field,
            field,
            field,
            pltpu.VMEM((ITERS, PAIRS, NS, LANES), bf16),
            pltpu.VMEM((ITERS, PAIRS, NS, LANES), bf16),
            pltpu.VMEM((5, AGGS, NS, LANES), f32),
            pltpu.VMEM((rows, 2 * LANES), bf16),
            pltpu.VMEM((ITERS, rows // 2, LANES), bf16),
            pltpu.VMEM((ITERS, ng, rows // 2, LANES), bf16),
            pltpu.VMEM((ITERS, rows // 2, LANES), f32),
            pltpu.VMEM((ITERS, 4, rows // 2, LANES), f32),
            pltpu.VMEM((ITERS, CX, HALF, NS, LANES), bf16),
            pltpu.VMEM((ITERS, CX, 2, NS, LANES), bf16),
            pltpu.VMEM((CX, HALF, 8, LANES), f32),
            pltpu.VMEM((CX, 2, 8, LANES), f32),
            pltpu.VMEM((2, 4, LANES), f32),
            pltpu.VMEM((2, 2 * along_y(nb), 4, LANES), f32),
            pltpu.VMEM((2, 4, LANES), f32),
            pltpu.VMEM((2, (nb // along_y(nb)) * (ng // 2), 4, LANES), f32),
            dma((14,)),
            dma((ITERS,)),
            dma((ITERS,)),
            dma((ITERS, 4)),
            dma((ITERS, 4)),
            dma((ITERS + 1, CX)),
            dma((ITERS + 1, CX)),
            dma((ITERS + 1, CX, 2)),
            dma((ITERS + 1, CX, 2)),
            dma((2,)),
            dma((2,)),
            dma((2,)),
            dma((2,)),
        ],
        compiler_params=pltpu.CompilerParams(
            collective_id=0, has_side_effects=True, vmem_limit_bytes=32 * 1024 * 1024
        ),
        cost_estimate=pl.CostEstimate(flops=200_000_000, bytes_accessed=3_000_000, transcendentals=0),
    )
    operands = (
        rhs,
        diag_blocks,
        precond_blocks,
        coupling,
        jnp.swapaxes(face_open, 1, 2),
        agg_id,
        jnp.swapaxes(coarse_basis, 0, 1),
        inverse,
    )
    return call(*[pltpu.with_memory_space_constraint(x, pltpu.HBM) for x in operands])


def solution(mesh):
    in_specs = (
        P("bulk", "group", None, None),
        P("bulk", "group", None, None),
        P("bulk", "group", None, None),
        P("bulk", "group", None),
        P("bulk", "group", None),
        P("bulk", "group"),
        P(),
        P("bulk", None, "group"),
    )
    out_specs = P("bulk", "group", None, None)
    return jax.shard_map(
        functools.partial(body, mesh.shape["bulk"], mesh.shape["group"]),
        mesh=mesh,
        in_specs=in_specs,
        out_specs=out_specs,
        check_vma=False,
    )
```
